32 devices in a mesh: section: 2 (over core), dp: 16 (over z, y, x).
Axes of the slice: x: 2, y: 2, z: 4, core: 2. Of those that a mesh axis runs over, the one named last changes fastest.
Arguments:
- inputs_down: bfloat16 [2, 512, 4096], P(None, 'dp', 'section'), may hold values from -6 to 6
- inputs_up: bfloat16 [2, 512, 4096], P(None, 'dp', 'section'), may hold values from -6 to 6
- cotan_down: bfloat16 [2, 512, 4096], P(None, 'dp', 'section'), may hold values from -0.119628906 to 0.119628906
- cotan_up: bfloat16 [2, 512, 4096], P(None, 'dp', 'section'), may hold values from -0.119628906 to 0.119628906
- norm_gains: bfloat16 [2, 4096], P('section'), may hold values from 0.099609375 to 1.8984375
- adapt_down: bfloat16 [2, 64, 4096], P('section'), may hold values from -0.09375 to 0.09375
- adapt_up: bfloat16 [2, 64, 4096], P('section'), may hold values from -0.75 to 0.75
Outputs:
- grad_adapt_down: float32 [2, 64, 4096], P('section', None, 'dp')
- grad_adapt_up: float32 [2, 64, 4096], P('section', None, 'dp')
The draws below stay inside these ranges and needn't reach their ends.
All inputs are finite; a program needn't handle non-finite values.
Results may differ from the reference program's by a relative error of at most 0.006.
Values may be sent and summed in bfloat16 or wider, within the bound.
No kernel may reach another device: no remote copies, remote signals or barrier semaphores. Data moves between devices by JAX's collectives and lax.ppermute only.
A program may use at most 64 MiB of HBM per device.

```python
import jax
import jax.numpy as jnp
from jax import lax

D = 4096
K = 64
MB = 2
LAYERS = 2
TOKENS = 512


def shard_levels(own_key, dims, pieces, least, largest):
    level = 1.0
    for position, parts in pieces:
        heights = jax.random.uniform(jax.random.fold_in(jax.random.fold_in(own_key, 6), position), (parts,), jnp.float32, least / len(pieces), largest / len(pieces))
        level = level * jnp.repeat(jnp.exp(heights), dims[position] // parts).reshape((-1,) + (1,) * (len(dims) - 1 - position))
    return level


def bell_draw(own_key, extent, width, most, pieces=(), dtype=jnp.bfloat16):
    gain = shard_levels(own_key, extent, pieces, -0.22, 0.18) if pieces else 1.0
    drawn = jax.random.normal(own_key, extent, jnp.float32) * width * gain
    return jnp.minimum(jnp.maximum(drawn, -most), most).astype(dtype)


def setup_inputs(seed: int = 0) -> dict:
    streams_of = jax.random.split(jax.random.key(seed), 8)
    return {
        "inputs_down": bell_draw(streams_of[0], (MB, TOKENS, D), 1.0, 6.0, ((1, 16), (2, 2))),
        "inputs_up": bell_draw(streams_of[1], (MB, TOKENS, D), 1.0, 6.0, ((1, 16), (2, 2))),
        "cotan_down": bell_draw(streams_of[2], (MB, TOKENS, D), 0.02, 0.119628906, ((1, 16), (2, 2))),
        "cotan_up": bell_draw(streams_of[3], (MB, TOKENS, D), 0.02, 0.119628906, ((1, 16), (2, 2))),
        "norm_gains": jnp.clip(1.0 + 0.18 * jax.random.normal(streams_of[4], (LAYERS, D), jnp.float32), 0.099609375, 1.8984375).astype(jnp.bfloat16),
        "adapt_down": bell_draw(streams_of[5], (LAYERS, K, D), D ** -0.5, 0.09375, ((0, 2),)),
        "adapt_up": bell_draw(streams_of[6], (LAYERS, K, D), K ** -0.5, 0.75, ((0, 2),)),
    }


epsilon = 1e-05

def norm_branch(hidden, norm_gain, down_proj):
    hidden_f = hidden.astype(jnp.float32)
    inverse = lax.rsqrt(lax.optimization_barrier(jnp.mean(hidden_f * hidden_f, axis=-1, keepdims=True)) + epsilon)
    normed = (hidden_f * inverse * norm_gain.astype(jnp.float32)).astype(jnp.bfloat16)
    bottle = lax.dot_general(normed, down_proj, (((1,), (1,)), ((), ())), preferred_element_type=jnp.float32)
    active = jax.nn.silu(bottle).astype(jnp.bfloat16)
    return (hidden_f, inverse, normed, bottle, active)

def block_forward(hidden, norm_gain, down_proj, up_proj):
    hidden_f, inverse, normed, bottle, active = norm_branch(hidden, norm_gain, down_proj)
    return (hidden_f + jnp.dot(active, up_proj, preferred_element_type=jnp.float32)).astype(jnp.bfloat16)

def block_backward(hidden, upstream, norm_gain, down_proj, up_proj):
    hidden_f, inverse, normed, bottle, active = norm_branch(hidden, norm_gain, down_proj)
    upstream_f = upstream.astype(jnp.float32)
    grad_up = lax.dot_general(active, upstream, (((0,), (0,)), ((), ())), preferred_element_type=jnp.float32)
    grad_active = lax.dot_general(upstream, up_proj, (((1,), (1,)), ((), ())), preferred_element_type=jnp.float32)
    sigma = jax.nn.sigmoid(bottle)
    grad_bottle = (grad_active * sigma * (1.0 + bottle * (1.0 - sigma))).astype(jnp.bfloat16)
    grad_down = lax.dot_general(grad_bottle, normed, (((0,), (0,)), ((), ())), preferred_element_type=jnp.float32)
    grad_normed = jnp.dot(grad_bottle, down_proj, preferred_element_type=jnp.float32)
    scaled = norm_gain.astype(jnp.float32) * grad_normed
    project = lax.optimization_barrier(jnp.mean(scaled * hidden_f, axis=-1, keepdims=True))
    downstream = (upstream_f + inverse * scaled - hidden_f * inverse ** 3 * project).astype(jnp.bfloat16)
    return (downstream, grad_down, grad_up)

def reference(inputs_down, inputs_up, cotan_down, cotan_up, norm_gains, adapt_down, adapt_up):
    depth = norm_gains.shape[0]
    sums_down = [jnp.zeros(adapt_down.shape[1:], jnp.float32) for layer_idx in range(depth)]
    sums_up = [jnp.zeros(adapt_up.shape[1:], jnp.float32) for layer_idx in range(depth)]
    for entering, closing in ((inputs_down, cotan_down), (inputs_up, cotan_up)):
        for micro_idx in range(entering.shape[0]):
            hidden = entering[micro_idx]
            stored = []
            for layer_idx in range(depth):
                stored.append(hidden)
                hidden = block_forward(hidden, norm_gains[layer_idx], adapt_down[layer_idx], adapt_up[layer_idx])
            upstream = closing[micro_idx]
            for layer_idx in range(depth - 1, -1, -1):
                upstream, grad_down, grad_up = block_backward(stored[layer_idx], upstream, norm_gains[layer_idx], adapt_down[layer_idx], adapt_up[layer_idx])
                sums_down[layer_idx] = sums_down[layer_idx] + grad_down
                sums_up[layer_idx] = sums_up[layer_idx] + grad_up
    return (jnp.stack(sums_down), jnp.stack(sums_up))
```

```python
import functools

import jax
import jax.numpy as jnp
from jax import lax
from jax.experimental import pallas as pl
from jax.experimental.pallas import tpu as pltpu
from jax.sharding import PartitionSpec as P

epsilon = 1e-05
BOTH = ("section", "dp")
VMEM_BYTES = 32 * 1024 * 1024
f32 = jnp.float32
bf16 = jnp.bfloat16


def from_partner(value, axis, flip):
    return lax.ppermute(value, axis, [(i, i ^ flip) for i in range(lax.axis_size(axis))])


def dot_nn(left, right):
    return lax.dot_general(left, right, (((1,), (0,)), ((), ())), preferred_element_type=f32)


def dot_nt(left, right):
    return lax.dot_general(left, right, (((1,), (1,)), ((), ())), preferred_element_type=f32)


def split(value):
    high = value.astype(bf16)
    return high, (value - high.astype(f32)).astype(bf16)


def dot_split(left, right):
    high, low = split(left)
    return dot_nn(high, right) + dot_nn(low, right)


def rows_of(ref):
    value = ref[...]
    return value.reshape(-1, value.shape[-1])


def pack_kernel(width, group, members, place, *refs):
    acts = refs[:4]
    outs = refs[4:-1]
    sems = refs[-1]
    copies = []
    for k, out in enumerate(outs):
        index = place[1] ^ (k + 1)
        for a, act in enumerate(acts):
            for part in range(group):
                span = pl.ds(pl.multiple_of((part * members + index) * width, width), width)
                copies.append(
                    pltpu.make_async_copy(
                        act.at[:, :, span],
                        out.at[a, :, :, pl.ds(part * width, width)],
                        sems.at[len(copies)],
                    )
                )
                copies[-1].start()
    for copy in copies:
        copy.wait()


def products_kernel(layers, width, group, members, place, *refs):
    enter_down, enter_up, close_down, close_up = refs[:4]
    weights = [refs[4 + 3 * k : 7 + 3 * k] for k in range(layers)]
    piece_out, gain_out, low_out, high_out, prod_out, gram_out = refs[
        4 + 3 * layers : 10 + 3 * layers
    ]
    low_scr, fine_scr, high_scr, hidden_scr, close_scr = refs[10 + 3 * layers :]
    bottle = weights[0][1].shape[1]
    section = place[0]
    member = place[1]
    for k in range(layers):
        gain, down, up = weights[k]
        layer = section ^ k
        exact = gain[0].astype(f32) * down[0].astype(f32)
        low = exact.astype(bf16)
        low_scr[layer] = low
        fine_scr[layer] = (exact - low.astype(f32)).astype(bf16)
        high_scr[layer] = up[0]
        if group:
            for part in range(group):
                span = pl.ds(pl.multiple_of((part * members + member) * width, width), width)
                here = slice(part * width, (part + 1) * width)
                gain_out[layer, :, here] = gain[0, :, span].astype(f32)
    half = hidden_scr.shape[0] // 2
    hidden_scr[:half] = rows_of(enter_down)
    hidden_scr[half:] = rows_of(enter_up)
    close_scr[:half] = rows_of(close_down)
    close_scr[half:] = rows_of(close_up)
    if group:
        for part in range(group):
            span = pl.ds(pl.multiple_of((part * members + member) * width, width), width)
            here = slice(part * width, (part + 1) * width)
            low_out[:, :, here] = low_scr[:, :, span]
            high_out[:, :, here] = high_scr[:, :, span]
            piece_out[0, :, here] = hidden_scr[:, span]
            piece_out[1, :, here] = close_scr[:, span]
    hidden = hidden_scr[...]
    features = hidden.shape[-1]
    low_all = low_scr[...].reshape(layers * bottle, features)
    fine_all = fine_scr[...].reshape(layers * bottle, features)
    high_all = high_scr[...].reshape(layers * bottle, features)
    at = 0
    prod_out[: layers * bottle] = dot_nt(low_all, hidden) + dot_nt(fine_all, hidden)
    at += layers * bottle
    if layers > 1:
        prod_out[at : at + (layers - 1) * bottle] = dot_nt(
            high_all[: (layers - 1) * bottle], hidden
        )
        at += (layers - 1) * bottle
    prod_out[at : at + layers * bottle] = dot_nt(high_all, close_scr[...])
    at += layers * bottle
    square = dot_nt(hidden, hidden)
    eye = lax.broadcasted_iota(jnp.int32, square.shape, 0) == lax.broadcasted_iota(
        jnp.int32, square.shape, 1
    )
    norms = jnp.sum(jnp.where(eye, square, 0.0), axis=0, keepdims=True)
    prod_out[at : at + 8] = jnp.broadcast_to(norms, (8, norms.shape[1]))
    if layers > 1:
        high_part = high_all[: (layers - 1) * bottle]
        low_part = low_all[bottle:]
        fine_part = fine_all[bottle:]
        size = (layers - 1) * bottle
        gram_out[:size, :size] = jnp.zeros((size, size), f32)
        gram_out[:size, size:] = dot_nt(low_part, high_part) + dot_nt(fine_part, high_part)
        gram_out[size:, :size] = dot_nt(high_part, low_part) + dot_nt(high_part, fine_part)
        gram_out[size:, size:] = dot_nt(high_part, high_part)
    else:
        gram_out[...] = jnp.zeros_like(gram_out)


def relay_kernel(layers, bottle, features, sections, *refs):
    prods = refs[:sections]
    grams = refs[sections : 2 * sections]
    coef_out = refs[2 * sections]
    prod = sum((ref[...] for ref in prods[1:]), prods[0][...])
    gram = sum((ref[...] for ref in grams[1:]), grams[0][...])
    K = bottle
    inner = layers - 1
    h_low = [prod[l * K : (l + 1) * K] for l in range(layers)]
    at = layers * K
    h_high = [prod[at + l * K : at + (l + 1) * K] for l in range(inner)]
    at += inner * K
    u_high = [prod[at + l * K : at + (l + 1) * K] for l in range(layers)]
    at += layers * K
    norm = prod[at : at + 1]

    def low_high(l, m):
        return gram[(l - 1) * K : l * K, (inner + m) * K : (inner + m + 1) * K]

    def high_low(m, l):
        return gram[(inner + m) * K : (inner + m + 1) * K, (l - 1) * K : l * K]

    def high_high(m, n):
        return gram[
            (inner + m) * K : (inner + m + 1) * K, (inner + n) * K : (inner + n + 1) * K
        ]

    inverses, bottles, actives, hidden_high = [], [], [], []
    for l in range(layers):
        inverse = lax.rsqrt(jnp.maximum(norm, 0.0) * (1.0 / features) + epsilon)
        value = h_low[l] * inverse
        active = (value * jax.nn.sigmoid(value)).astype(bf16)
        inverses.append(inverse)
        bottles.append(value)
        actives.append(active)
        hidden_high.append(list(h_high))
        if l < inner:
            before = h_high[l]
            h_high = [h_high[n] + dot_split(high_high(n, l), active) for n in range(inner)]
            for n in range(l + 1, layers):
                h_low[n] = h_low[n] + dot_split(low_high(n, l), active)
            norm = norm + jnp.sum(
                active.astype(f32) * (before + h_high[l]), axis=0, keepdims=True
            )
    grads, pulls = [None] * layers, [None] * layers
    for l in range(layers - 1, -1, -1):
        sigma = jax.nn.sigmoid(bottles[l])
        grad = (u_high[l] * sigma * (1.0 + bottles[l] * (1.0 - sigma))).astype(bf16).astype(f32)
        scaled, fine = split(grad * inverses[l])
        pull = (
            inverses[l]
            * inverses[l]
            * jnp.sum(grad * bottles[l], axis=0, keepdims=True)
            * (1.0 / features)
        )
        grads[l], pulls[l] = grad.astype(bf16), pull
        for n in range(l):
            u_high[n] = (
                u_high[n]
                + dot_split(high_low(n, l), scaled)
                + dot_nn(high_low(n, l).astype(bf16), fine)
                - pull * hidden_high[l][n]
            )
    for l in range(layers):
        coef_out[l * K : (l + 1) * K] = actives[l]
        coef_out[(layers + l) * K : (layers + l + 1) * K] = grads[l]
    tail = coef_out.shape[0] - 2 * layers * K
    lines = [line.astype(bf16) for line in pulls[1:]]
    for l in range(layers):
        lines.extend(split(inverses[l]))
    lines = [line.astype(f32) for line in lines]
    lines += [jnp.zeros_like(pulls[0])] * (tail - len(lines))
    coef_out[2 * layers * K :] = jnp.concatenate(lines, axis=0).astype(bf16)


def grads_kernel(layers, bottle, width, group, members, place, *refs):
    K = bottle
    inner = layers - 1
    coefs = refs[:members]
    pieces = refs[members : 2 * members]
    gain, low, high = refs[2 * members : 2 * members + 3]
    outs = refs[2 * members + 3 : -1]
    parcel = refs[-1]
    by_hidden, by_close = 0.0, 0.0
    grad_active = [[0.0] * layers for _ in range(layers)]
    active_grad = [[0.0] * layers for _ in range(layers)]
    active_active = [[0.0] * layers for _ in range(layers)]
    for k in range(members):
        coef = coefs[k][...]
        actives = [coef[l * K : (l + 1) * K] for l in range(layers)]
        lines = coef[2 * layers * K :].astype(f32)
        scaled, fine = [], []
        for l in range(layers):
            at = inner + 2 * l
            inverse = lines[at : at + 1] + lines[at + 1 : at + 2]
            grad = coef[(layers + l) * K : (layers + l + 1) * K].astype(f32)
            coarse, rest = split(grad * inverse)
            scaled.append(coarse)
            fine.append(rest)
        pulled = [None] * layers
        total = None
        for l in range(inner - 1, -1, -1):
            line = lines[l : l + 1]
            total = line if total is None else total + line
            pulled[l] = (-total * actives[l].astype(f32)).astype(bf16)
        hidden = pieces[k][0]
        close = pieces[k][1]
        left = jnp.concatenate(scaled + fine + pulled[:inner], axis=0)
        by_hidden = by_hidden + dot_nn(left, hidden)
        by_close = by_close + dot_nn(coef[: layers * K], close)
        for l in range(layers):
            for n in range(l):
                grad_active[l][n] = grad_active[l][n] + dot_nt(scaled[l], actives[n])
                active_grad[n][l] = active_grad[n][l] + dot_nt(actives[n], scaled[l])
        for l in range(inner):
            for n in range(inner):
                if n <= l:
                    term = dot_nt(pulled[l], actives[n])
                else:
                    term = dot_nt(actives[l], pulled[n])
                active_active[l][n] = active_active[l][n] + term
    for l in range(layers):
        grad_down = (
            by_hidden[l * K : (l + 1) * K]
            + by_hidden[(layers + l) * K : (layers + l + 1) * K]
        )
        for n in range(l):
            grad_down = grad_down + dot_nn(grad_active[l][n].astype(bf16), high[n])
        grad_down = grad_down * gain[l]
        grad_up = by_close[l * K : (l + 1) * K]
        for n in range(l + 1, layers):
            grad_up = grad_up + dot_nn(active_grad[l][n].astype(bf16), low[n])
        if l < inner:
            grad_up = grad_up + by_hidden[
                (2 * layers + l) * K : (2 * layers + l + 1) * K
            ]
            for n in range(inner):
                grad_up = grad_up + dot_nn(active_active[l][n].astype(bf16), high[n])
        for part in range(group):
            here = slice(part * width, (part + 1) * width)
            parcel[l * group + part, 0] = grad_down[:, here].astype(bf16)
            parcel[l * group + part, 1] = grad_up[:, here].astype(bf16)
    if len(outs) == 1:
        outs[0][...] = parcel[...]
    else:
        for r, out in enumerate(outs):
            out[...] = parcel[place[2] ^ r]


def whole_spec(shape):
    return pl.BlockSpec(shape, lambda i, place: (0,) * len(shape))


def per_device(inputs_down, inputs_up, cotan_down, cotan_up, norm_gains, adapt_down, adapt_up):
    sections = lax.axis_size("section")
    replicas = lax.axis_size("dp")
    section = lax.axis_index("section")
    replica = lax.axis_index("dp")
    layers = sections
    members = min(4, replicas // sections)
    lines = replicas // members
    group = lines // sections
    bottle = adapt_down.shape[1]
    features = adapt_down.shape[2]
    share = features // sections
    width = features // replicas
    columns = group * width
    member = replica % members
    line = replica // members
    micro, tokens = inputs_down.shape[0], inputs_down.shape[1]
    half = micro * tokens
    rows = 2 * half
    aligned = width % 128 == 0
    place = jnp.stack([section, member, line]).astype(jnp.int32)

    own = (norm_gains[:, None, :], adapt_down, adapt_up)
    weights = [own]
    for k in range(1, sections):
        weights.append(tuple(from_partner(w, "section", k) for w in own))

    def piece(k):
        index = member ^ k
        parts = [
            lax.dynamic_index_in_dim(
                v.reshape(half, group, members, width), index, 2, keepdims=False
            ).reshape(half, columns)
            for v in (inputs_down, inputs_up, cotan_down, cotan_up)
        ]
        return jnp.concatenate(parts, axis=0).reshape(2, rows, columns)

    params = pltpu.CompilerParams(vmem_limit_bytes=VMEM_BYTES)
    acts = (inputs_down, inputs_up, cotan_down, cotan_up)
    if aligned:
        cut = (4, micro, tokens, columns)
        packed = pl.pallas_call(
            functools.partial(pack_kernel, width, group, members),
            out_shape=[jax.ShapeDtypeStruct(cut, bf16)] * (members - 1),
            in_specs=[pl.BlockSpec(memory_space=pltpu.SMEM)]
            + [pl.BlockSpec(memory_space=pl.ANY)] * 4,
            out_specs=[pl.BlockSpec(memory_space=pl.ANY)] * (members - 1),
            scratch_shapes=[pltpu.SemaphoreType.DMA((4 * group * (members - 1),))],
            compiler_params=params,
            name="pack",
        )(place, *acts)
        packed = [v.reshape(2, rows, columns) for v in packed]
    else:
        packed = [piece(k) for k in range(1, members)]
    pieces = [from_partner(v, "dp", k + 1) for k, v in enumerate(packed)]

    inner = max(layers - 1, 1)
    prod_rows = (3 * layers - 1) * bottle + 8
    block = pl.BlockSpec((1, 1, share), lambda i, place: (0, 0, place[0]))
    wide = pl.BlockSpec((1, bottle, share), lambda i, place: (0, 0, place[0]))
    own_shape = (layers, bottle, columns)
    out_shapes = [
        ((2, rows, columns), bf16),
        ((layers, 1, columns), f32),
        (own_shape, bf16),
        (own_shape, bf16),
        ((prod_rows, rows), f32),
        ((2 * inner * bottle, 2 * inner * bottle), f32),
    ]
    piece_own, gain_own, low_own, high_own, prod, gram = pl.pallas_call(
        functools.partial(
            products_kernel, layers, width, group if aligned else 0, members
        ),
        out_shape=[jax.ShapeDtypeStruct(s, d) for s, d in out_shapes],
        grid_spec=pltpu.PrefetchScalarGridSpec(
            num_scalar_prefetch=1,
            grid=(1,),
            in_specs=[whole_spec(v.shape) for v in acts] + [block, wide, wide] * sections,
            out_specs=[whole_spec(s) for s, _ in out_shapes],
            scratch_shapes=[
                pltpu.VMEM((layers, bottle, share), bf16),
                pltpu.VMEM((layers, bottle, share), bf16),
                pltpu.VMEM((layers, bottle, share), bf16),
                pltpu.VMEM((rows, share), bf16),
                pltpu.VMEM((rows, share), bf16),
            ],
        ),
        compiler_params=params,
        name="products",
    )(place, *acts, *[w for ws in weights for w in ws])
    if not aligned:
        piece_own = piece(0)
        layer_of = [section ^ k for k in range(sections)]

        def own_columns(which):
            shape = weights[0][which].shape[1]
            held = jnp.zeros((layers, shape, columns), bf16)
            for k in range(sections):
                cut = weights[k][which][0].reshape(shape, sections, group, members, width)
                cut = lax.dynamic_index_in_dim(cut, section, 1, keepdims=False)
                cut = lax.dynamic_index_in_dim(cut, member, 2, keepdims=False)
                held = lax.dynamic_update_index_in_dim(
                    held, cut.reshape(shape, columns), layer_of[k], 0
                )
            return held

        gain_own = own_columns(0).astype(f32)
        low_own = (own_columns(1).astype(f32) * gain_own).astype(bf16)
        high_own = own_columns(2)

    prods, grams = [prod], [gram]
    for k in range(1, sections):
        prods.append(from_partner(prod, "section", k))
        grams.append(from_partner(gram, "section", k))

    tail = layers - 1 + 2 * layers
    coef_rows = 2 * layers * bottle + -(-tail // 16) * 16
    coef = pl.pallas_call(
        functools.partial(relay_kernel, layers, bottle, features, sections),
        out_shape=jax.ShapeDtypeStruct((coef_rows, rows), bf16),
        compiler_params=params,
        name="relay",
    )(*prods, *grams)
    coefs = [coef]
    for k in range(1, members):
        coefs.append(from_partner(coef, "dp", k))

    message = (2, bottle, width)
    if aligned:
        sends = [(message, bf16)] * lines
    else:
        sends = [((lines,) + message, bf16)]
    operands = (*coefs, piece_own, *pieces, gain_own, low_own, high_own)
    parcels = pl.pallas_call(
        functools.partial(grads_kernel, layers, bottle, width, group, members),
        out_shape=[jax.ShapeDtypeStruct(s, d) for s, d in sends],
        grid_spec=pltpu.PrefetchScalarGridSpec(
            num_scalar_prefetch=1,
            grid=(1,),
            in_specs=[whole_spec(v.shape) for v in operands],
            out_specs=[whole_spec(s) for s, _ in sends],
            scratch_shapes=[pltpu.VMEM((lines,) + message, bf16)],
        ),
        compiler_params=params,
        name="grads",
    )(place, *operands)
    if not aligned:
        parcels = [
            lax.dynamic_index_in_dim(parcels[0], line ^ r, 0, keepdims=False)
            for r in range(lines)
        ]

    total = jnp.zeros(message, f32)
    for r in range(lines):
        route = []
        for c in range(sections):
            for g in range(lines):
                layer, part = divmod(g ^ r, group)
                for m in range(members):
                    target = (c * group + part) * members + m
                    route.append(
                        (c * replicas + g * members + m, layer * replicas + target)
                    )
        total = total + lax.ppermute(parcels[r], BOTH, route).astype(f32)
    return (total[0][None], total[1][None])


def solution(mesh):
    placed = (
        P(None, "dp", "section"),
        P(None, "dp", "section"),
        P(None, "dp", "section"),
        P(None, "dp", "section"),
        P("section", None),
        P("section", None, None),
        P("section", None, None),
    )
    return jax.shard_map(
        per_device,
        mesh=mesh,
        in_specs=placed,
        out_specs=(P("section", None, "dp"), P("section", None, "dp")),
        check_vma=False,
    )
```

```python
import functools

import jax
import jax.numpy as jnp
from jax import lax
from jax.experimental import pallas as pl
from jax.experimental.pallas import tpu as pltpu
from jax.sharding import PartitionSpec as P

epsilon = 1e-05
BOTH = ("section", "dp")
VMEM_BYTES = 32 * 1024 * 1024
f32 = jnp.float32
bf16 = jnp.bfloat16


def from_partner(value, axis, flip):
    return lax.ppermute(value, axis, [(i, i ^ flip) for i in range(lax.axis_size(axis))])


def dot_nn(left, right):
    return lax.dot_general(left, right, (((1,), (0,)), ((), ())), preferred_element_type=f32)


def dot_nt(left, right):
    return lax.dot_general(left, right, (((1,), (1,)), ((), ())), preferred_element_type=f32)


def split(value):
    high = value.astype(bf16)
    return high, (value - high.astype(f32)).astype(bf16)


def dot_split(left, right):
    high, low = split(left)
    return dot_nn(high, right) + dot_nn(low, right)


def pack_kernel(width, group, members, place, *refs):
    acts = refs[:4]
    both = refs[4]
    outs = refs[5 : 5 + members]
    sems = refs[-1]
    micro, tokens = acts[0].shape[0], acts[0].shape[1]
    copies = []
    for a, act in enumerate(acts):
        for m in range(micro):
            start = ((a % 2) * micro + m) * tokens
            copies.append(
                pltpu.make_async_copy(
                    act.at[m], both.at[a // 2, pl.ds(start, tokens)], sems.at[len(copies)]
                )
            )
            copies[-1].start()
    for n, copy in enumerate(copies):
        copy.wait()
        a, m = divmod(n, micro)
        start = ((a % 2) * micro + m) * tokens
        for k, out in enumerate(outs):
            index = place[1] ^ k
            for part in range(group):
                span = pl.ds(pl.multiple_of((part * members + index) * width, width), width)
                out[a // 2, start : start + tokens, part * width : (part + 1) * width] = both[
                    a // 2, start : start + tokens, span
                ]


def products_kernel(layers, width, group, members, place, *refs):
    acts = refs[0]
    weights = [refs[1 + 3 * k : 4 + 3 * k] for k in range(layers)]
    gain_out, low_out, high_out, prod_out, gram_out = refs[1 + 3 * layers : 6 + 3 * layers]
    low_scr, fine_scr, high_scr = refs[6 + 3 * layers :]
    bottle = weights[0][1].shape[1]
    features = acts.shape[2]
    section = place[0]
    member = place[1]
    mine = pl.ds(pl.multiple_of(section * features, features), features)
    for k in range(layers):
        gain, down, up = weights[k]
        layer = section ^ k
        exact = gain[0, :, mine].astype(f32) * down[0, :, mine].astype(f32)
        low = exact.astype(bf16)
        low_scr[layer] = low
        fine_scr[layer] = (exact - low.astype(f32)).astype(bf16)
        high_scr[layer] = up[0, :, mine]
        if group:
            for part in range(group):
                begin = section * features + (part * members + member) * width
                span = pl.ds(pl.multiple_of(begin, width), width)
                here = slice(part * width, (part + 1) * width)
                gain_out[layer, :, here] = gain[0, :, span].astype(f32)
    if group:
        for part in range(group):
            span = pl.ds(pl.multiple_of((part * members + member) * width, width), width)
            here = slice(part * width, (part + 1) * width)
            low_out[:, :, here] = low_scr[:, :, span]
            high_out[:, :, here] = high_scr[:, :, span]
    hidden = acts[0]
    low_all = low_scr[...].reshape(layers * bottle, features)
    fine_all = fine_scr[...].reshape(layers * bottle, features)
    high_all = high_scr[...].reshape(layers * bottle, features)
    at = 0
    prod_out[: layers * bottle] = dot_nt(low_all, hidden) + dot_nt(fine_all, hidden)
    at += layers * bottle
    if layers > 1:
        prod_out[at : at + (layers - 1) * bottle] = dot_nt(
            high_all[: (layers - 1) * bottle], hidden
        )
        at += (layers - 1) * bottle
    prod_out[at : at + layers * bottle] = dot_nt(high_all, acts[1])
    at += layers * bottle
    square = dot_nt(hidden, hidden)
    eye = lax.broadcasted_iota(jnp.int32, square.shape, 0) == lax.broadcasted_iota(
        jnp.int32, square.shape, 1
    )
    norms = jnp.sum(jnp.where(eye, square, 0.0), axis=0, keepdims=True)
    prod_out[at : at + 8] = jnp.broadcast_to(norms, (8, norms.shape[1]))
    if layers > 1:
        high_part = high_all[: (layers - 1) * bottle]
        low_part = low_all[bottle:]
        fine_part = fine_all[bottle:]
        size = (layers - 1) * bottle
        gram_out[:size, :size] = jnp.zeros((size, size), f32)
        gram_out[:size, size:] = dot_nt(low_part, high_part) + dot_nt(fine_part, high_part)
        gram_out[size:, :size] = dot_nt(high_part, low_part) + dot_nt(high_part, fine_part)
        gram_out[size:, size:] = dot_nt(high_part, high_part)
    else:
        gram_out[...] = jnp.zeros_like(gram_out)


def relay_kernel(layers, bottle, features, sections, *refs):
    prods = refs[:sections]
    grams = refs[sections : 2 * sections]
    coef_out = refs[2 * sections]
    prod = sum((ref[...] for ref in prods[1:]), prods[0][...])
    gram = sum((ref[...] for ref in grams[1:]), grams[0][...])
    K = bottle
    inner = layers - 1
    h_low = [prod[l * K : (l + 1) * K] for l in range(layers)]
    at = layers * K
    h_high = [prod[at + l * K : at + (l + 1) * K] for l in range(inner)]
    at += inner * K
    u_high = [prod[at + l * K : at + (l + 1) * K] for l in range(layers)]
    at += layers * K
    norm = prod[at : at + 1]

    def low_high(l, m):
        return gram[(l - 1) * K : l * K, (inner + m) * K : (inner + m + 1) * K]

    def high_low(m, l):
        return gram[(inner + m) * K : (inner + m + 1) * K, (l - 1) * K : l * K]

    def high_high(m, n):
        return gram[
            (inner + m) * K : (inner + m + 1) * K, (inner + n) * K : (inner + n + 1) * K
        ]

    inverses, bottles, actives, hidden_high = [], [], [], []
    for l in range(layers):
        inverse = lax.rsqrt(jnp.maximum(norm, 0.0) * (1.0 / features) + epsilon)
        value = h_low[l] * inverse
        active = (value * jax.nn.sigmoid(value)).astype(bf16)
        inverses.append(inverse)
        bottles.append(value)
        actives.append(active)
        hidden_high.append(list(h_high))
        if l < inner:
            before = h_high[l]
            h_high = [h_high[n] + dot_split(high_high(n, l), active) for n in range(inner)]
            for n in range(l + 1, layers):
                h_low[n] = h_low[n] + dot_split(low_high(n, l), active)
            norm = norm + jnp.sum(
                active.astype(f32) * (before + h_high[l]), axis=0, keepdims=True
            )
    grads, pulls = [None] * layers, [None] * layers
    for l in range(layers - 1, -1, -1):
        sigma = jax.nn.sigmoid(bottles[l])
        grad = (u_high[l] * sigma * (1.0 + bottles[l] * (1.0 - sigma))).astype(bf16).astype(f32)
        scaled, fine = split(grad * inverses[l])
        pull = (
            inverses[l]
            * inverses[l]
            * jnp.sum(grad * bottles[l], axis=0, keepdims=True)
            * (1.0 / features)
        )
        grads[l], pulls[l] = grad.astype(bf16), pull
        for n in range(l):
            u_high[n] = (
                u_high[n]
                + dot_split(high_low(n, l), scaled)
                + dot_nn(high_low(n, l).astype(bf16), fine)
                - pull * hidden_high[l][n]
            )
    for l in range(layers):
        coef_out[l * K : (l + 1) * K] = actives[l]
        coef_out[(layers + l) * K : (layers + l + 1) * K] = grads[l]
    tail = coef_out.shape[0] - 2 * layers * K
    lines = [line.astype(bf16) for line in pulls[1:]]
    for l in range(layers):
        lines.extend(split(inverses[l]))
    lines = [line.astype(f32) for line in lines]
    lines += [jnp.zeros_like(pulls[0])] * (tail - len(lines))
    coef_out[2 * layers * K :] = jnp.concatenate(lines, axis=0).astype(bf16)


def grads_kernel(layers, bottle, width, group, members, place, *refs):
    K = bottle
    inner = layers - 1
    coefs = refs[:members]
    pieces = refs[members : 2 * members]
    gain, low, high = refs[2 * members : 2 * members + 3]
    outs = refs[2 * members + 3 : -1]
    parcel = refs[-1]
    by_hidden, by_close = 0.0, 0.0
    grad_active = [[0.0] * layers for _ in range(layers)]
    active_grad = [[0.0] * layers for _ in range(layers)]
    active_active = [[0.0] * layers for _ in range(layers)]
    for k in range(members):
        coef = coefs[k][...]
        actives = [coef[l * K : (l + 1) * K] for l in range(layers)]
        lines = coef[2 * layers * K :].astype(f32)
        scaled, fine = [], []
        for l in range(layers):
            at = inner + 2 * l
            inverse = lines[at : at + 1] + lines[at + 1 : at + 2]
            grad = coef[(layers + l) * K : (layers + l + 1) * K].astype(f32)
            coarse, rest = split(grad * inverse)
            scaled.append(coarse)
            fine.append(rest)
        pulled = [None] * layers
        total = None
        for l in range(inner - 1, -1, -1):
            line = lines[l : l + 1]
            total = line if total is None else total + line
            pulled[l] = (-total * actives[l].astype(f32)).astype(bf16)
        hidden = pieces[k][0]
        close = pieces[k][1]
        left = jnp.concatenate(scaled + fine + pulled[:inner], axis=0)
        by_hidden = by_hidden + dot_nn(left, hidden)
        by_close = by_close + dot_nn(coef[: layers * K], close)
        for l in range(layers):
            for n in range(l):
                grad_active[l][n] = grad_active[l][n] + dot_nt(scaled[l], actives[n])
                active_grad[n][l] = active_grad[n][l] + dot_nt(actives[n], scaled[l])
        for l in range(inner):
            for n in range(inner):
                if n <= l:
                    term = dot_nt(pulled[l], actives[n])
                else:
                    term = dot_nt(actives[l], pulled[n])
                active_active[l][n] = active_active[l][n] + term
    for l in range(layers):
        grad_down = (
            by_hidden[l * K : (l + 1) * K]
            + by_hidden[(layers + l) * K : (layers + l + 1) * K]
        )
        for n in range(l):
            grad_down = grad_down + dot_nn(grad_active[l][n].astype(bf16), high[n])
        grad_down = grad_down * gain[l]
        grad_up = by_close[l * K : (l + 1) * K]
        for n in range(l + 1, layers):
            grad_up = grad_up + dot_nn(active_grad[l][n].astype(bf16), low[n])
        if l < inner:
            grad_up = grad_up + by_hidden[
                (2 * layers + l) * K : (2 * layers + l + 1) * K
            ]
            for n in range(inner):
                grad_up = grad_up + dot_nn(active_active[l][n].astype(bf16), high[n])
        for part in range(group):
            here = slice(part * width, (part + 1) * width)
            parcel[l * group + part, 0] = grad_down[:, here].astype(bf16)
            parcel[l * group + part, 1] = grad_up[:, here].astype(bf16)
    if len(outs) == 1:
        outs[0][...] = parcel[...]
    else:
        for r, out in enumerate(outs):
            out[...] = parcel[place[2] ^ r]


IN_SMEM = pl.BlockSpec(memory_space=pltpu.SMEM)
IN_VMEM = pl.BlockSpec(memory_space=pltpu.VMEM)


def per_device(inputs_down, inputs_up, cotan_down, cotan_up, norm_gains, adapt_down, adapt_up):
    sections = lax.axis_size("section")
    replicas = lax.axis_size("dp")
    section = lax.axis_index("section")
    replica = lax.axis_index("dp")
    layers = sections
    members = min(4, replicas // sections)
    lines = replicas // members
    group = lines // sections
    bottle = adapt_down.shape[1]
    features = adapt_down.shape[2]
    share = features // sections
    width = features // replicas
    columns = group * width
    member = replica % members
    line = replica // members
    micro, tokens = inputs_down.shape[0], inputs_down.shape[1]
    half = micro * tokens
    rows = 2 * half
    aligned = width % 128 == 0
    place = jnp.stack([section, member, line]).astype(jnp.int32)

    own = (norm_gains[:, None, :], adapt_down, adapt_up)
    weights = [own]
    for k in range(1, sections):
        weights.append(tuple(from_partner(w, "section", k) for w in own))

    def piece(k):
        index = member ^ k
        parts = [
            lax.dynamic_index_in_dim(
                v.reshape(half, group, members, width), index, 2, keepdims=False
            ).reshape(half, columns)
            for v in (inputs_down, inputs_up, cotan_down, cotan_up)
        ]
        return jnp.concatenate(parts, axis=0).reshape(2, rows, columns)

    params = pltpu.CompilerParams(vmem_limit_bytes=VMEM_BYTES)
    acts = (inputs_down, inputs_up, cotan_down, cotan_up)
    if aligned:
        both, piece_own, *packed = pl.pallas_call(
            functools.partial(pack_kernel, width, group, members),
            out_shape=[pltpu.VMEM((2, rows, share), bf16)]
            + [pltpu.VMEM((2, rows, columns), bf16)] * members,
            in_specs=[IN_SMEM] + [pl.BlockSpec(memory_space=pltpu.HBM)] * 4,
            out_specs=[IN_VMEM] * (1 + members),
            scratch_shapes=[pltpu.SemaphoreType.DMA((4 * micro,))],
            compiler_params=params,
            name="pack",
        )(place, *[pltpu.with_memory_space_constraint(v, pltpu.HBM) for v in acts])
    else:
        both = jnp.concatenate([v.reshape(half, share) for v in acts], axis=0)
        both = both.reshape(2, rows, share)
        packed = [piece(k) for k in range(1, members)]
    pieces = [from_partner(v, "dp", k + 1) for k, v in enumerate(packed)]

    inner = max(layers - 1, 1)
    prod_rows = (3 * layers - 1) * bottle + 8
    own_shape = (layers, bottle, columns)
    out_shapes = [
        ((layers, 1, columns), f32),
        (own_shape, bf16),
        (own_shape, bf16),
        ((prod_rows, rows), f32),
        ((2 * inner * bottle, 2 * inner * bottle), f32),
    ]
    gain_own, low_own, high_own, prod, gram = pl.pallas_call(
        functools.partial(
            products_kernel, layers, width, group if aligned else 0, members
        ),
        out_shape=[jax.ShapeDtypeStruct(s, d) for s, d in out_shapes],
        in_specs=[IN_SMEM] + [IN_VMEM] * (1 + 3 * sections),
        out_specs=[IN_VMEM] * len(out_shapes),
        scratch_shapes=[pltpu.VMEM((layers, bottle, share), bf16)] * 3,
        compiler_params=params,
        name="products",
    )(place, both, *[w for ws in weights for w in ws])
    if not aligned:
        piece_own = piece(0)
        layer_of = [section ^ k for k in range(sections)]

        def own_columns(which):
            shape = weights[0][which].shape[1]
            held = jnp.zeros((layers, shape, columns), bf16)
            for k in range(sections):
                cut = weights[k][which][0].reshape(shape, sections, group, members, width)
                cut = lax.dynamic_index_in_dim(cut, section, 1, keepdims=False)
                cut = lax.dynamic_index_in_dim(cut, member, 2, keepdims=False)
                held = lax.dynamic_update_index_in_dim(
                    held, cut.reshape(shape, columns), layer_of[k], 0
                )
            return held

        gain_own = own_columns(0).astype(f32)
        low_own = (own_columns(1).astype(f32) * gain_own).astype(bf16)
        high_own = own_columns(2)

    prods, grams = [prod], [gram]
    for k in range(1, sections):
        prods.append(from_partner(prod, "section", k))
        grams.append(from_partner(gram, "section", k))

    tail = layers - 1 + 2 * layers
    coef_rows = 2 * layers * bottle + -(-tail // 16) * 16
    coef = pl.pallas_call(
        functools.partial(relay_kernel, layers, bottle, features, sections),
        out_shape=jax.ShapeDtypeStruct((coef_rows, rows), bf16),
        compiler_params=params,
        name="relay",
    )(*prods, *grams)
    coefs = [coef]
    for k in range(1, members):
        coefs.append(from_partner(coef, "dp", k))

    message = (2, bottle, width)
    if aligned:
        sends = [(message, bf16)] * lines
    else:
        sends = [((lines,) + message, bf16)]
    operands = (*coefs, piece_own, *pieces, gain_own, low_own, high_own)
    parcels = pl.pallas_call(
        functools.partial(grads_kernel, layers, bottle, width, group, members),
        out_shape=[jax.ShapeDtypeStruct(s, d) for s, d in sends],
        in_specs=[IN_SMEM] + [IN_VMEM] * len(operands),
        out_specs=[IN_VMEM] * len(sends),
        scratch_shapes=[pltpu.VMEM((lines,) + message, bf16)],
        compiler_params=params,
        name="grads",
    )(place, *operands)
    if not aligned:
        parcels = [
            lax.dynamic_index_in_dim(parcels[0], line ^ r, 0, keepdims=False)
            for r in range(lines)
        ]

    total = jnp.zeros(message, f32)
    for r in range(lines):
        route = []
        for c in range(sections):
            for g in range(lines):
                layer, part = divmod(g ^ r, group)
                for m in range(members):
                    target = (c * group + part) * members + m
                    route.append(
                        (c * replicas + g * members + m, layer * replicas + target)
                    )
        total = total + lax.ppermute(parcels[r], BOTH, route).astype(f32)
    return (total[0][None], total[1][None])


def solution(mesh):
    placed = (
        P(None, "dp", "section"),
        P(None, "dp", "section"),
        P(None, "dp", "section"),
        P(None, "dp", "section"),
        P("section", None),
        P("section", None, None),
        P("section", None, None),
    )
    return jax.shard_map(
        per_device,
        mesh=mesh,
        in_specs=placed,
        out_specs=(P("section", None, "dp"), P("section", None, "dp")),
        check_vma=False,
    )
```

```python
import functools

import jax
import jax.numpy as jnp
from jax import lax
from jax.experimental import pallas as pl
from jax.experimental.pallas import tpu as pltpu
from jax.sharding import PartitionSpec as P

epsilon = 1e-05
VMEM_BYTES = 32 * 1024 * 1024
MEMBERS = 4
STAR = True
TWIST = 0
COST_PRODUCTS = 12
COST_SMALL = 0.1
f32 = jnp.float32
bf16 = jnp.bfloat16
IN_VMEM = pl.BlockSpec(memory_space=pltpu.VMEM)
IN_HBM = pl.BlockSpec(memory_space=pltpu.HBM)


def cost(micros):
    return pl.CostEstimate(flops=int(micros * 1.1e9), bytes_accessed=0, transcendentals=0)


def from_partner(value, axis, flip):
    return lax.ppermute(value, axis, [(i, i ^ flip) for i in range(lax.axis_size(axis))])


def dot_nn(left, right):
    return lax.dot_general(left, right, (((1,), (0,)), ((), ())), preferred_element_type=f32)


def dot_nt(left, right):
    return lax.dot_general(left, right, (((1,), (1,)), ((), ())), preferred_element_type=f32)


def split(value):
    high = value.astype(bf16)
    return high, (value - high.astype(f32)).astype(bf16)


def dot_split(left, right):
    high, low = split(left)
    return dot_nn(high, right) + dot_nn(low, right)


LEADERS = (0, 1, 2, 4) if STAR else (0, 1, 2, 3)


def leader(label):
    return label + (label == 3) if STAR else label


def mask(slot, group, chunks):
    section, part = divmod(slot, group)
    low = (part & 1) * 7 + (part >> 1) * 8 if STAR else part * 4
    return section * chunks ^ (section & 1) * TWIST ^ low


def label_slot(replica, group, chunks):
    section = replica // chunks
    local = replica % chunks ^ (section & 1) * TWIST
    if not STAR:
        return local % 4, section * group + local // 4
    low = local & 7
    label = (low & 3) ^ (low >> 2) * 3
    odd = (low != 0) & (low != 1) & (low != 2) & (low != 4)
    return label, section * group + (local >> 3) * 2 + odd.astype(jnp.int32)


def whereabouts(group, chunks):
    section = lax.axis_index("section")
    label, slot = label_slot(lax.axis_index("dp"), group, chunks)
    return section, label, slot


def chunk_of(label, part, section):
    low = (part & 1) * 7 + (part >> 1) * 8 if STAR else part * 4
    return leader(label) ^ low ^ (section & 1) * TWIST


def pack_kernel(width, group, chunks, *refs):
    acts = refs[:4]
    both = refs[4]
    outs = refs[5:-1]
    sems = refs[-1]
    micro, tokens = acts[0].shape[0], acts[0].shape[1]
    section, label, _ = whereabouts(group, chunks)
    copies = []
    for a, act in enumerate(acts):
        for m in range(micro):
            start = ((a % 2) * micro + m) * tokens
            copies.append(
                pltpu.make_async_copy(
                    act.at[m], both.at[a // 2, pl.ds(start, tokens)], sems.at[len(copies)]
                )
            )
            copies[-1].start()
    for n, copy in enumerate(copies):
        copy.wait()
        a, m = divmod(n, micro)
        start = ((a % 2) * micro + m) * tokens
        for k, out in enumerate(outs):
            for part in range(group):
                chunk = chunk_of(label ^ k, part, section)
                span = pl.ds(pl.multiple_of(chunk * width, width), width)
                out[a // 2, start : start + tokens, part * width : (part + 1) * width] = both[
                    a // 2, start : start + tokens, span
                ]


def two_parts(refs):
    if len(refs) == 2:
        return refs
    height, side = refs[0].shape
    return refs[0].at[: height - side], refs[0].at[height - side :]


def products_kernel(layers, *refs):
    acts = refs[0]
    weights = [refs[1 + 3 * k : 4 + 3 * k] for k in range(layers)]
    outs = refs[1 + 3 * layers : -3]
    prod_out, gram_out = two_parts(outs)
    low_scr, fine_scr, high_scr = refs[-3:]
    bottle = weights[0][1].shape[1]
    features = acts.shape[2]
    section = lax.axis_index("section")
    mine = pl.ds(pl.multiple_of(section * features, features), features)
    for k in range(layers):
        gain, down, up = weights[k]
        layer = section ^ k
        exact = gain[0, :, mine].astype(f32) * down[0, :, mine].astype(f32)
        low, fine = split(exact)
        low_scr[layer] = low
        fine_scr[layer] = fine
        high_scr[layer] = up[0, :, mine]
    hidden = acts[0]
    low_all = low_scr[...].reshape(layers * bottle, features)
    fine_all = fine_scr[...].reshape(layers * bottle, features)
    high_all = high_scr[...].reshape(layers * bottle, features)
    size = (layers - 1) * bottle
    at = layers * bottle
    prod_out[:at] = dot_nt(low_all, hidden) + dot_nt(fine_all, hidden)
    if layers > 1:
        prod_out[at : at + size] = dot_nt(high_all[:size], hidden)
    at += size
    prod_out[at : at + layers * bottle] = dot_nt(high_all, acts[1])
    at += layers * bottle
    square = dot_nt(hidden, hidden)
    eye = lax.broadcasted_iota(jnp.int32, square.shape, 0) == lax.broadcasted_iota(
        jnp.int32, square.shape, 1
    )
    norms = jnp.sum(jnp.where(eye, square, 0.0), axis=0, keepdims=True)
    prod_out[at : at + 8] = jnp.broadcast_to(norms, (8, norms.shape[1]))
    if layers > 1:
        high_part = high_all[:size]
        low_part = low_all[bottle:]
        fine_part = fine_all[bottle:]
        gram_out[:size, :size] = jnp.zeros((size, size), f32)
        gram_out[:size, size:] = dot_nt(low_part, high_part) + dot_nt(fine_part, high_part)
        gram_out[size:, :size] = dot_nt(high_part, low_part) + dot_nt(high_part, fine_part)
        gram_out[size:, size:] = dot_nt(high_part, high_part)
    else:
        gram_out[...] = jnp.zeros_like(gram_out)


def relay_kernel(layers, bottle, features, sections, *refs):
    coef_out, hold = refs[-2:]
    each = (len(refs) - 2) // sections
    prods, grams = zip(
        *(two_parts(refs[each * k : each * (k + 1)]) for k in range(sections)), strict=True
    )
    section = lax.axis_index("section")
    prod = sum((ref[...] for ref in prods[1:]), prods[0][...])
    gram = sum((ref[...] for ref in grams[1:]), grams[0][...])
    K = bottle
    inner = layers - 1
    h_low = [prod[l * K : (l + 1) * K] for l in range(layers)]
    at = layers * K
    h_high = [prod[at + l * K : at + (l + 1) * K] for l in range(inner)]
    at += inner * K
    u_high = [prod[at + l * K : at + (l + 1) * K] for l in range(layers)]
    at += layers * K
    norm = prod[at : at + 1]

    def low_high(l, m):
        return gram[(l - 1) * K : l * K, (inner + m) * K : (inner + m + 1) * K]

    def high_low(m, l):
        return gram[(inner + m) * K : (inner + m + 1) * K, (l - 1) * K : l * K]

    def high_high(m, n):
        return gram[
            (inner + m) * K : (inner + m + 1) * K, (inner + n) * K : (inner + n + 1) * K
        ]

    inverses, bottles, hidden_high = [], [], []
    for l in range(layers):
        inverse = lax.rsqrt(jnp.maximum(norm, 0.0) * (1.0 / features) + epsilon)
        value = h_low[l] * inverse
        active = (value * jax.nn.sigmoid(value)).astype(bf16)
        inverses.append(inverse)
        bottles.append(value)
        hold[l] = active
        hidden_high.append(list(h_high))
        if l < inner:
            before = h_high[l]
            h_high = [h_high[n] + dot_split(high_high(n, l), active) for n in range(inner)]
            for n in range(l + 1, layers):
                h_low[n] = h_low[n] + dot_split(low_high(n, l), active)
            norm = norm + jnp.sum(
                active.astype(f32) * (before + h_high[l]), axis=0, keepdims=True
            )
    pulls = [None] * layers
    for l in range(layers - 1, -1, -1):
        sigma = jax.nn.sigmoid(bottles[l])
        coarse = (u_high[l] * sigma * (1.0 + bottles[l] * (1.0 - sigma))).astype(bf16)
        hold[layers + l] = coarse
        if l == 0:
            break
        grad = coarse.astype(f32)
        scaled, fine = split(grad * inverses[l])
        pull = (
            inverses[l]
            * inverses[l]
            * jnp.sum(grad * bottles[l], axis=0, keepdims=True)
            * (1.0 / features)
        )
        pulls[l] = pull
        for n in range(l):
            u_high[n] = (
                u_high[n]
                + dot_split(high_low(n, l), scaled)
                + dot_nn(high_low(n, l).astype(bf16), fine)
                - pull * hidden_high[l][n]
            )
    blocks = [hold[layers + section], hold[section]]
    for i in range(inner):
        other = i + jnp.where(section <= i, 1, 0)
        blocks.append(hold[jnp.where(section <= i, layers + other, other)])
    blocks += [hold[n] for n in range(1, inner)]
    for n, block in enumerate(blocks):
        coef_out[n * K : (n + 1) * K] = block

    def inverse_at(layer):
        value = inverses[0]
        for l in range(1, layers):
            value = jnp.where(layer == l, inverses[l], value)
        return value

    lines = [line.astype(bf16).astype(f32) for line in pulls[1:]]
    scales = [inverse_at(section)]
    scales += [inverse_at(i + jnp.where(section <= i, 1, 0)) for i in range(inner)]
    for scale in scales:
        lines.extend(part.astype(f32) for part in split(scale))
    tail = coef_out.shape[0] - len(blocks) * K
    lines += [jnp.zeros_like(norm)] * (tail - len(lines))
    coef_out[len(blocks) * K :] = jnp.concatenate(lines, axis=0).astype(bf16)


def cut_kernel(layers, width, group, chunks, *refs):
    weights = [refs[3 * k : 3 * k + 3] for k in range(layers)]
    gain_out, both_out = refs[3 * layers :]
    here_section, label, _ = whereabouts(group, chunks)
    for k in range(layers):
        section = here_section ^ k
        for part in range(group):
            chunk = section * chunks + chunk_of(label, part, section)
            span = pl.ds(pl.multiple_of(chunk * width, width), width)
            here = slice(part * width, (part + 1) * width)
            gain_out[k, :, here] = weights[0][0][0, :, span].astype(f32)
            for w in range(layers):
                gain, down, up = weights[w]
                layer = here_section ^ w
                low = gain[0, :, span].astype(f32) * down[0, :, span].astype(f32)
                both_out[k, layer, :, here] = low.astype(bf16)
                both_out[k, layers + layer, :, here] = up[0, :, span]


def stack_kernel(*refs):
    for k, ref in enumerate(refs[:-1]):
        refs[-1][k] = ref[...]


def grads_kernel(layers, bottle, width, group, chunks, *refs):
    K = bottle
    inner = layers - 1
    coefs = refs[:MEMBERS]
    pieces = refs[MEMBERS : MEMBERS + layers]
    gain, both = refs[MEMBERS + layers : MEMBERS + layers + 2]
    outs = refs[MEMBERS + layers + 2 : -1]
    parcel = refs[-1]
    section, _, own_slot = whereabouts(group, chunks)
    above = [section <= i for i in range(inner)]
    other_of = [i + jnp.where(above[i], 1, 0) for i in range(inner)]
    by_hidden = [0.0] * layers
    by_close = [0.0] * layers
    cross = [0.0] * inner
    drag = [0.0] * inner
    for m in range(MEMBERS):
        coef = coefs[m][...]
        grad, active = coef[:K], coef[K : 2 * K]
        others = [coef[(2 + i) * K : (3 + i) * K] for i in range(inner)]
        extras = [coef[(1 + layers + i) * K : (2 + layers + i) * K] for i in range(inner - 1)]
        at = (2 + inner + max(inner - 1, 0)) * K
        lines = coef[at:].astype(f32)
        active_f = active.astype(f32)

        def scale(i):
            row = inner + 2 * i
            return lines[row : row + 1] + lines[row + 1 : row + 2]

        def weight(n):
            total = jnp.zeros_like(lines[:1])
            for l in range(n + 1, layers):
                total = total + jnp.where(section < l, lines[l - 1 : l], 0.0)
            return total

        coarse, fine = split(grad.astype(f32) * scale(0))
        full = jnp.zeros_like(lines[:1])
        for l in range(1, layers):
            full = full + jnp.where(section < l, lines[l - 1 : l], 0.0)
        pulled = (-full * active_f).astype(bf16)
        left = jnp.concatenate([coarse, fine, pulled], axis=0)
        for k in range(layers):
            by_hidden[k] = by_hidden[k] + dot_nn(left, pieces[k][m, 0])
            by_close[k] = by_close[k] + dot_nn(active, pieces[k][m, 1])
        for i in range(inner):
            factor = jnp.where(above[i], scale(1 + i), 1.0)
            other = (others[i].astype(f32) * factor).astype(bf16)
            mate = jnp.where(above[i], active_f, coarse.astype(f32)).astype(bf16)
            cross[i] = cross[i] + dot_nt(mate, other)
        for n in range(inner):
            held = others[n]
            if n >= 1:
                held = jnp.where(section < n, extras[n - 1].astype(f32), held.astype(f32))
            held = jnp.where(section == n, active_f, held.astype(f32)).astype(bf16)
            drag[n] = drag[n] + dot_nt((-weight(n) * active_f).astype(bf16), held)
    for k in range(layers):
        down = by_hidden[k][:K] + by_hidden[k][K : 2 * K]
        up = by_close[k] + by_hidden[k][2 * K :]
        for i in range(inner):
            index = jnp.where(above[i], other_of[i], layers + other_of[i])
            term = dot_nn(cross[i].astype(bf16), both[k, index])
            up = up + jnp.where(above[i], term, 0.0)
            down = down + jnp.where(above[i], 0.0, term)
            up = up + dot_nn(drag[i].astype(bf16), both[k, layers + i])
        down = down * gain[k]
        for part in range(group):
            here = slice(part * width, (part + 1) * width)
            slot = (section ^ k) * group + part
            parcel[slot, 0] = down[:, here]
            parcel[slot, 1] = up[:, here]
    if len(outs) == 1:
        outs[0][...] = parcel[...]
    else:
        for r, out in enumerate(outs):
            out[...] = parcel[own_slot ^ r].astype(out.dtype)


def per_device(inputs_down, inputs_up, cotan_down, cotan_up, norm_gains, adapt_down, adapt_up):
    sections = lax.axis_size("section")
    replicas = lax.axis_size("dp")
    section = lax.axis_index("section")
    replica = lax.axis_index("dp")
    layers = sections
    chunks = replicas // sections
    group = chunks // MEMBERS
    slots = replicas // MEMBERS
    bottle = adapt_down.shape[1]
    features = adapt_down.shape[2]
    share = features // sections
    width = features // replicas
    columns = group * width
    label, slot = label_slot(replica, group, chunks)
    micro, tokens = inputs_down.shape[0], inputs_down.shape[1]
    half = micro * tokens
    rows = 2 * half
    inner = layers - 1
    aligned = width % 128 == 0
    params = pltpu.CompilerParams(vmem_limit_bytes=VMEM_BYTES)

    own = (norm_gains[:, None, :], adapt_down, adapt_up)
    weights = [own]
    for k in range(1, sections):
        weights.append(tuple(from_partner(w, "section", k) for w in own))
    flat = [w for ws in weights for w in ws]

    acts = (inputs_down, inputs_up, cotan_down, cotan_up)
    if aligned:
        both, *packed = pl.pallas_call(
            functools.partial(pack_kernel, width, group, chunks),
            out_shape=[pltpu.VMEM((2, rows, share), bf16)]
            + [pltpu.VMEM((2, rows, columns), bf16)] * MEMBERS,
            in_specs=[IN_HBM] * 4,
            out_specs=[IN_VMEM] * (1 + MEMBERS),
            scratch_shapes=[pltpu.SemaphoreType.DMA((4 * micro,))],
            compiler_params=params,
            name="pack",
        )(*[pltpu.with_memory_space_constraint(v, pltpu.HBM) for v in acts])
    else:
        both = jnp.concatenate([v.reshape(half, share) for v in acts], axis=0)
        both = both.reshape(2, rows, share)
        parts = both.reshape(2, rows, chunks, width)
        packed = []
        for k in range(MEMBERS):
            cuts = [
                lax.dynamic_index_in_dim(
                    parts, chunk_of(label ^ k, part, section), 2, keepdims=False
                )
                for part in range(group)
            ]
            packed.append(jnp.concatenate(cuts, axis=2))
    pieces = [packed[0]]
    for k in range(1, MEMBERS):
        pieces.append(from_partner(packed[k], "dp", LEADERS[k]))
    prod_rows = (3 * layers - 1) * bottle + 8
    gram_side = 2 * max(inner, 1) * bottle
    sides = [(prod_rows, rows), (gram_side, gram_side)]
    if rows == gram_side:
        sides = [(prod_rows + gram_side, rows)]
    sums = pl.pallas_call(
        functools.partial(products_kernel, layers),
        out_shape=[jax.ShapeDtypeStruct(side, f32) for side in sides],
        in_specs=[IN_VMEM] * (1 + 3 * sections),
        out_specs=[IN_VMEM] * len(sides),
        scratch_shapes=[pltpu.VMEM((layers, bottle, share), bf16)] * 3,
        compiler_params=params,
        cost_estimate=cost(COST_PRODUCTS),
        name="products",
    )(both, *flat)
    sums = list(sums)
    for k in range(1, sections):
        sums += [from_partner(v, "section", k) for v in sums[: len(sides)]]

    tail = inner + 2 * layers
    coef_rows = (2 + inner + max(inner - 1, 0)) * bottle + -(-tail // 16) * 16
    coef = pl.pallas_call(
        functools.partial(relay_kernel, layers, bottle, features, sections),
        out_shape=jax.ShapeDtypeStruct((coef_rows, rows), bf16),
        in_specs=[IN_VMEM] * len(sums),
        out_specs=IN_VMEM,
        scratch_shapes=[pltpu.VMEM((2 * layers, bottle, rows), bf16)],
        compiler_params=params,
        cost_estimate=cost(COST_SMALL),
        name="relay",
    )(*sums)
    coefs = [coef] + [from_partner(coef, "dp", LEADERS[k]) for k in range(1, MEMBERS)]
    cut_shapes = [
        jax.ShapeDtypeStruct((layers, 1, columns), f32),
        jax.ShapeDtypeStruct((layers, 2 * layers, bottle, columns), bf16),
    ]
    if aligned:
        gain_cut, both_cut = pl.pallas_call(
            functools.partial(cut_kernel, layers, width, group, chunks),
            out_shape=cut_shapes,
            in_specs=[IN_VMEM] * len(flat),
            out_specs=[IN_VMEM] * 2,
            compiler_params=params,
            cost_estimate=cost(COST_SMALL),
            name="cut",
        )(*flat)
    else:
        gain_cut = jnp.zeros(cut_shapes[0].shape, f32)
        both_cut = jnp.zeros(cut_shapes[1].shape, bf16)
        for k in range(layers):
            for part in range(group):
                at = section ^ k
                chunk = at * chunks + chunk_of(label, part, at)
                for w, ws in enumerate(weights):
                    gain, down, up = (
                        lax.dynamic_index_in_dim(
                            v[0].reshape(v.shape[1], replicas, width), chunk, 1, keepdims=False
                        )
                        for v in ws
                    )
                    low = (gain.astype(f32) * down.astype(f32)).astype(bf16)
                    layer = section ^ w
                    spot = (k, layer, 0, part * width)
                    both_cut = lax.dynamic_update_slice(both_cut, low[None, None], spot)
                    spot = (k, layers + layer, 0, part * width)
                    both_cut = lax.dynamic_update_slice(both_cut, up[None, None], spot)
                    if w == 0:
                        gain_cut = lax.dynamic_update_slice(
                            gain_cut, gain.astype(f32)[None], (k, 0, part * width)
                        )

    pieces = list(lax.optimization_barrier((*pieces, coef))[:-1])
    stacked = pl.pallas_call(
        stack_kernel,
        out_shape=jax.ShapeDtypeStruct((MEMBERS, 2, rows, columns), bf16),
        in_specs=[IN_VMEM] * MEMBERS,
        out_specs=IN_VMEM,
        compiler_params=params,
        cost_estimate=cost(COST_SMALL),
        name="stack",
    )(*pieces)
    pieces = [stacked] + [from_partner(stacked, "section", k) for k in range(1, sections)]

    message = (2, bottle, width)
    if aligned:
        sends = [(message, f32)] + [(message, bf16)] * (slots - 1)
    else:
        sends = [((slots,) + message, f32)]
    operands = (*coefs, *pieces, gain_cut, both_cut)
    parcels = pl.pallas_call(
        functools.partial(grads_kernel, layers, bottle, width, group, chunks),
        out_shape=[jax.ShapeDtypeStruct(s, d) for s, d in sends],
        in_specs=[IN_VMEM] * len(operands),
        out_specs=[IN_VMEM] * len(sends),
        scratch_shapes=[pltpu.VMEM((slots,) + message, f32)],
        compiler_params=params,
        name="grads",
    )(*operands)
    if not aligned:
        parcels = [
            lax.dynamic_index_in_dim(parcels[0], slot ^ r, 0, keepdims=False)
            for r in range(slots)
        ]
        parcels[1:] = [v.astype(bf16) for v in parcels[1:]]

    total = parcels[0]
    for r in range(1, slots):
        received = from_partner(parcels[r], "dp", mask(r, group, chunks))
        total = total + received.astype(f32)
    return (total[0][None], total[1][None])


def solution(mesh):
    placed = (
        P(None, "dp", "section"),
        P(None, "dp", "section"),
        P(None, "dp", "section"),
        P(None, "dp", "section"),
        P("section", None),
        P("section", None, None),
        P("section", None, None),
    )
    return jax.shard_map(
        per_device,
        mesh=mesh,
        in_specs=placed,
        out_specs=(P("section", None, "dp"), P("section", None, "dp")),
        check_vma=False,
    )
```

```python
import functools

import jax
import jax.numpy as jnp
from jax import lax
from jax.experimental import pallas as pl
from jax.experimental.pallas import tpu as pltpu
from jax.sharding import PartitionSpec as P

epsilon = 1e-05
VMEM_BYTES = 32 * 1024 * 1024
MEMBERS = 4
STAR = True
TWIST = 0
COST_PRODUCTS = 12
COST_SMALL = 0.1
COST_GRADS = 10
f32 = jnp.float32
bf16 = jnp.bfloat16
IN_VMEM = pl.BlockSpec(memory_space=pltpu.VMEM)
IN_HBM = pl.BlockSpec(memory_space=pltpu.HBM)


def cost(micros):
    return pl.CostEstimate(flops=int(micros * 1.1e9), bytes_accessed=0, transcendentals=0)


def from_partner(value, axis, flip):
    return lax.ppermute(value, axis, [(i, i ^ flip) for i in range(lax.axis_size(axis))])


def dot_nn(left, right):
    return lax.dot_general(left, right, (((1,), (0,)), ((), ())), preferred_element_type=f32)


def dot_nt(left, right):
    return lax.dot_general(left, right, (((1,), (1,)), ((), ())), preferred_element_type=f32)


def split(value):
    high = value.astype(bf16)
    return high, (value - high.astype(f32)).astype(bf16)


def dot_tn(left, right):
    return lax.dot_general(left, right, (((0,), (0,)), ((), ())), preferred_element_type=f32)


def dot_split(left, right, dot=dot_nn):
    high, low = split(left)
    return dot(high, right) + dot(low, right)


LEADERS = (0, 1, 2, 4) if STAR else (0, 1, 2, 3)


def leader(label):
    return label + (label == 3) if STAR else label


def mask(slot, group, chunks):
    section, part = divmod(slot, group)
    low = (part & 1) * 7 + (part >> 1) * 8 if STAR else part * 4
    return section * chunks ^ (section & 1) * TWIST ^ low


def label_slot(replica, group, chunks):
    section = replica // chunks
    local = replica % chunks ^ (section & 1) * TWIST
    if not STAR:
        return local % 4, section * group + local // 4
    low = local & 7
    label = (low & 3) ^ (low >> 2) * 3
    odd = (low != 0) & (low != 1) & (low != 2) & (low != 4)
    return label, section * group + (local >> 3) * 2 + odd.astype(jnp.int32)


def whereabouts(group, chunks):
    section = lax.axis_index("section")
    label, slot = label_slot(lax.axis_index("dp"), group, chunks)
    return section, label, slot


def chunk_of(label, part, section):
    low = (part & 1) * 7 + (part >> 1) * 8 if STAR else part * 4
    return leader(label) ^ low ^ (section & 1) * TWIST


def pack_kernel(width, group, chunks, *refs):
    acts, gain = refs[:4], refs[4]
    both, gain_out = refs[5:7]
    outs = refs[7:-1]
    sems = refs[-1]
    micro, tokens = acts[0].shape[0], acts[0].shape[1]
    section, label, _ = whereabouts(group, chunks)
    copies = []
    for a, act in enumerate(acts):
        for m in range(micro):
            start = ((a % 2) * micro + m) * tokens
            copies.append(
                pltpu.make_async_copy(
                    act.at[m], both.at[a // 2, pl.ds(start, tokens)], sems.at[len(copies)]
                )
            )
            copies[-1].start()
    last = pltpu.make_async_copy(gain, gain_out, sems.at[len(copies)])
    last.start()
    for n, copy in enumerate(copies):
        copy.wait()
        a, m = divmod(n, micro)
        start = ((a % 2) * micro + m) * tokens
        for k, out in enumerate(outs):
            for part in range(group):
                chunk = chunk_of(label ^ k, part, section)
                span = pl.ds(pl.multiple_of(chunk * width, width), width)
                out[a // 2, start : start + tokens, part * width : (part + 1) * width] = both[
                    a // 2, start : start + tokens, span
                ]
    last.wait()


def two_parts(refs):
    if len(refs) == 2:
        return refs
    height, side = refs[0].shape
    return refs[0].at[: height - side // 2], refs[0].at[height - side // 2 :]


def products_kernel(layers, *refs):
    acts = refs[0]
    weights = [refs[1 + 3 * k : 4 + 3 * k] for k in range(layers)]
    outs = refs[1 + 3 * layers : -3]
    prod_out, gram_out = two_parts(outs)
    low_scr, fine_scr, high_scr = refs[-3:]
    bottle = weights[0][1].shape[1]
    features = acts.shape[2]
    section = lax.axis_index("section")
    mine = pl.ds(pl.multiple_of(section * features, features), features)
    for k in range(layers):
        gain, down, up = weights[k]
        layer = section ^ k
        exact = gain[0, :, mine].astype(f32) * down[0, :, mine].astype(f32)
        low, fine = split(exact)
        low_scr[layer] = low
        fine_scr[layer] = fine
        high_scr[layer] = up[0, :, mine]
    hidden = acts[0]
    low_all = low_scr[...].reshape(layers * bottle, features)
    fine_all = fine_scr[...].reshape(layers * bottle, features)
    high_all = high_scr[...].reshape(layers * bottle, features)
    size = (layers - 1) * bottle
    at = layers * bottle
    prod_out[:at] = dot_nt(low_all, hidden) + dot_nt(fine_all, hidden)
    if layers > 1:
        prod_out[at : at + size] = dot_nt(high_all[:size], hidden)
    at += size
    prod_out[at : at + layers * bottle] = dot_nt(high_all, acts[1])
    at += layers * bottle
    square = dot_nt(hidden, hidden)
    eye = lax.broadcasted_iota(jnp.int32, square.shape, 0) == lax.broadcasted_iota(
        jnp.int32, square.shape, 1
    )
    norms = jnp.sum(jnp.where(eye, square, 0.0), axis=0, keepdims=True)
    prod_out[at : at + 8] = jnp.broadcast_to(norms, (8, norms.shape[1]))
    if layers > 1:
        high_part = high_all[:size]
        low_part = low_all[bottle:]
        fine_part = fine_all[bottle:]
        gram_out[:, :size] = dot_nt(high_part, low_part) + dot_nt(high_part, fine_part)
        gram_out[:, size:] = dot_nt(high_part, high_part)
    else:
        gram_out[...] = jnp.zeros_like(gram_out)


def relay_kernel(layers, bottle, features, sections, *refs):
    coef_out, hold = refs[-2:]
    each = (len(refs) - 2) // sections
    prods, grams = zip(
        *(two_parts(refs[each * k : each * (k + 1)]) for k in range(sections)), strict=True
    )
    section = lax.axis_index("section")
    prod = sum((ref[...] for ref in prods[1:]), prods[0][...])
    gram = sum((ref[...] for ref in grams[1:]), grams[0][...])
    K = bottle
    inner = layers - 1
    h_low = [prod[l * K : (l + 1) * K] for l in range(layers)]
    at = layers * K
    h_high = [prod[at + l * K : at + (l + 1) * K] for l in range(inner)]
    at += inner * K
    u_high = [prod[at + l * K : at + (l + 1) * K] for l in range(layers)]
    at += layers * K
    norm = prod[at : at + 1]

    def high_low(m, l):
        return gram[m * K : (m + 1) * K, (l - 1) * K : l * K]

    def high_high(m, n):
        return gram[m * K : (m + 1) * K, (inner + n) * K : (inner + n + 1) * K]

    inverses, bottles, hidden_high = [], [], []
    for l in range(layers):
        inverse = lax.rsqrt(jnp.maximum(norm, 0.0) * (1.0 / features) + epsilon)
        value = h_low[l] * inverse
        active = (value * jax.nn.sigmoid(value)).astype(bf16)
        inverses.append(inverse)
        bottles.append(value)
        hold[l] = active
        hidden_high.append(list(h_high))
        if l < inner:
            before = h_high[l]
            h_high = [h_high[n] + dot_split(high_high(n, l), active) for n in range(inner)]
            for n in range(l + 1, layers):
                h_low[n] = h_low[n] + dot_split(high_low(l, n), active, dot_tn)
            norm = norm + jnp.sum(
                active.astype(f32) * (before + h_high[l]), axis=0, keepdims=True
            )
    pulls = [None] * layers
    for l in range(layers - 1, -1, -1):
        sigma = jax.nn.sigmoid(bottles[l])
        coarse = (u_high[l] * sigma * (1.0 + bottles[l] * (1.0 - sigma))).astype(bf16)
        hold[layers + l] = coarse
        if l == 0:
            break
        grad = coarse.astype(f32)
        scaled, fine = split(grad * inverses[l])
        pull = (
            inverses[l]
            * inverses[l]
            * jnp.sum(grad * bottles[l], axis=0, keepdims=True)
            * (1.0 / features)
        )
        pulls[l] = pull
        for n in range(l):
            u_high[n] = (
                u_high[n]
                + dot_split(high_low(n, l), scaled)
                + dot_nn(high_low(n, l).astype(bf16), fine)
                - pull * hidden_high[l][n]
            )
    blocks = [hold[layers + section], hold[section]]
    for i in range(inner):
        other = i + jnp.where(section <= i, 1, 0)
        blocks.append(hold[jnp.where(section <= i, layers + other, other)])
    blocks += [hold[n] for n in range(1, inner)]
    for n, block in enumerate(blocks):
        coef_out[n * K : (n + 1) * K] = block

    def inverse_at(layer):
        value = inverses[0]
        for l in range(1, layers):
            value = jnp.where(layer == l, inverses[l], value)
        return value

    lines = [line.astype(bf16).astype(f32) for line in pulls[1:]]
    scales = [inverse_at(section)]
    scales += [inverse_at(i + jnp.where(section <= i, 1, 0)) for i in range(inner)]
    for scale in scales:
        lines.extend(part.astype(f32) for part in split(scale))
    tail = coef_out.shape[0] - len(blocks) * K
    lines += [jnp.zeros_like(norm)] * (tail - len(lines))
    coef_out[len(blocks) * K :] = jnp.concatenate(lines, axis=0).astype(bf16)


def cut_kernel(layers, width, group, chunks, *refs):
    weights = [refs[3 * k : 3 * k + 3] for k in range(layers)]
    gain_out, both_out = refs[3 * layers :]
    here_section, label, _ = whereabouts(group, chunks)
    for k in range(layers):
        section = here_section ^ k
        for part in range(group):
            chunk = section * chunks + chunk_of(label, part, section)
            span = pl.ds(pl.multiple_of(chunk * width, width), width)
            here = slice(part * width, (part + 1) * width)
            gain_out[k, :, here] = weights[0][0][0, :, span].astype(f32)
            for w in range(layers):
                gain, down, up = weights[w]
                layer = here_section ^ w
                low = gain[0, :, span].astype(f32) * down[0, :, span].astype(f32)
                both_out[k, layer, :, here] = low.astype(bf16)
                both_out[k, layers + layer, :, here] = up[0, :, span]


def stack_kernel(*refs):
    for k, ref in enumerate(refs[:-1]):
        refs[-1][k] = ref[...]


def factors_kernel_part(layers, bottle, section, coefs, lefts, mates):
    K = bottle
    inner = layers - 1
    above = [section <= i for i in range(inner)]
    cross = [0.0] * inner
    drag = [0.0] * inner
    for m in range(MEMBERS):
        coef = coefs[m][...]
        grad, active = coef[:K], coef[K : 2 * K]
        others = [coef[(2 + i) * K : (3 + i) * K] for i in range(inner)]
        extras = [coef[(1 + layers + i) * K : (2 + layers + i) * K] for i in range(inner - 1)]
        at = (2 + inner + max(inner - 1, 0)) * K
        lines = coef[at:].astype(f32)
        active_f = active.astype(f32)

        def scale(i):
            row = inner + 2 * i
            return lines[row : row + 1] + lines[row + 1 : row + 2]

        def weight(n):
            total = jnp.zeros_like(lines[:1])
            for l in range(n + 1, layers):
                total = total + jnp.where(section < l, lines[l - 1 : l], 0.0)
            return total

        coarse, fine = split(grad.astype(f32) * scale(0))
        lefts[m, :K] = coarse
        lefts[m, K : 2 * K] = fine
        lefts[m, 2 * K : 3 * K] = (-weight(0) * active_f).astype(bf16)
        lefts[m, 3 * K :] = active
        for i in range(inner):
            factor = jnp.where(above[i], scale(1 + i), 1.0)
            other = (others[i].astype(f32) * factor).astype(bf16)
            mate = jnp.where(above[i], active_f, coarse.astype(f32)).astype(bf16)
            cross[i] = cross[i] + dot_nt(mate, other)
        for n in range(inner):
            held = others[n]
            if n >= 1:
                held = jnp.where(section < n, extras[n - 1].astype(f32), held.astype(f32))
            held = jnp.where(section == n, active_f, held.astype(f32)).astype(bf16)
            drag[n] = drag[n] + dot_nt((-weight(n) * active_f).astype(bf16), held)
    for i in range(inner):
        mates[2 * i] = cross[i].astype(bf16)
        mates[2 * i + 1] = drag[i].astype(bf16)


def grads_kernel(layers, bottle, width, group, chunks, turn, *refs):
    K = bottle
    inner = layers - 1
    section, _, own_slot = whereabouts(group, chunks)
    final = turn == layers - 1
    if turn == 0:
        coefs, refs = refs[:MEMBERS], refs[MEMBERS:]
        pieces, refs = refs[:MEMBERS], refs[MEMBERS:]
        gain, both, *outs, lefts, mates = refs
        factors_kernel_part(layers, bottle, section, coefs, lefts, mates)
        pieces = [ref[...] for ref in pieces]
        before = []
    else:
        lefts, mates, pieces, gain, both = refs[:5]
        before, outs = refs[5 : 5 + turn], list(refs[5 + turn :])
        pieces = [pieces[m] for m in range(MEMBERS)]
    parcel = outs.pop() if final else outs[0]
    by_hidden, by_close = 0.0, 0.0
    for m in range(MEMBERS):
        by_hidden = by_hidden + dot_nn(lefts[m, : 3 * K], pieces[m][0])
        by_close = by_close + dot_nn(lefts[m, 3 * K :], pieces[m][1])
    down = by_hidden[:K] + by_hidden[K : 2 * K]
    up = by_close + by_hidden[2 * K :]
    for i in range(inner):
        above = section <= i
        other = i + jnp.where(above, 1, 0)
        term = dot_nn(mates[2 * i], both[turn, jnp.where(above, other, layers + other)])
        up = up + jnp.where(above, term, 0.0)
        down = down + jnp.where(above, 0.0, term)
        up = up + dot_nn(mates[2 * i + 1], both[turn, layers + i])
    down = down * gain[turn]
    start = (section ^ turn) * group if final else 0
    for part in range(group):
        here = slice(part * width, (part + 1) * width)
        parcel[start + part, 0] = down[:, here]
        parcel[start + part, 1] = up[:, here]
    if not final:
        return
    for k, ref in enumerate(before):
        for part in range(group):
            parcel[(section ^ k) * group + part] = ref[part]
    if len(outs) == 1:
        outs[0][...] = parcel[...]
    else:
        for r, out in enumerate(outs):
            out[...] = parcel[own_slot ^ r].astype(out.dtype)


def per_device(inputs_down, inputs_up, cotan_down, cotan_up, norm_gains, adapt_down, adapt_up):
    sections = lax.axis_size("section")
    replicas = lax.axis_size("dp")
    section = lax.axis_index("section")
    replica = lax.axis_index("dp")
    layers = sections
    chunks = replicas // sections
    group = chunks // MEMBERS
    slots = replicas // MEMBERS
    bottle = adapt_down.shape[1]
    features = adapt_down.shape[2]
    share = features // sections
    width = features // replicas
    columns = group * width
    label, slot = label_slot(replica, group, chunks)
    micro, tokens = inputs_down.shape[0], inputs_down.shape[1]
    half = micro * tokens
    rows = 2 * half
    inner = layers - 1
    aligned = width % 128 == 0
    params = pltpu.CompilerParams(vmem_limit_bytes=VMEM_BYTES)

    own = (norm_gains[:, None, :], adapt_down, adapt_up)
    weights = [own]
    for k in range(1, sections):
        weights.append(tuple(from_partner(w, "section", k) for w in own))
    acts = (inputs_down, inputs_up, cotan_down, cotan_up)
    if aligned:
        both, gain, *packed = pl.pallas_call(
            functools.partial(pack_kernel, width, group, chunks),
            out_shape=[pltpu.VMEM((2, rows, share), bf16), pltpu.VMEM(own[0].shape, bf16)]
            + [pltpu.VMEM((2, rows, columns), bf16)] * MEMBERS,
            in_specs=[IN_HBM] * 5,
            out_specs=[IN_VMEM] * (2 + MEMBERS),
            scratch_shapes=[pltpu.SemaphoreType.DMA((4 * micro + 1,))],
            compiler_params=params,
            name="pack",
        )(*[pltpu.with_memory_space_constraint(v, pltpu.HBM) for v in (*acts, own[0])])
        weights[0] = (gain, *own[1:])
    else:
        both = jnp.concatenate([v.reshape(half, share) for v in acts], axis=0)
        both = both.reshape(2, rows, share)
        parts = both.reshape(2, rows, chunks, width)
        packed = []
        for k in range(MEMBERS):
            cuts = [
                lax.dynamic_index_in_dim(
                    parts, chunk_of(label ^ k, part, section), 2, keepdims=False
                )
                for part in range(group)
            ]
            packed.append(jnp.concatenate(cuts, axis=2))
    flat = [w for ws in weights for w in ws]
    pieces = [packed[0]]
    for k in range(1, MEMBERS):
        pieces.append(from_partner(packed[k], "dp", LEADERS[k]))
    prod_rows = (3 * layers - 1) * bottle + 8
    gram_rows = max(inner, 1) * bottle
    sides = [(prod_rows, rows), (gram_rows, 2 * gram_rows)]
    if rows == 2 * gram_rows:
        sides = [(prod_rows + gram_rows, rows)]
    sums = pl.pallas_call(
        functools.partial(products_kernel, layers),
        out_shape=[jax.ShapeDtypeStruct(side, f32) for side in sides],
        in_specs=[IN_VMEM] * (1 + 3 * sections),
        out_specs=[IN_VMEM] * len(sides),
        scratch_shapes=[pltpu.VMEM((layers, bottle, share), bf16)] * 3,
        compiler_params=params,
        cost_estimate=cost(COST_PRODUCTS),
        name="products",
    )(both, *flat)
    sums = list(sums)
    for k in range(1, sections):
        sums += [from_partner(v, "section", k) for v in sums[: len(sides)]]

    tail = inner + 2 * layers
    coef_rows = (2 + inner + max(inner - 1, 0)) * bottle + -(-tail // 16) * 16
    coef = pl.pallas_call(
        functools.partial(relay_kernel, layers, bottle, features, sections),
        out_shape=jax.ShapeDtypeStruct((coef_rows, rows), bf16),
        in_specs=[IN_VMEM] * len(sums),
        out_specs=IN_VMEM,
        scratch_shapes=[pltpu.VMEM((2 * layers, bottle, rows), bf16)],
        compiler_params=params,
        cost_estimate=cost(COST_SMALL),
        name="relay",
    )(*sums)
    coefs = [coef] + [from_partner(coef, "dp", LEADERS[k]) for k in range(1, MEMBERS)]
    cut_shapes = [
        jax.ShapeDtypeStruct((layers, 1, columns), f32),
        jax.ShapeDtypeStruct((layers, 2 * layers, bottle, columns), bf16),
    ]
    if aligned:
        gain_cut, both_cut = pl.pallas_call(
            functools.partial(cut_kernel, layers, width, group, chunks),
            out_shape=cut_shapes,
            in_specs=[IN_VMEM] * len(flat),
            out_specs=[IN_VMEM] * 2,
            compiler_params=params,
            cost_estimate=cost(COST_SMALL),
            name="cut",
        )(*flat)
    else:
        gain_cut = jnp.zeros(cut_shapes[0].shape, f32)
        both_cut = jnp.zeros(cut_shapes[1].shape, bf16)
        for k in range(layers):
            for part in range(group):
                at = section ^ k
                chunk = at * chunks + chunk_of(label, part, at)
                for w, ws in enumerate(weights):
                    gain, down, up = (
                        lax.dynamic_index_in_dim(
                            v[0].reshape(v.shape[1], replicas, width), chunk, 1, keepdims=False
                        )
                        for v in ws
                    )
                    low = (gain.astype(f32) * down.astype(f32)).astype(bf16)
                    layer = section ^ w
                    spot = (k, layer, 0, part * width)
                    both_cut = lax.dynamic_update_slice(both_cut, low[None, None], spot)
                    spot = (k, layers + layer, 0, part * width)
                    both_cut = lax.dynamic_update_slice(both_cut, up[None, None], spot)
                    if w == 0:
                        gain_cut = lax.dynamic_update_slice(
                            gain_cut, gain.astype(f32)[None], (k, 0, part * width)
                        )

    gated = list(lax.optimization_barrier((*pieces, coef))[:-1])
    stacked = pl.pallas_call(
        stack_kernel,
        out_shape=jax.ShapeDtypeStruct((MEMBERS, 2, rows, columns), bf16),
        in_specs=[IN_VMEM] * MEMBERS,
        out_specs=IN_VMEM,
        compiler_params=params,
        cost_estimate=cost(COST_SMALL),
        name="stack",
    )(*gated)
    handed = [None] + [from_partner(stacked, "section", k) for k in range(1, sections)]

    message = (2, bottle, width)
    left_shape = jax.ShapeDtypeStruct((MEMBERS, 4 * bottle, rows), bf16)
    mate_shape = jax.ShapeDtypeStruct((max(2 * inner, 1), bottle, bottle), bf16)
    held = jax.ShapeDtypeStruct((group,) + message, f32)
    before = []
    for k in range(sections):
        shapes, scratch = [held], []
        if k == sections - 1:
            scratch = [pltpu.VMEM((slots,) + message, f32)]
            shapes = [jax.ShapeDtypeStruct((slots,) + message, f32)]
            if aligned:
                shapes = [jax.ShapeDtypeStruct(message, f32)]
                shapes += [jax.ShapeDtypeStruct(message, bf16)] * (slots - 1)
        if k == 0:
            shapes += [left_shape, mate_shape]
            operands = (*coefs, *pieces, gain_cut, both_cut)
        else:
            operands = (lefts, mates, handed[k], gain_cut, both_cut, *before)
        parcels = pl.pallas_call(
            functools.partial(grads_kernel, layers, bottle, width, group, chunks, k),
            out_shape=shapes,
            in_specs=[IN_VMEM] * len(operands),
            out_specs=[IN_VMEM] * len(shapes),
            scratch_shapes=scratch,
            compiler_params=params,
            cost_estimate=cost(COST_GRADS),
            name="grads",
        )(*operands)
        if k == 0:
            *parcels, lefts, mates = parcels
        if k < sections - 1:
            before += parcels
    if not aligned:
        parcels = [
            lax.dynamic_index_in_dim(parcels[0], slot ^ r, 0, keepdims=False)
            for r in range(slots)
        ]
        parcels[1:] = [v.astype(bf16) for v in parcels[1:]]

    total = parcels[0]
    for r in range(1, slots):
        received = from_partner(parcels[r], "dp", mask(r, group, chunks))
        total = total + received.astype(f32)
    return (total[0][None], total[1][None])


def solution(mesh):
    placed = (
        P(None, "dp", "section"),
        P(None, "dp", "section"),
        P(None, "dp", "section"),
        P(None, "dp", "section"),
        P("section", None),
        P("section", None, None),
        P("section", None, None),
    )
    return jax.shard_map(
        per_device,
        mesh=mesh,
        in_specs=placed,
        out_specs=(P("section", None, "dp"), P("section", None, "dp")),
        check_vma=False,
    )
```

```python
import functools

import jax
import jax.numpy as jnp
from jax import lax
from jax.experimental import pallas as pl
from jax.experimental.pallas import tpu as pltpu
from jax.sharding import PartitionSpec as P

epsilon = 1e-05
VMEM_BYTES = 32 * 1024 * 1024
MEMBERS = 4
STAR = True
TWIST = 0
COST_PRODUCTS = 12
COST_SMALL = 0.1
COST_GRADS = 10
f32 = jnp.float32
bf16 = jnp.bfloat16
IN_VMEM = pl.BlockSpec(memory_space=pltpu.VMEM)
IN_HBM = pl.BlockSpec(memory_space=pltpu.HBM)


def cost(micros):
    return pl.CostEstimate(flops=int(micros * 1.1e9), bytes_accessed=0, transcendentals=0)


def from_partner(value, axis, flip):
    return lax.ppermute(value, axis, [(i, i ^ flip) for i in range(lax.axis_size(axis))])


def dot_nn(left, right):
    return lax.dot_general(left, right, (((1,), (0,)), ((), ())), preferred_element_type=f32)


def dot_nt(left, right):
    return lax.dot_general(left, right, (((1,), (1,)), ((), ())), preferred_element_type=f32)


def split(value):
    high = value.astype(bf16)
    return high, (value - high.astype(f32)).astype(bf16)


def dot_tn(left, right):
    return lax.dot_general(left, right, (((0,), (0,)), ((), ())), preferred_element_type=f32)


def dot_split(left, right, dot=dot_nn):
    high, low = split(left)
    return dot(high, right) + dot(low, right)


LEADERS = (0, 1, 2, 4) if STAR else (0, 1, 2, 3)


def leader(label):
    return label + (label == 3) if STAR else label


def mask(slot, group, chunks):
    section, part = divmod(slot, group)
    low = (part & 1) * 7 + (part >> 1) * 8 if STAR else part * 4
    return section * chunks ^ (section & 1) * TWIST ^ low


def label_slot(replica, group, chunks):
    section = replica // chunks
    local = replica % chunks ^ (section & 1) * TWIST
    if not STAR:
        return local % 4, section * group + local // 4
    low = local & 7
    label = (low & 3) ^ (low >> 2) * 3
    odd = (low != 0) & (low != 1) & (low != 2) & (low != 4)
    return label, section * group + (local >> 3) * 2 + odd.astype(jnp.int32)


def whereabouts(group, chunks):
    section = lax.axis_index("section")
    label, slot = label_slot(lax.axis_index("dp"), group, chunks)
    return section, label, slot


def chunk_of(label, part, section):
    low = (part & 1) * 7 + (part >> 1) * 8 if STAR else part * 4
    return leader(label) ^ low ^ (section & 1) * TWIST


def pack_kernel(width, group, chunks, *refs):
    acts, gain, down = refs[:4], refs[4], refs[5]
    both, tall = refs[6:8]
    outs = refs[8:-2]
    line, sems = refs[-2:]
    micro, tokens = acts[0].shape[0], acts[0].shape[1]
    bottle = down.shape[1]
    section, label, _ = whereabouts(group, chunks)
    copies = []
    for a, act in enumerate(acts):
        for m in range(micro):
            start = ((a % 2) * micro + m) * tokens
            copies.append(
                pltpu.make_async_copy(
                    act.at[m], both.at[a // 2, pl.ds(start, tokens)], sems.at[len(copies)]
                )
            )
    count = len(copies)
    copies.append(pltpu.make_async_copy(gain.at[0], line, sems.at[count]))
    copies.append(
        pltpu.make_async_copy(down.at[0], tall.at[pl.ds(0, bottle)], sems.at[count + 1])
    )
    for copy in copies:
        copy.start()
    for n in range(count):
        copies[n].wait()
        a, m = divmod(n, micro)
        start = ((a % 2) * micro + m) * tokens
        for k, out in enumerate(outs):
            for part in range(group):
                chunk = chunk_of(label ^ k, part, section)
                span = pl.ds(pl.multiple_of(chunk * width, width), width)
                out[a // 2, start : start + tokens, part * width : (part + 1) * width] = both[
                    a // 2, start : start + tokens, span
                ]
    copies[count].wait()
    tall[bottle:] = jnp.broadcast_to(line[...], (tall.shape[0] - bottle, tall.shape[1]))
    copies[count + 1].wait()


def two_parts(refs):
    if len(refs) == 2:
        return refs
    height, side = refs[0].shape
    return refs[0].at[: height - side // 2], refs[0].at[height - side // 2 :]


def products_kernel(layers, *refs):
    acts = refs[0]
    weights = [refs[1 + 2 * k : 3 + 2 * k] for k in range(layers)]
    outs = refs[1 + 2 * layers : -3]
    prod_out, gram_out = two_parts(outs)
    low_scr, fine_scr, high_scr = refs[-3:]
    bottle = weights[0][1].shape[1]
    gain_row = slice(bottle, bottle + 1)
    features = acts.shape[2]
    section = lax.axis_index("section")
    mine = pl.ds(pl.multiple_of(section * features, features), features)
    for k in range(layers):
        tall, up = weights[k]
        layer = section ^ k
        exact = tall[gain_row, mine].astype(f32) * tall[:bottle, mine].astype(f32)
        low, fine = split(exact)
        low_scr[layer] = low
        fine_scr[layer] = fine
        high_scr[layer] = up[0, :, mine]
    hidden = acts[0]
    low_all = low_scr[...].reshape(layers * bottle, features)
    fine_all = fine_scr[...].reshape(layers * bottle, features)
    high_all = high_scr[...].reshape(layers * bottle, features)
    size = (layers - 1) * bottle
    at = layers * bottle
    prod_out[:at] = dot_nt(low_all, hidden) + dot_nt(fine_all, hidden)
    if layers > 1:
        prod_out[at : at + size] = dot_nt(high_all[:size], hidden)
    at += size
    prod_out[at : at + layers * bottle] = dot_nt(high_all, acts[1])
    at += layers * bottle
    square = dot_nt(hidden, hidden)
    eye = lax.broadcasted_iota(jnp.int32, square.shape, 0) == lax.broadcasted_iota(
        jnp.int32, square.shape, 1
    )
    norms = jnp.sum(jnp.where(eye, square, 0.0), axis=0, keepdims=True)
    prod_out[at : at + 8] = jnp.broadcast_to(norms, (8, norms.shape[1]))
    if layers > 1:
        high_part = high_all[:size]
        low_part = low_all[bottle:]
        fine_part = fine_all[bottle:]
        gram_out[:, :size] = dot_nt(high_part, low_part) + dot_nt(high_part, fine_part)
        gram_out[:, size:] = dot_nt(high_part, high_part)
    else:
        gram_out[...] = jnp.zeros_like(gram_out)


def relay_kernel(layers, bottle, features, sections, *refs):
    coef_out, hold = refs[-2:]
    each = (len(refs) - 2) // sections
    prods, grams = zip(
        *(two_parts(refs[each * k : each * (k + 1)]) for k in range(sections)), strict=True
    )
    section = lax.axis_index("section")
    prod = sum((ref[...] for ref in prods[1:]), prods[0][...])
    gram = sum((ref[...] for ref in grams[1:]), grams[0][...])
    K = bottle
    inner = layers - 1
    h_low = [prod[l * K : (l + 1) * K] for l in range(layers)]
    at = layers * K
    h_high = [prod[at + l * K : at + (l + 1) * K] for l in range(inner)]
    at += inner * K
    u_high = [prod[at + l * K : at + (l + 1) * K] for l in range(layers)]
    at += layers * K
    norm = prod[at : at + 1]

    def high_low(m, l):
        return gram[m * K : (m + 1) * K, (l - 1) * K : l * K]

    def high_high(m, n):
        return gram[m * K : (m + 1) * K, (inner + n) * K : (inner + n + 1) * K]

    inverses, bottles, hidden_high = [], [], []
    for l in range(layers):
        inverse = lax.rsqrt(jnp.maximum(norm, 0.0) * (1.0 / features) + epsilon)
        value = h_low[l] * inverse
        active = (value * jax.nn.sigmoid(value)).astype(bf16)
        inverses.append(inverse)
        bottles.append(value)
        hold[l] = active
        hidden_high.append(list(h_high))
        if l < inner:
            before = h_high[l]
            h_high = [h_high[n] + dot_split(high_high(n, l), active) for n in range(inner)]
            for n in range(l + 1, layers):
                h_low[n] = h_low[n] + dot_split(high_low(l, n), active, dot_tn)
            norm = norm + jnp.sum(
                active.astype(f32) * (before + h_high[l]), axis=0, keepdims=True
            )
    pulls = [None] * layers
    for l in range(layers - 1, -1, -1):
        sigma = jax.nn.sigmoid(bottles[l])
        coarse = (u_high[l] * sigma * (1.0 + bottles[l] * (1.0 - sigma))).astype(bf16)
        hold[layers + l] = coarse
        if l == 0:
            break
        grad = coarse.astype(f32)
        scaled, fine = split(grad * inverses[l])
        pull = (
            inverses[l]
            * inverses[l]
            * jnp.sum(grad * bottles[l], axis=0, keepdims=True)
            * (1.0 / features)
        )
        pulls[l] = pull
        for n in range(l):
            u_high[n] = (
                u_high[n]
                + dot_split(high_low(n, l), scaled)
                + dot_nn(high_low(n, l).astype(bf16), fine)
                - pull * hidden_high[l][n]
            )
    blocks = [hold[layers + section], hold[section]]
    for i in range(inner):
        other = i + jnp.where(section <= i, 1, 0)
        blocks.append(hold[jnp.where(section <= i, layers + other, other)])
    blocks += [hold[n] for n in range(1, inner)]
    for n, block in enumerate(blocks):
        coef_out[n * K : (n + 1) * K] = block

    def inverse_at(layer):
        value = inverses[0]
        for l in range(1, layers):
            value = jnp.where(layer == l, inverses[l], value)
        return value

    lines = [line.astype(bf16).astype(f32) for line in pulls[1:]]
    scales = [inverse_at(section)]
    scales += [inverse_at(i + jnp.where(section <= i, 1, 0)) for i in range(inner)]
    for scale in scales:
        lines.extend(part.astype(f32) for part in split(scale))
    tail = coef_out.shape[0] - len(blocks) * K
    lines += [jnp.zeros_like(norm)] * (tail - len(lines))
    coef_out[len(blocks) * K :] = jnp.concatenate(lines, axis=0).astype(bf16)


def cut_kernel(layers, width, group, chunks, *refs):
    weights = [refs[2 * k : 2 * k + 2] for k in range(layers)]
    gain_out, both_out = refs[2 * layers :]
    bottle = weights[0][1].shape[1]
    gain_row = slice(bottle, bottle + 1)
    here_section, label, _ = whereabouts(group, chunks)
    for k in range(layers):
        section = here_section ^ k
        for part in range(group):
            chunk = section * chunks + chunk_of(label, part, section)
            span = pl.ds(pl.multiple_of(chunk * width, width), width)
            here = slice(part * width, (part + 1) * width)
            gain_out[k, :, here] = weights[0][0][gain_row, span].astype(f32)
            for w in range(layers):
                tall, up = weights[w]
                layer = here_section ^ w
                low = tall[gain_row, span].astype(f32) * tall[:bottle, span].astype(f32)
                both_out[k, layer, :, here] = low.astype(bf16)
                both_out[k, layers + layer, :, here] = up[0, :, span]


def stack_kernel(*refs):
    for k, ref in enumerate(refs[:-1]):
        refs[-1][k] = ref[...]


def factors_kernel_part(layers, bottle, section, coefs, lefts, mates):
    K = bottle
    inner = layers - 1
    above = [section <= i for i in range(inner)]
    cross = [0.0] * inner
    drag = [0.0] * inner
    for m in range(MEMBERS):
        coef = coefs[m][...]
        grad, active = coef[:K], coef[K : 2 * K]
        others = [coef[(2 + i) * K : (3 + i) * K] for i in range(inner)]
        extras = [coef[(1 + layers + i) * K : (2 + layers + i) * K] for i in range(inner - 1)]
        at = (2 + inner + max(inner - 1, 0)) * K
        lines = coef[at:].astype(f32)
        active_f = active.astype(f32)

        def scale(i):
            row = inner + 2 * i
            return lines[row : row + 1] + lines[row + 1 : row + 2]

        def weight(n):
            total = jnp.zeros_like(lines[:1])
            for l in range(n + 1, layers):
                total = total + jnp.where(section < l, lines[l - 1 : l], 0.0)
            return total

        coarse, fine = split(grad.astype(f32) * scale(0))
        lefts[m, :K] = coarse
        lefts[m, K : 2 * K] = fine
        lefts[m, 2 * K : 3 * K] = (-weight(0) * active_f).astype(bf16)
        lefts[m, 3 * K :] = active
        for i in range(inner):
            factor = jnp.where(above[i], scale(1 + i), 1.0)
            other = (others[i].astype(f32) * factor).astype(bf16)
            mate = jnp.where(above[i], active_f, coarse.astype(f32)).astype(bf16)
            cross[i] = cross[i] + dot_nt(mate, other)
        for n in range(inner):
            held = others[n]
            if n >= 1:
                held = jnp.where(section < n, extras[n - 1].astype(f32), held.astype(f32))
            held = jnp.where(section == n, active_f, held.astype(f32)).astype(bf16)
            drag[n] = drag[n] + dot_nt((-weight(n) * active_f).astype(bf16), held)
    for i in range(inner):
        mates[2 * i] = cross[i].astype(bf16)
        mates[2 * i + 1] = drag[i].astype(bf16)


def grads_kernel(layers, bottle, width, group, chunks, turn, *refs):
    K = bottle
    inner = layers - 1
    section, _, own_slot = whereabouts(group, chunks)
    final = turn == layers - 1
    if turn == 0:
        coefs, refs = refs[:MEMBERS], refs[MEMBERS:]
        pieces, refs = refs[:MEMBERS], refs[MEMBERS:]
        gain, both, *outs, lefts, mates = refs
        factors_kernel_part(layers, bottle, section, coefs, lefts, mates)
        pieces = [ref[...] for ref in pieces]
        before = []
    else:
        lefts, mates, pieces, gain, both = refs[:5]
        before, outs = refs[5 : 5 + turn], list(refs[5 + turn :])
        pieces = [pieces[m] for m in range(MEMBERS)]
    parcel = outs.pop() if final else outs[0]
    by_hidden, by_close = 0.0, 0.0
    for m in range(MEMBERS):
        by_hidden = by_hidden + dot_nn(lefts[m, : 3 * K], pieces[m][0])
        by_close = by_close + dot_nn(lefts[m, 3 * K :], pieces[m][1])
    down = by_hidden[:K] + by_hidden[K : 2 * K]
    up = by_close + by_hidden[2 * K :]
    for i in range(inner):
        above = section <= i
        other = i + jnp.where(above, 1, 0)
        term = dot_nn(mates[2 * i], both[turn, jnp.where(above, other, layers + other)])
        up = up + jnp.where(above, term, 0.0)
        down = down + jnp.where(above, 0.0, term)
        up = up + dot_nn(mates[2 * i + 1], both[turn, layers + i])
    down = down * gain[turn]
    start = (section ^ turn) * group if final else 0
    for part in range(group):
        here = slice(part * width, (part + 1) * width)
        parcel[start + part, 0] = down[:, here]
        parcel[start + part, 1] = up[:, here]
    if not final:
        return
    for k, ref in enumerate(before):
        for part in range(group):
            parcel[(section ^ k) * group + part] = ref[part]
    if len(outs) == 1:
        outs[0][...] = parcel[...]
    else:
        for r, out in enumerate(outs):
            out[...] = parcel[own_slot ^ r].astype(out.dtype)


def per_device(inputs_down, inputs_up, cotan_down, cotan_up, norm_gains, adapt_down, adapt_up):
    sections = lax.axis_size("section")
    replicas = lax.axis_size("dp")
    section = lax.axis_index("section")
    replica = lax.axis_index("dp")
    layers = sections
    chunks = replicas // sections
    group = chunks // MEMBERS
    slots = replicas // MEMBERS
    bottle = adapt_down.shape[1]
    features = adapt_down.shape[2]
    share = features // sections
    width = features // replicas
    columns = group * width
    label, slot = label_slot(replica, group, chunks)
    micro, tokens = inputs_down.shape[0], inputs_down.shape[1]
    half = micro * tokens
    rows = 2 * half
    inner = layers - 1
    aligned = width % 128 == 0
    params = pltpu.CompilerParams(vmem_limit_bytes=VMEM_BYTES)

    acts = (inputs_down, inputs_up, cotan_down, cotan_up)
    if aligned:
        taken = (*acts, norm_gains[:, None, :], adapt_down)
        both, tall, *packed = pl.pallas_call(
            functools.partial(pack_kernel, width, group, chunks),
            out_shape=[
                pltpu.VMEM((2, rows, share), bf16),
                pltpu.VMEM((bottle + 16, features), bf16),
            ]
            + [pltpu.VMEM((2, rows, columns), bf16)] * MEMBERS,
            in_specs=[IN_HBM] * 6,
            out_specs=[IN_VMEM] * (2 + MEMBERS),
            scratch_shapes=[
                pltpu.VMEM((1, features), bf16),
                pltpu.SemaphoreType.DMA((4 * micro + 2,)),
            ],
            compiler_params=params,
            name="pack",
        )(*[pltpu.with_memory_space_constraint(v, pltpu.HBM) for v in taken])
    else:
        tall = jnp.concatenate(
            [adapt_down[0], jnp.broadcast_to(norm_gains, (16, features))], axis=0
        )
        both = jnp.concatenate([v.reshape(half, share) for v in acts], axis=0)
        both = both.reshape(2, rows, share)
        parts = both.reshape(2, rows, chunks, width)
        packed = []
        for k in range(MEMBERS):
            cuts = [
                lax.dynamic_index_in_dim(
                    parts, chunk_of(label ^ k, part, section), 2, keepdims=False
                )
                for part in range(group)
            ]
            packed.append(jnp.concatenate(cuts, axis=2))

    own = (tall, lax.optimization_barrier((adapt_up, packed[1]))[0])
    weights = [(tall, adapt_up)]
    for k in range(1, sections):
        weights.append(tuple(from_partner(w, "section", k) for w in own))
    flat = [w for ws in weights for w in ws]
    pieces = [packed[0]]
    for k in range(1, MEMBERS):
        pieces.append(from_partner(packed[k], "dp", LEADERS[k]))
    prod_rows = (3 * layers - 1) * bottle + 8
    gram_rows = max(inner, 1) * bottle
    sides = [(prod_rows, rows), (gram_rows, 2 * gram_rows)]
    if rows == 2 * gram_rows:
        sides = [(prod_rows + gram_rows, rows)]
    sums = pl.pallas_call(
        functools.partial(products_kernel, layers),
        out_shape=[jax.ShapeDtypeStruct(side, f32) for side in sides],
        in_specs=[IN_VMEM] * (1 + 2 * sections),
        out_specs=[IN_VMEM] * len(sides),
        scratch_shapes=[pltpu.VMEM((layers, bottle, share), bf16)] * 3,
        compiler_params=params,
        cost_estimate=cost(COST_PRODUCTS),
        name="products",
    )(both, *flat)
    sums = list(sums)
    for k in range(1, sections):
        sums += [from_partner(v, "section", k) for v in sums[: len(sides)]]

    tail = inner + 2 * layers
    coef_rows = (2 + inner + max(inner - 1, 0)) * bottle + -(-tail // 16) * 16
    coef = pl.pallas_call(
        functools.partial(relay_kernel, layers, bottle, features, sections),
        out_shape=jax.ShapeDtypeStruct((coef_rows, rows), bf16),
        in_specs=[IN_VMEM] * len(sums),
        out_specs=IN_VMEM,
        scratch_shapes=[pltpu.VMEM((2 * layers, bottle, rows), bf16)],
        compiler_params=params,
        cost_estimate=cost(COST_SMALL),
        name="relay",
    )(*sums)
    coefs = [coef] + [from_partner(coef, "dp", LEADERS[k]) for k in range(1, MEMBERS)]
    cut_shapes = [
        jax.ShapeDtypeStruct((layers, 1, columns), f32),
        jax.ShapeDtypeStruct((layers, 2 * layers, bottle, columns), bf16),
    ]
    if aligned:
        gain_cut, both_cut = pl.pallas_call(
            functools.partial(cut_kernel, layers, width, group, chunks),
            out_shape=cut_shapes,
            in_specs=[IN_VMEM] * len(flat),
            out_specs=[IN_VMEM] * 2,
            compiler_params=params,
            cost_estimate=cost(COST_SMALL),
            name="cut",
        )(*flat)
    else:
        gain_cut = jnp.zeros(cut_shapes[0].shape, f32)
        both_cut = jnp.zeros(cut_shapes[1].shape, bf16)
        for k in range(layers):
            for part in range(group):
                at = section ^ k
                chunk = at * chunks + chunk_of(label, part, at)
                for w, ws in enumerate(weights):
                    down, up = (
                        lax.dynamic_index_in_dim(
                            v.reshape(-1, replicas, width), chunk, 1, keepdims=False
                        )
                        for v in ws
                    )
                    down, gain = down[:bottle], down[bottle : bottle + 1]
                    low = (gain.astype(f32) * down.astype(f32)).astype(bf16)
                    layer = section ^ w
                    spot = (k, layer, 0, part * width)
                    both_cut = lax.dynamic_update_slice(both_cut, low[None, None], spot)
                    spot = (k, layers + layer, 0, part * width)
                    both_cut = lax.dynamic_update_slice(both_cut, up[None, None], spot)
                    if w == 0:
                        gain_cut = lax.dynamic_update_slice(
                            gain_cut, gain.astype(f32)[None], (k, 0, part * width)
                        )

    gated = list(lax.optimization_barrier((*pieces, coef))[:-1])
    stacked = pl.pallas_call(
        stack_kernel,
        out_shape=jax.ShapeDtypeStruct((MEMBERS, 2, rows, columns), bf16),
        in_specs=[IN_VMEM] * MEMBERS,
        out_specs=IN_VMEM,
        compiler_params=params,
        cost_estimate=cost(COST_SMALL),
        name="stack",
    )(*gated)
    handed = [None] + [from_partner(stacked, "section", k) for k in range(1, sections)]

    message = (2, bottle, width)
    left_shape = jax.ShapeDtypeStruct((MEMBERS, 4 * bottle, rows), bf16)
    mate_shape = jax.ShapeDtypeStruct((max(2 * inner, 1), bottle, bottle), bf16)
    held = jax.ShapeDtypeStruct((group,) + message, f32)
    before = []
    for k in range(sections):
        shapes, scratch = [held], []
        if k == sections - 1:
            scratch = [pltpu.VMEM((slots,) + message, f32)]
            shapes = [jax.ShapeDtypeStruct((slots,) + message, f32)]
            if aligned:
                shapes = [jax.ShapeDtypeStruct(message, f32)]
                shapes += [jax.ShapeDtypeStruct(message, bf16)] * (slots - 1)
        if k == 0:
            shapes += [left_shape, mate_shape]
            operands = (*coefs, *pieces, gain_cut, both_cut)
        else:
            operands = (lefts, mates, handed[k], gain_cut, both_cut, *before)
        parcels = pl.pallas_call(
            functools.partial(grads_kernel, layers, bottle, width, group, chunks, k),
            out_shape=shapes,
            in_specs=[IN_VMEM] * len(operands),
            out_specs=[IN_VMEM] * len(shapes),
            scratch_shapes=scratch,
            compiler_params=params,
            cost_estimate=cost(COST_GRADS),
            name="grads",
        )(*operands)
        if k == 0:
            *parcels, lefts, mates = parcels
        if k < sections - 1:
            before += parcels
    if not aligned:
        parcels = [
            lax.dynamic_index_in_dim(parcels[0], slot ^ r, 0, keepdims=False)
            for r in range(slots)
        ]
        parcels[1:] = [v.astype(bf16) for v in parcels[1:]]

    total = parcels[0]
    for r in (*range(slots // 2, slots), *range(1, slots // 2)):
        received = from_partner(parcels[r], "dp", mask(r, group, chunks))
        total = total + received.astype(f32)
    return (total[0][None], total[1][None])


def solution(mesh):
    placed = (
        P(None, "dp", "section"),
        P(None, "dp", "section"),
        P(None, "dp", "section"),
        P(None, "dp", "section"),
        P("section", None),
        P("section", None, None),
        P("section", None, None),
    )
    return jax.shard_map(
        per_device,
        mesh=mesh,
        in_specs=placed,
        out_specs=(P("section", None, "dp"), P("section", None, "dp")),
        check_vma=False,
    )
```

```python
import functools

import jax
import jax.numpy as jnp
from jax import lax
from jax.experimental import pallas as pl
from jax.experimental.pallas import tpu as pltpu
from jax.sharding import PartitionSpec as P

epsilon = 1e-05
VMEM_BYTES = 32 * 1024 * 1024
MEMBERS = 4
STAR = True
TWIST = 0
COST_PRODUCTS = 12
COST_SMALL = 0.1
COST_GRADS = 10
f32 = jnp.float32
bf16 = jnp.bfloat16
IN_VMEM = pl.BlockSpec(memory_space=pltpu.VMEM)
IN_HBM = pl.BlockSpec(memory_space=pltpu.HBM)


def cost(micros):
    return pl.CostEstimate(flops=int(micros * 1.1e9), bytes_accessed=0, transcendentals=0)


def from_partner(value, axis, flip):
    return lax.ppermute(value, axis, [(i, i ^ flip) for i in range(lax.axis_size(axis))])


def dot_nn(left, right):
    return lax.dot_general(left, right, (((1,), (0,)), ((), ())), preferred_element_type=f32)


def dot_nt(left, right):
    return lax.dot_general(left, right, (((1,), (1,)), ((), ())), preferred_element_type=f32)


def split(value):
    high = value.astype(bf16)
    return high, (value - high.astype(f32)).astype(bf16)


def dot_tn(left, right):
    return lax.dot_general(left, right, (((0,), (0,)), ((), ())), preferred_element_type=f32)


def dot_split(left, right, dot=dot_nn):
    high, low = split(left)
    return dot(high, right) + dot(low, right)


LEADERS = (0, 1, 2, 4) if STAR else (0, 1, 2, 3)


def leader(label):
    return label + (label == 3) if STAR else label


def mask(slot, group, chunks):
    section, part = divmod(slot, group)
    low = (part & 1) * 7 + (part >> 1) * 8 if STAR else part * 4
    return section * chunks ^ (section & 1) * TWIST ^ low


def label_slot(replica, group, chunks):
    section = replica // chunks
    local = replica % chunks ^ (section & 1) * TWIST
    if not STAR:
        return local % 4, section * group + local // 4
    low = local & 7
    label = (low & 3) ^ (low >> 2) * 3
    odd = (low != 0) & (low != 1) & (low != 2) & (low != 4)
    return label, section * group + (local >> 3) * 2 + odd.astype(jnp.int32)


def whereabouts(group, chunks):
    section = lax.axis_index("section")
    label, slot = label_slot(lax.axis_index("dp"), group, chunks)
    return section, label, slot


def chunk_of(label, part, section):
    low = (part & 1) * 7 + (part >> 1) * 8 if STAR else part * 4
    return leader(label) ^ low ^ (section & 1) * TWIST


def pack_kernel(width, group, chunks, *refs):
    acts, gain, down = refs[:4], refs[4], refs[5]
    both, tall = refs[6:8]
    outs = refs[8:-2]
    line, sems = refs[-2:]
    micro, tokens = acts[0].shape[0], acts[0].shape[1]
    bottle = down.shape[1]
    section, label, _ = whereabouts(group, chunks)
    copies = []
    for a, act in enumerate(acts):
        for m in range(micro):
            start = ((a % 2) * micro + m) * tokens
            copies.append(
                pltpu.make_async_copy(
                    act.at[m], both.at[a // 2, pl.ds(start, tokens)], sems.at[len(copies)]
                )
            )
    count = len(copies)
    copies.append(pltpu.make_async_copy(gain.at[0], line, sems.at[count]))
    copies.append(
        pltpu.make_async_copy(down.at[0], tall.at[pl.ds(0, bottle)], sems.at[count + 1])
    )
    for copy in copies:
        copy.start()
    for n in range(count):
        copies[n].wait()
        a, m = divmod(n, micro)
        start = ((a % 2) * micro + m) * tokens
        for k, out in enumerate(outs):
            for part in range(group):
                chunk = chunk_of(label ^ k, part, section)
                span = pl.ds(pl.multiple_of(chunk * width, width), width)
                out[a // 2, start : start + tokens, part * width : (part + 1) * width] = both[
                    a // 2, start : start + tokens, span
                ]
    copies[count].wait()
    tall[bottle:] = jnp.broadcast_to(line[...], (tall.shape[0] - bottle, tall.shape[1]))
    copies[count + 1].wait()


def two_parts(refs):
    if len(refs) == 2:
        return refs
    height, side = refs[0].shape
    return refs[0].at[: height - side // 2], refs[0].at[height - side // 2 :]


def products_kernel(layers, *refs):
    acts = refs[0]
    weights = [refs[1 + 2 * k : 3 + 2 * k] for k in range(layers)]
    outs = refs[1 + 2 * layers : -3]
    prod_out, gram_out = two_parts(outs)
    low_scr, fine_scr, high_scr = refs[-3:]
    bottle = weights[0][1].shape[1]
    gain_row = slice(bottle, bottle + 1)
    features = acts.shape[2]
    section = lax.axis_index("section")
    mine = pl.ds(pl.multiple_of(section * features, features), features)
    for k in range(layers):
        tall, up = weights[k]
        layer = section ^ k
        exact = tall[gain_row, mine].astype(f32) * tall[:bottle, mine].astype(f32)
        low, fine = split(exact)
        low_scr[layer] = low
        fine_scr[layer] = fine
        high_scr[layer] = up[0, :, mine]
    hidden = acts[0]
    low_all = low_scr[...].reshape(layers * bottle, features)
    fine_all = fine_scr[...].reshape(layers * bottle, features)
    high_all = high_scr[...].reshape(layers * bottle, features)
    size = (layers - 1) * bottle
    at = layers * bottle
    prod_out[:at] = dot_nt(low_all, hidden) + dot_nt(fine_all, hidden)
    if layers > 1:
        prod_out[at : at + size] = dot_nt(high_all[:size], hidden)
    at += size
    prod_out[at : at + layers * bottle] = dot_nt(high_all, acts[1])
    at += layers * bottle
    square = dot_nt(hidden, hidden)
    eye = lax.broadcasted_iota(jnp.int32, square.shape, 0) == lax.broadcasted_iota(
        jnp.int32, square.shape, 1
    )
    norms = jnp.sum(jnp.where(eye, square, 0.0), axis=0, keepdims=True)
    prod_out[at : at + 8] = jnp.broadcast_to(norms, (8, norms.shape[1]))
    if layers > 1:
        high_part = high_all[:size]
        low_part = low_all[bottle:]
        fine_part = fine_all[bottle:]
        gram_out[:, :size] = dot_nt(high_part, low_part) + dot_nt(high_part, fine_part)
        gram_out[:, size:] = dot_nt(high_part, high_part)
    else:
        gram_out[...] = jnp.zeros_like(gram_out)


def relay_kernel(layers, bottle, features, sections, *refs):
    coef_out, hold = refs[-2:]
    each = (len(refs) - 2) // sections
    prods, grams = zip(
        *(two_parts(refs[each * k : each * (k + 1)]) for k in range(sections)), strict=True
    )
    section = lax.axis_index("section")
    prod = sum((ref[...] for ref in prods[1:]), prods[0][...])
    gram = sum((ref[...] for ref in grams[1:]), grams[0][...])
    K = bottle
    inner = layers - 1
    h_low = [prod[l * K : (l + 1) * K] for l in range(layers)]
    at = layers * K
    h_high = [prod[at + l * K : at + (l + 1) * K] for l in range(inner)]
    at += inner * K
    u_high = [prod[at + l * K : at + (l + 1) * K] for l in range(layers)]
    at += layers * K
    norm = prod[at : at + 1]

    def high_low(m, l):
        return gram[m * K : (m + 1) * K, (l - 1) * K : l * K]

    def high_high(m, n):
        return gram[m * K : (m + 1) * K, (inner + n) * K : (inner + n + 1) * K]

    inverses, bottles, hidden_high = [], [], []
    for l in range(layers):
        inverse = lax.rsqrt(jnp.maximum(norm, 0.0) * (1.0 / features) + epsilon)
        value = h_low[l] * inverse
        active = (value * jax.nn.sigmoid(value)).astype(bf16)
        inverses.append(inverse)
        bottles.append(value)
        hold[l] = active
        hidden_high.append(list(h_high))
        if l < inner:
            before = h_high[l]
            h_high = [h_high[n] + dot_split(high_high(n, l), active) for n in range(inner)]
            for n in range(l + 1, layers):
                h_low[n] = h_low[n] + dot_split(high_low(l, n), active, dot_tn)
            norm = norm + jnp.sum(
                active.astype(f32) * (before + h_high[l]), axis=0, keepdims=True
            )
    pulls = [None] * layers
    for l in range(layers - 1, -1, -1):
        sigma = jax.nn.sigmoid(bottles[l])
        coarse = (u_high[l] * sigma * (1.0 + bottles[l] * (1.0 - sigma))).astype(bf16)
        hold[layers + l] = coarse
        if l == 0:
            break
        grad = coarse.astype(f32)
        scaled, fine = split(grad * inverses[l])
        pull = (
            inverses[l]
            * inverses[l]
            * jnp.sum(grad * bottles[l], axis=0, keepdims=True)
            * (1.0 / features)
        )
        pulls[l] = pull
        for n in range(l):
            u_high[n] = (
                u_high[n]
                + dot_split(high_low(n, l), scaled)
                + dot_nn(high_low(n, l).astype(bf16), fine)
                - pull * hidden_high[l][n]
            )
    blocks = [hold[layers + section], hold[section]]
    for i in range(inner):
        other = i + jnp.where(section <= i, 1, 0)
        blocks.append(hold[jnp.where(section <= i, layers + other, other)])
    blocks += [hold[n] for n in range(1, inner)]
    for n, block in enumerate(blocks):
        coef_out[n * K : (n + 1) * K] = block

    def inverse_at(layer):
        value = inverses[0]
        for l in range(1, layers):
            value = jnp.where(layer == l, inverses[l], value)
        return value

    lines = [line.astype(bf16).astype(f32) for line in pulls[1:]]
    scales = [inverse_at(section)]
    scales += [inverse_at(i + jnp.where(section <= i, 1, 0)) for i in range(inner)]
    for scale in scales:
        lines.extend(part.astype(f32) for part in split(scale))
    tail = coef_out.shape[0] - len(blocks) * K
    lines += [jnp.zeros_like(norm)] * (tail - len(lines))
    coef_out[len(blocks) * K :] = jnp.concatenate(lines, axis=0).astype(bf16)


def cut_kernel(layers, width, group, chunks, *refs):
    weights = [refs[2 * k : 2 * k + 2] for k in range(layers)]
    gain_out, both_out = refs[2 * layers :]
    bottle = weights[0][1].shape[1]
    gain_row = slice(bottle, bottle + 1)
    here_section, label, _ = whereabouts(group, chunks)
    for k in range(layers):
        section = here_section ^ k
        for part in range(group):
            chunk = section * chunks + chunk_of(label, part, section)
            span = pl.ds(pl.multiple_of(chunk * width, width), width)
            here = slice(part * width, (part + 1) * width)
            gain_out[k, :, here] = weights[0][0][gain_row, span].astype(f32)
            for w in range(layers):
                tall, up = weights[w]
                layer = here_section ^ w
                low = tall[gain_row, span].astype(f32) * tall[:bottle, span].astype(f32)
                both_out[k, layer, :, here] = low.astype(bf16)
                both_out[k, layers + layer, :, here] = up[0, :, span]


def stack_kernel(*refs):
    for k, ref in enumerate(refs[:-1]):
        refs[-1][k] = ref[...]


def factors_kernel_part(layers, bottle, section, coefs, lefts, mates):
    K = bottle
    inner = layers - 1
    above = [section <= i for i in range(inner)]
    cross = [0.0] * inner
    drag = [0.0] * inner
    for m in range(MEMBERS):
        coef = coefs[m][...]
        grad, active = coef[:K], coef[K : 2 * K]
        others = [coef[(2 + i) * K : (3 + i) * K] for i in range(inner)]
        extras = [coef[(1 + layers + i) * K : (2 + layers + i) * K] for i in range(inner - 1)]
        at = (2 + inner + max(inner - 1, 0)) * K
        lines = coef[at:].astype(f32)
        active_f = active.astype(f32)

        def scale(i):
            row = inner + 2 * i
            return lines[row : row + 1] + lines[row + 1 : row + 2]

        def weight(n):
            total = jnp.zeros_like(lines[:1])
            for l in range(n + 1, layers):
                total = total + jnp.where(section < l, lines[l - 1 : l], 0.0)
            return total

        coarse, fine = split(grad.astype(f32) * scale(0))
        lefts[m, :K] = coarse
        lefts[m, K : 2 * K] = fine
        lefts[m, 2 * K : 3 * K] = (-weight(0) * active_f).astype(bf16)
        lefts[m, 3 * K :] = active
        for i in range(inner):
            factor = jnp.where(above[i], scale(1 + i), 1.0)
            other = (others[i].astype(f32) * factor).astype(bf16)
            mate = jnp.where(above[i], active_f, coarse.astype(f32)).astype(bf16)
            cross[i] = cross[i] + dot_nt(mate, other)
        for n in range(inner):
            held = others[n]
            if n >= 1:
                held = jnp.where(section < n, extras[n - 1].astype(f32), held.astype(f32))
            held = jnp.where(section == n, active_f, held.astype(f32)).astype(bf16)
            drag[n] = drag[n] + dot_nt((-weight(n) * active_f).astype(bf16), held)
    for i in range(inner):
        mates[2 * i] = cross[i].astype(bf16)
        mates[2 * i + 1] = drag[i].astype(bf16)


def grads_kernel(layers, bottle, width, group, chunks, turn, *refs):
    K = bottle
    inner = layers - 1
    section, _, own_slot = whereabouts(group, chunks)
    final = turn == layers - 1
    if turn == 0:
        coefs, refs = refs[:MEMBERS], refs[MEMBERS:]
        pieces, refs = refs[:MEMBERS], refs[MEMBERS:]
        gain, both, *outs, lefts, mates = refs
        factors_kernel_part(layers, bottle, section, coefs, lefts, mates)
        pieces = [ref[...] for ref in pieces]
        before = []
    else:
        lefts, mates, pieces, gain, both = refs[:5]
        before, outs = refs[5 : 5 + turn], list(refs[5 + turn :])
        pieces = [pieces[m] for m in range(MEMBERS)]
    parcel = outs.pop() if final else outs[0]
    by_hidden, by_close = 0.0, 0.0
    for m in range(MEMBERS):
        by_hidden = by_hidden + dot_nn(lefts[m, : 3 * K], pieces[m][0])
        by_close = by_close + dot_nn(lefts[m, 3 * K :], pieces[m][1])
    down = by_hidden[:K] + by_hidden[K : 2 * K]
    up = by_close + by_hidden[2 * K :]
    for i in range(inner):
        above = section <= i
        other = i + jnp.where(above, 1, 0)
        term = dot_nn(mates[2 * i], both[turn, jnp.where(above, other, layers + other)])
        up = up + jnp.where(above, term, 0.0)
        down = down + jnp.where(above, 0.0, term)
        up = up + dot_nn(mates[2 * i + 1], both[turn, layers + i])
    down = down * gain[turn]
    start = (section ^ turn) * group if final else 0
    for part in range(group):
        here = slice(part * width, (part + 1) * width)
        parcel[start + part, 0] = down[:, here]
        parcel[start + part, 1] = up[:, here]
    if not final:
        return
    for k, ref in enumerate(before):
        for part in range(group):
            parcel[(section ^ k) * group + part] = ref[part]
    if len(outs) == 1:
        outs[0][...] = parcel[...]
    else:
        for r, out in enumerate(outs):
            out[...] = parcel[own_slot ^ r].astype(out.dtype)


def per_device(inputs_down, inputs_up, cotan_down, cotan_up, norm_gains, adapt_down, adapt_up):
    sections = lax.axis_size("section")
    replicas = lax.axis_size("dp")
    section = lax.axis_index("section")
    replica = lax.axis_index("dp")
    layers = sections
    chunks = replicas // sections
    group = chunks // MEMBERS
    slots = replicas // MEMBERS
    bottle = adapt_down.shape[1]
    features = adapt_down.shape[2]
    share = features // sections
    width = features // replicas
    columns = group * width
    label, slot = label_slot(replica, group, chunks)
    micro, tokens = inputs_down.shape[0], inputs_down.shape[1]
    half = micro * tokens
    rows = 2 * half
    inner = layers - 1
    aligned = width % 128 == 0
    params = pltpu.CompilerParams(vmem_limit_bytes=VMEM_BYTES)

    acts = (inputs_down, inputs_up, cotan_down, cotan_up)
    if aligned:
        taken = (*acts, norm_gains[:, None, :], adapt_down)
        both, tall, *packed = pl.pallas_call(
            functools.partial(pack_kernel, width, group, chunks),
            out_shape=[
                pltpu.VMEM((2, rows, share), bf16),
                pltpu.VMEM((bottle + 16, features), bf16),
            ]
            + [pltpu.VMEM((2, rows, columns), bf16)] * MEMBERS,
            in_specs=[IN_HBM] * 6,
            out_specs=[IN_VMEM] * (2 + MEMBERS),
            scratch_shapes=[
                pltpu.VMEM((1, features), bf16),
                pltpu.SemaphoreType.DMA((4 * micro + 2,)),
            ],
            compiler_params=params,
            name="pack",
        )(*[pltpu.with_memory_space_constraint(v, pltpu.HBM) for v in taken])
    else:
        tall = jnp.concatenate(
            [adapt_down[0], jnp.broadcast_to(norm_gains, (16, features))], axis=0
        )
        both = jnp.concatenate([v.reshape(half, share) for v in acts], axis=0)
        both = both.reshape(2, rows, share)
        parts = both.reshape(2, rows, chunks, width)
        packed = []
        for k in range(MEMBERS):
            cuts = [
                lax.dynamic_index_in_dim(
                    parts, chunk_of(label ^ k, part, section), 2, keepdims=False
                )
                for part in range(group)
            ]
            packed.append(jnp.concatenate(cuts, axis=2))

    own = (tall, lax.optimization_barrier((adapt_up, *packed))[0])
    weights = [own]
    for k in range(1, sections):
        weights.append(tuple(from_partner(w, "section", k) for w in own))
    flat = [w for ws in weights for w in ws]
    pieces = [packed[0]]
    for k in range(1, MEMBERS):
        pieces.append(from_partner(packed[k], "dp", LEADERS[k]))
    prod_rows = (3 * layers - 1) * bottle + 8
    gram_rows = max(inner, 1) * bottle
    sides = [(prod_rows, rows), (gram_rows, 2 * gram_rows)]
    if rows == 2 * gram_rows:
        sides = [(prod_rows + gram_rows, rows)]
    sums = pl.pallas_call(
        functools.partial(products_kernel, layers),
        out_shape=[jax.ShapeDtypeStruct(side, f32) for side in sides],
        in_specs=[IN_VMEM] * (1 + 2 * sections),
        out_specs=[IN_VMEM] * len(sides),
        scratch_shapes=[pltpu.VMEM((layers, bottle, share), bf16)] * 3,
        compiler_params=params,
        cost_estimate=cost(COST_PRODUCTS),
        name="products",
    )(both, *flat)
    sums = list(sums)
    for k in range(1, sections):
        sums += [from_partner(v, "section", k) for v in sums[: len(sides)]]

    tail = inner + 2 * layers
    coef_rows = (2 + inner + max(inner - 1, 0)) * bottle + -(-tail // 16) * 16
    coef = pl.pallas_call(
        functools.partial(relay_kernel, layers, bottle, features, sections),
        out_shape=jax.ShapeDtypeStruct((coef_rows, rows), bf16),
        in_specs=[IN_VMEM] * len(sums),
        out_specs=IN_VMEM,
        scratch_shapes=[pltpu.VMEM((2 * layers, bottle, rows), bf16)],
        compiler_params=params,
        cost_estimate=cost(COST_SMALL),
        name="relay",
    )(*sums)
    coefs = [coef] + [from_partner(coef, "dp", LEADERS[k]) for k in range(1, MEMBERS)]
    cut_shapes = [
        jax.ShapeDtypeStruct((layers, 1, columns), f32),
        jax.ShapeDtypeStruct((layers, 2 * layers, bottle, columns), bf16),
    ]
    if aligned:
        gain_cut, both_cut = pl.pallas_call(
            functools.partial(cut_kernel, layers, width, group, chunks),
            out_shape=cut_shapes,
            in_specs=[IN_VMEM] * len(flat),
            out_specs=[IN_VMEM] * 2,
            compiler_params=params,
            cost_estimate=cost(COST_SMALL),
            name="cut",
        )(*flat)
    else:
        gain_cut = jnp.zeros(cut_shapes[0].shape, f32)
        both_cut = jnp.zeros(cut_shapes[1].shape, bf16)
        for k in range(layers):
            for part in range(group):
                at = section ^ k
                chunk = at * chunks + chunk_of(label, part, at)
                for w, ws in enumerate(weights):
                    down, up = (
                        lax.dynamic_index_in_dim(
                            v.reshape(-1, replicas, width), chunk, 1, keepdims=False
                        )
                        for v in ws
                    )
                    down, gain = down[:bottle], down[bottle : bottle + 1]
                    low = (gain.astype(f32) * down.astype(f32)).astype(bf16)
                    layer = section ^ w
                    spot = (k, layer, 0, part * width)
                    both_cut = lax.dynamic_update_slice(both_cut, low[None, None], spot)
                    spot = (k, layers + layer, 0, part * width)
                    both_cut = lax.dynamic_update_slice(both_cut, up[None, None], spot)
                    if w == 0:
                        gain_cut = lax.dynamic_update_slice(
                            gain_cut, gain.astype(f32)[None], (k, 0, part * width)
                        )

    gated = list(lax.optimization_barrier((*pieces, coef))[:-1])
    stacked = pl.pallas_call(
        stack_kernel,
        out_shape=jax.ShapeDtypeStruct((MEMBERS, 2, rows, columns), bf16),
        in_specs=[IN_VMEM] * MEMBERS,
        out_specs=IN_VMEM,
        compiler_params=params,
        cost_estimate=cost(COST_SMALL),
        name="stack",
    )(*gated)
    handed = [None] + [from_partner(stacked, "section", k) for k in range(1, sections)]

    message = (2, bottle, width)
    left_shape = jax.ShapeDtypeStruct((MEMBERS, 4 * bottle, rows), bf16)
    mate_shape = jax.ShapeDtypeStruct((max(2 * inner, 1), bottle, bottle), bf16)
    held = jax.ShapeDtypeStruct((group,) + message, f32)
    before = []
    for k in range(sections):
        shapes, scratch = [held], []
        if k == sections - 1:
            scratch = [pltpu.VMEM((slots,) + message, f32)]
            shapes = [jax.ShapeDtypeStruct((slots,) + message, f32)]
            if aligned:
                shapes = [jax.ShapeDtypeStruct(message, f32)]
                shapes += [jax.ShapeDtypeStruct(message, bf16)] * (slots - 1)
        if k == 0:
            shapes += [left_shape, mate_shape]
            operands = (*coefs, *pieces, gain_cut, both_cut)
        else:
            operands = (lefts, mates, handed[k], gain_cut, both_cut, *before)
        parcels = pl.pallas_call(
            functools.partial(grads_kernel, layers, bottle, width, group, chunks, k),
            out_shape=shapes,
            in_specs=[IN_VMEM] * len(operands),
            out_specs=[IN_VMEM] * len(shapes),
            scratch_shapes=scratch,
            compiler_params=params,
            cost_estimate=cost(COST_GRADS),
            name="grads",
        )(*operands)
        if k == 0:
            *parcels, lefts, mates = parcels
        if k < sections - 1:
            before += parcels
    if not aligned:
        parcels = [
            lax.dynamic_index_in_dim(parcels[0], slot ^ r, 0, keepdims=False)
            for r in range(slots)
        ]
        parcels[1:] = [v.astype(bf16) for v in parcels[1:]]

    total = parcels[0]
    for r in (*range(slots // 2, slots), *range(1, slots // 2)):
        received = from_partner(parcels[r], "dp", mask(r, group, chunks))
        total = total + received.astype(f32)
    return (total[0][None], total[1][None])


def solution(mesh):
    placed = (
        P(None, "dp", "section"),
        P(None, "dp", "section"),
        P(None, "dp", "section"),
        P(None, "dp", "section"),
        P("section", None),
        P("section", None, None),
        P("section", None, None),
    )
    return jax.shard_map(
        per_device,
        mesh=mesh,
        in_specs=placed,
        out_specs=(P("section", None, "dp"), P("section", None, "dp")),
        check_vma=False,
    )
```

```python
import functools

import jax
import jax.numpy as jnp
from jax import lax
from jax.experimental import pallas as pl
from jax.experimental.pallas import tpu as pltpu
from jax.sharding import PartitionSpec as P

epsilon = 1e-05
VMEM_BYTES = 32 * 1024 * 1024
MEMBERS = 4
STAR = True
TWIST = 0
COST_PRODUCTS = 12
COST_SMALL = 0.1
COST_GRADS = 10
f32 = jnp.float32
bf16 = jnp.bfloat16
IN_VMEM = pl.BlockSpec(memory_space=pltpu.VMEM)
IN_HBM = pl.BlockSpec(memory_space=pltpu.HBM)


def cost(micros):
    return pl.CostEstimate(flops=int(micros * 1.1e9), bytes_accessed=0, transcendentals=0)


def from_partner(value, axis, flip):
    return lax.ppermute(value, axis, [(i, i ^ flip) for i in range(lax.axis_size(axis))])


def dot_nn(left, right):
    return lax.dot_general(left, right, (((1,), (0,)), ((), ())), preferred_element_type=f32)


def dot_nt(left, right):
    return lax.dot_general(left, right, (((1,), (1,)), ((), ())), preferred_element_type=f32)


def split(value):
    high = value.astype(bf16)
    return high, (value - high.astype(f32)).astype(bf16)


def dot_tn(left, right):
    return lax.dot_general(left, right, (((0,), (0,)), ((), ())), preferred_element_type=f32)


def dot_split(left, right, dot=dot_nn):
    high, low = split(left)
    return dot(high, right) + dot(low, right)


LEADERS = (0, 1, 2, 4) if STAR else (0, 1, 2, 3)


def leader(label):
    return label + (label == 3) if STAR else label


def mask(slot, group, chunks):
    section, part = divmod(slot, group)
    low = (part & 1) * 7 + (part >> 1) * 8 if STAR else part * 4
    return section * chunks ^ (section & 1) * TWIST ^ low


def label_slot(replica, group, chunks):
    section = replica // chunks
    local = replica % chunks ^ (section & 1) * TWIST
    if not STAR:
        return local % 4, section * group + local // 4
    low = local & 7
    label = (low & 3) ^ (low >> 2) * 3
    odd = (low != 0) & (low != 1) & (low != 2) & (low != 4)
    return label, section * group + (local >> 3) * 2 + odd.astype(jnp.int32)


def whereabouts(group, chunks):
    section = lax.axis_index("section")
    label, slot = label_slot(lax.axis_index("dp"), group, chunks)
    return section, label, slot


def chunk_of(label, part, section):
    low = (part & 1) * 7 + (part >> 1) * 8 if STAR else part * 4
    return leader(label) ^ low ^ (section & 1) * TWIST


def pack_kernel(width, group, chunks, *refs):
    acts, gain, down = refs[:4], refs[4], refs[5]
    both, tall = refs[6:8]
    outs = refs[8:-2]
    line, sems = refs[-2:]
    micro, tokens = acts[0].shape[0], acts[0].shape[1]
    bottle = down.shape[1]
    section, label, _ = whereabouts(group, chunks)
    copies = []
    for a, act in enumerate(acts):
        for m in range(micro):
            start = ((a % 2) * micro + m) * tokens
            copies.append(
                pltpu.make_async_copy(
                    act.at[m], both.at[a // 2, pl.ds(start, tokens)], sems.at[len(copies)]
                )
            )
    count = len(copies)
    copies.append(pltpu.make_async_copy(gain.at[0], line, sems.at[count]))
    copies.append(
        pltpu.make_async_copy(down.at[0], tall.at[pl.ds(0, bottle)], sems.at[count + 1])
    )
    for copy in copies:
        copy.start()
    for n in range(count):
        copies[n].wait()
        a, m = divmod(n, micro)
        start = ((a % 2) * micro + m) * tokens
        for k, out in enumerate(outs):
            for part in range(group):
                chunk = chunk_of(label ^ k, part, section)
                span = pl.ds(pl.multiple_of(chunk * width, width), width)
                out[a // 2, start : start + tokens, part * width : (part + 1) * width] = both[
                    a // 2, start : start + tokens, span
                ]
    copies[count].wait()
    tall[bottle:] = jnp.broadcast_to(line[...], (tall.shape[0] - bottle, tall.shape[1]))
    copies[count + 1].wait()


def two_parts(refs):
    if len(refs) == 2:
        return refs
    height, side = refs[0].shape
    return refs[0].at[: height - side // 2], refs[0].at[height - side // 2 :]


def products_kernel(layers, *refs):
    acts = refs[0]
    weights = [refs[1 + 2 * k : 3 + 2 * k] for k in range(layers)]
    outs = refs[1 + 2 * layers : -3]
    prod_out, gram_out = two_parts(outs)
    low_scr, fine_scr, high_scr = refs[-3:]
    bottle = weights[0][1].shape[1]
    gain_row = slice(bottle, bottle + 1)
    features = acts.shape[2]
    section = lax.axis_index("section")
    mine = pl.ds(pl.multiple_of(section * features, features), features)
    for k in range(layers):
        tall, up = weights[k]
        layer = section ^ k
        exact = tall[gain_row, mine].astype(f32) * tall[:bottle, mine].astype(f32)
        low, fine = split(exact)
        low_scr[layer] = low
        fine_scr[layer] = fine
        high_scr[layer] = up[0, :, mine]
    hidden = acts[0]
    low_all = low_scr[...].reshape(layers * bottle, features)
    fine_all = fine_scr[...].reshape(layers * bottle, features)
    high_all = high_scr[...].reshape(layers * bottle, features)
    size = (layers - 1) * bottle
    at = layers * bottle
    prod_out[:at] = dot_nt(low_all, hidden) + dot_nt(fine_all, hidden)
    if layers > 1:
        prod_out[at : at + size] = dot_nt(high_all[:size], hidden)
    at += size
    prod_out[at : at + layers * bottle] = dot_nt(high_all, acts[1])
    at += layers * bottle
    square = dot_nt(hidden, hidden)
    eye = lax.broadcasted_iota(jnp.int32, square.shape, 0) == lax.broadcasted_iota(
        jnp.int32, square.shape, 1
    )
    norms = jnp.sum(jnp.where(eye, square, 0.0), axis=0, keepdims=True)
    prod_out[at : at + 8] = jnp.broadcast_to(norms, (8, norms.shape[1]))
    if layers > 1:
        high_part = high_all[:size]
        low_part = low_all[bottle:]
        fine_part = fine_all[bottle:]
        gram_out[:, :size] = dot_nt(high_part, low_part) + dot_nt(high_part, fine_part)
        gram_out[:, size:] = dot_nt(high_part, high_part)
    else:
        gram_out[...] = jnp.zeros_like(gram_out)


def relay_kernel(layers, bottle, features, sections, *refs):
    coef_out, hold = refs[-2:]
    each = (len(refs) - 2) // sections
    prods, grams = zip(
        *(two_parts(refs[each * k : each * (k + 1)]) for k in range(sections)), strict=True
    )
    section = lax.axis_index("section")
    prod = sum((ref[...] for ref in prods[1:]), prods[0][...])
    gram = sum((ref[...] for ref in grams[1:]), grams[0][...])
    K = bottle
    inner = layers - 1
    h_low = [prod[l * K : (l + 1) * K] for l in range(layers)]
    at = layers * K
    h_high = [prod[at + l * K : at + (l + 1) * K] for l in range(inner)]
    at += inner * K
    u_high = [prod[at + l * K : at + (l + 1) * K] for l in range(layers)]
    at += layers * K
    norm = prod[at : at + 1]

    def high_low(m, l):
        return gram[m * K : (m + 1) * K, (l - 1) * K : l * K]

    def high_high(m, n):
        return gram[m * K : (m + 1) * K, (inner + n) * K : (inner + n + 1) * K]

    inverses, bottles, hidden_high = [], [], []
    for l in range(layers):
        inverse = lax.rsqrt(jnp.maximum(norm, 0.0) * (1.0 / features) + epsilon)
        value = h_low[l] * inverse
        active = (value * jax.nn.sigmoid(value)).astype(bf16)
        inverses.append(inverse)
        bottles.append(value)
        hold[l] = active
        hidden_high.append(list(h_high))
        if l < inner:
            before = h_high[l]
            h_high = [h_high[n] + dot_split(high_high(n, l), active) for n in range(inner)]
            for n in range(l + 1, layers):
                h_low[n] = h_low[n] + dot_split(high_low(l, n), active, dot_tn)
            norm = norm + jnp.sum(
                active.astype(f32) * (before + h_high[l]), axis=0, keepdims=True
            )
    pulls = [None] * layers
    for l in range(layers - 1, -1, -1):
        sigma = jax.nn.sigmoid(bottles[l])
        coarse = (u_high[l] * sigma * (1.0 + bottles[l] * (1.0 - sigma))).astype(bf16)
        hold[layers + l] = coarse
        if l == 0:
            break
        grad = coarse.astype(f32)
        scaled, fine = split(grad * inverses[l])
        pull = (
            inverses[l]
            * inverses[l]
            * jnp.sum(grad * bottles[l], axis=0, keepdims=True)
            * (1.0 / features)
        )
        pulls[l] = pull
        for n in range(l):
            u_high[n] = (
                u_high[n]
                + dot_split(high_low(n, l), scaled)
                + dot_nn(high_low(n, l).astype(bf16), fine)
                - pull * hidden_high[l][n]
            )
    blocks = [hold[layers + section], hold[section]]
    for i in range(inner):
        other = i + jnp.where(section <= i, 1, 0)
        blocks.append(hold[jnp.where(section <= i, layers + other, other)])
    blocks += [hold[n] for n in range(1, inner)]
    for n, block in enumerate(blocks):
        coef_out[n * K : (n + 1) * K] = block

    def inverse_at(layer):
        value = inverses[0]
        for l in range(1, layers):
            value = jnp.where(layer == l, inverses[l], value)
        return value

    lines = [line.astype(bf16).astype(f32) for line in pulls[1:]]
    scales = [inverse_at(section)]
    scales += [inverse_at(i + jnp.where(section <= i, 1, 0)) for i in range(inner)]
    for scale in scales:
        lines.extend(part.astype(f32) for part in split(scale))
    tail = coef_out.shape[0] - len(blocks) * K
    lines += [jnp.zeros_like(norm)] * (tail - len(lines))
    coef_out[len(blocks) * K :] = jnp.concatenate(lines, axis=0).astype(bf16)


def cut_kernel(layers, width, group, chunks, *refs):
    weights = [refs[2 * k : 2 * k + 2] for k in range(layers)]
    gain_out, both_out = refs[2 * layers :]
    bottle = weights[0][1].shape[1]
    gain_row = slice(bottle, bottle + 1)
    here_section, label, _ = whereabouts(group, chunks)
    for k in range(layers):
        section = here_section ^ k
        for part in range(group):
            chunk = section * chunks + chunk_of(label, part, section)
            span = pl.ds(pl.multiple_of(chunk * width, width), width)
            here = slice(part * width, (part + 1) * width)
            gain_out[k, :, here] = weights[0][0][gain_row, span].astype(f32)
            for w in range(layers):
                tall, up = weights[w]
                layer = here_section ^ w
                low = tall[gain_row, span].astype(f32) * tall[:bottle, span].astype(f32)
                both_out[k, layer, :, here] = low.astype(bf16)
                both_out[k, layers + layer, :, here] = up[0, :, span]


def stack_kernel(*refs):
    rows = refs[0].shape[1]
    for k, ref in enumerate(refs[:-1]):
        refs[-1][:, k * rows : (k + 1) * rows] = ref[...]


def factors_kernel_part(layers, bottle, section, coefs, lefts, mates):
    K = bottle
    inner = layers - 1
    above = [section <= i for i in range(inner)]
    mates_of = [([], [], [], []) for _ in range(inner)]
    for m in range(MEMBERS):
        coef = coefs[m][...]
        grad, active = coef[:K], coef[K : 2 * K]
        others = [coef[(2 + i) * K : (3 + i) * K] for i in range(inner)]
        extras = [coef[(1 + layers + i) * K : (2 + layers + i) * K] for i in range(inner - 1)]
        at = (2 + inner + max(inner - 1, 0)) * K
        lines = coef[at:].astype(f32)
        active_f = active.astype(f32)

        def scale(i):
            row = inner + 2 * i
            return lines[row : row + 1] + lines[row + 1 : row + 2]

        def weight(n):
            total = jnp.zeros_like(lines[:1])
            for l in range(n + 1, layers):
                total = total + jnp.where(section < l, lines[l - 1 : l], 0.0)
            return total

        coarse, fine = split(grad.astype(f32) * scale(0))
        here = slice(m * coef.shape[1], (m + 1) * coef.shape[1])
        lefts[:K, here] = coarse
        lefts[K : 2 * K, here] = fine
        lefts[2 * K : 3 * K, here] = (-weight(0) * active_f).astype(bf16)
        lefts[3 * K :, here] = active
        for i in range(inner):
            factor = jnp.where(above[i], scale(1 + i), 1.0)
            other = (others[i].astype(f32) * factor).astype(bf16)
            mate = jnp.where(above[i], active_f, coarse.astype(f32)).astype(bf16)
            held = others[i]
            if i >= 1:
                held = jnp.where(section < i, extras[i - 1].astype(f32), held.astype(f32))
            held = jnp.where(section == i, active_f, held.astype(f32)).astype(bf16)
            pulled = (-weight(i) * active_f).astype(bf16)
            for values, value in zip(mates_of[i], (mate, other, pulled, held), strict=True):
                values.append(value)
    for i in range(inner):
        mate, other, pulled, held = (jnp.concatenate(v, axis=1) for v in mates_of[i])
        mates[2 * i] = dot_nt(mate, other).astype(bf16)
        mates[2 * i + 1] = dot_nt(pulled, held).astype(bf16)


def grads_kernel(layers, bottle, width, group, chunks, turn, *refs):
    K = bottle
    inner = layers - 1
    section, _, own_slot = whereabouts(group, chunks)
    final = turn == layers - 1
    if turn == 0:
        coefs, refs = refs[:MEMBERS], refs[MEMBERS:]
        pieces, gain, both, *outs, lefts, mates = refs
        factors_kernel_part(layers, bottle, section, coefs, lefts, mates)
        before = []
    else:
        lefts, mates, pieces, gain, both = refs[:5]
        before, outs = refs[5 : 5 + turn], list(refs[5 + turn :])
    parcel = outs.pop() if final else outs[0]
    by_hidden = dot_nn(lefts[: 3 * K], pieces[0])
    by_close = dot_nn(lefts[3 * K :], pieces[1])
    down = by_hidden[:K] + by_hidden[K : 2 * K]
    up = by_close + by_hidden[2 * K :]
    for i in range(inner):
        above = section <= i
        other = i + jnp.where(above, 1, 0)
        term = dot_nn(mates[2 * i], both[turn, jnp.where(above, other, layers + other)])
        up = up + jnp.where(above, term, 0.0)
        down = down + jnp.where(above, 0.0, term)
        up = up + dot_nn(mates[2 * i + 1], both[turn, layers + i])
    down = down * gain[turn]
    start = (section ^ turn) * group if final else 0
    for part in range(group):
        here = slice(part * width, (part + 1) * width)
        parcel[start + part, 0] = down[:, here]
        parcel[start + part, 1] = up[:, here]
    if not final:
        return
    for k, ref in enumerate(before):
        for part in range(group):
            parcel[(section ^ k) * group + part] = ref[part]
    if len(outs) == 1:
        outs[0][...] = parcel[...]
    else:
        for r, out in enumerate(outs):
            out[...] = parcel[own_slot ^ r].astype(out.dtype)


def per_device(inputs_down, inputs_up, cotan_down, cotan_up, norm_gains, adapt_down, adapt_up):
    sections = lax.axis_size("section")
    replicas = lax.axis_size("dp")
    section = lax.axis_index("section")
    replica = lax.axis_index("dp")
    layers = sections
    chunks = replicas // sections
    group = chunks // MEMBERS
    slots = replicas // MEMBERS
    bottle = adapt_down.shape[1]
    features = adapt_down.shape[2]
    share = features // sections
    width = features // replicas
    columns = group * width
    label, slot = label_slot(replica, group, chunks)
    micro, tokens = inputs_down.shape[0], inputs_down.shape[1]
    half = micro * tokens
    rows = 2 * half
    inner = layers - 1
    aligned = width % 128 == 0
    params = pltpu.CompilerParams(vmem_limit_bytes=VMEM_BYTES)

    acts = (inputs_down, inputs_up, cotan_down, cotan_up)
    if aligned:
        taken = (*acts, norm_gains[:, None, :], adapt_down)
        both, tall, *packed = pl.pallas_call(
            functools.partial(pack_kernel, width, group, chunks),
            out_shape=[
                pltpu.VMEM((2, rows, share), bf16),
                pltpu.VMEM((bottle + 16, features), bf16),
            ]
            + [pltpu.VMEM((2, rows, columns), bf16)] * MEMBERS,
            in_specs=[IN_HBM] * 6,
            out_specs=[IN_VMEM] * (2 + MEMBERS),
            scratch_shapes=[
                pltpu.VMEM((1, features), bf16),
                pltpu.SemaphoreType.DMA((4 * micro + 2,)),
            ],
            compiler_params=params,
            name="pack",
        )(*[pltpu.with_memory_space_constraint(v, pltpu.HBM) for v in taken])
    else:
        tall = jnp.concatenate(
            [adapt_down[0], jnp.broadcast_to(norm_gains, (16, features))], axis=0
        )
        both = jnp.concatenate([v.reshape(half, share) for v in acts], axis=0)
        both = both.reshape(2, rows, share)
        parts = both.reshape(2, rows, chunks, width)
        packed = []
        for k in range(MEMBERS):
            cuts = [
                lax.dynamic_index_in_dim(
                    parts, chunk_of(label ^ k, part, section), 2, keepdims=False
                )
                for part in range(group)
            ]
            packed.append(jnp.concatenate(cuts, axis=2))

    own = (tall, lax.optimization_barrier((adapt_up, *packed))[0])
    weights = [own]
    for k in range(1, sections):
        weights.append(tuple(from_partner(w, "section", k) for w in own))
    flat = [w for ws in weights for w in ws]
    pieces = [packed[0]]
    for k in range(1, MEMBERS):
        pieces.append(from_partner(packed[k], "dp", LEADERS[k]))
    prod_rows = (3 * layers - 1) * bottle + 8
    gram_rows = max(inner, 1) * bottle
    sides = [(prod_rows, rows), (gram_rows, 2 * gram_rows)]
    if rows == 2 * gram_rows:
        sides = [(prod_rows + gram_rows, rows)]
    sums = pl.pallas_call(
        functools.partial(products_kernel, layers),
        out_shape=[jax.ShapeDtypeStruct(side, f32) for side in sides],
        in_specs=[IN_VMEM] * (1 + 2 * sections),
        out_specs=[IN_VMEM] * len(sides),
        scratch_shapes=[pltpu.VMEM((layers, bottle, share), bf16)] * 3,
        compiler_params=params,
        cost_estimate=cost(COST_PRODUCTS),
        name="products",
    )(both, *flat)
    sums = list(sums)
    for k in range(1, sections):
        sums += [from_partner(v, "section", k) for v in sums[: len(sides)]]

    tail = inner + 2 * layers
    coef_rows = (2 + inner + max(inner - 1, 0)) * bottle + -(-tail // 16) * 16
    coef = pl.pallas_call(
        functools.partial(relay_kernel, layers, bottle, features, sections),
        out_shape=jax.ShapeDtypeStruct((coef_rows, rows), bf16),
        in_specs=[IN_VMEM] * len(sums),
        out_specs=IN_VMEM,
        scratch_shapes=[pltpu.VMEM((2 * layers, bottle, rows), bf16)],
        compiler_params=params,
        cost_estimate=cost(COST_SMALL),
        name="relay",
    )(*sums)
    coefs = [coef] + [from_partner(coef, "dp", LEADERS[k]) for k in range(1, MEMBERS)]
    cut_shapes = [
        jax.ShapeDtypeStruct((layers, 1, columns), f32),
        jax.ShapeDtypeStruct((layers, 2 * layers, bottle, columns), bf16),
    ]
    if aligned:
        gain_cut, both_cut = pl.pallas_call(
            functools.partial(cut_kernel, layers, width, group, chunks),
            out_shape=cut_shapes,
            in_specs=[IN_VMEM] * len(flat),
            out_specs=[IN_VMEM] * 2,
            compiler_params=params,
            cost_estimate=cost(COST_SMALL),
            name="cut",
        )(*flat)
    else:
        gain_cut = jnp.zeros(cut_shapes[0].shape, f32)
        both_cut = jnp.zeros(cut_shapes[1].shape, bf16)
        for k in range(layers):
            for part in range(group):
                at = section ^ k
                chunk = at * chunks + chunk_of(label, part, at)
                for w, ws in enumerate(weights):
                    down, up = (
                        lax.dynamic_index_in_dim(
                            v.reshape(-1, replicas, width), chunk, 1, keepdims=False
                        )
                        for v in ws
                    )
                    down, gain = down[:bottle], down[bottle : bottle + 1]
                    low = (gain.astype(f32) * down.astype(f32)).astype(bf16)
                    layer = section ^ w
                    spot = (k, layer, 0, part * width)
                    both_cut = lax.dynamic_update_slice(both_cut, low[None, None], spot)
                    spot = (k, layers + layer, 0, part * width)
                    both_cut = lax.dynamic_update_slice(both_cut, up[None, None], spot)
                    if w == 0:
                        gain_cut = lax.dynamic_update_slice(
                            gain_cut, gain.astype(f32)[None], (k, 0, part * width)
                        )

    gated = list(lax.optimization_barrier((*pieces, coef))[:-1])
    stacked = pl.pallas_call(
        stack_kernel,
        out_shape=jax.ShapeDtypeStruct((2, MEMBERS * rows, columns), bf16),
        in_specs=[IN_VMEM] * MEMBERS,
        out_specs=IN_VMEM,
        compiler_params=params,
        cost_estimate=cost(COST_SMALL),
        name="stack",
    )(*gated)
    handed = [None] + [from_partner(stacked, "section", k) for k in range(1, sections)]

    message = (2, bottle, width)
    left_shape = jax.ShapeDtypeStruct((4 * bottle, MEMBERS * rows), bf16)
    mate_shape = jax.ShapeDtypeStruct((max(2 * inner, 1), bottle, bottle), bf16)
    held = jax.ShapeDtypeStruct((group,) + message, f32)
    before = []
    for k in range(sections):
        shapes, scratch = [held], []
        if k == sections - 1:
            scratch = [pltpu.VMEM((slots,) + message, f32)]
            shapes = [jax.ShapeDtypeStruct((slots,) + message, f32)]
            if aligned:
                shapes = [jax.ShapeDtypeStruct(message, f32)]
                shapes += [jax.ShapeDtypeStruct(message, bf16)] * (slots - 1)
        if k == 0:
            shapes += [left_shape, mate_shape]
            operands = (*coefs, stacked, gain_cut, both_cut)
        else:
            operands = (lefts, mates, handed[k], gain_cut, both_cut, *before)
        parcels = pl.pallas_call(
            functools.partial(grads_kernel, layers, bottle, width, group, chunks, k),
            out_shape=shapes,
            in_specs=[IN_VMEM] * len(operands),
            out_specs=[IN_VMEM] * len(shapes),
            scratch_shapes=scratch,
            compiler_params=params,
            cost_estimate=cost(COST_GRADS),
            name="grads",
        )(*operands)
        if k == 0:
            *parcels, lefts, mates = parcels
        if k < sections - 1:
            before += parcels
    if not aligned:
        parcels = [
            lax.dynamic_index_in_dim(parcels[0], slot ^ r, 0, keepdims=False)
            for r in range(slots)
        ]
        parcels[1:] = [v.astype(bf16) for v in parcels[1:]]

    total = parcels[0]
    for r in (*range(slots // 2, slots), *range(1, slots // 2)):
        received = from_partner(parcels[r], "dp", mask(r, group, chunks))
        total = total + received.astype(f32)
    return (total[0][None], total[1][None])


def solution(mesh):
    placed = (
        P(None, "dp", "section"),
        P(None, "dp", "section"),
        P(None, "dp", "section"),
        P(None, "dp", "section"),
        P("section", None),
        P("section", None, None),
        P("section", None, None),
    )
    return jax.shard_map(
        per_device,
        mesh=mesh,
        in_specs=placed,
        out_specs=(P("section", None, "dp"), P("section", None, "dp")),
        check_vma=False,
    )
```

```python
import functools

import jax
import jax.numpy as jnp
from jax import lax
from jax.experimental import pallas as pl
from jax.experimental.pallas import tpu as pltpu
from jax.sharding import PartitionSpec as P

epsilon = 1e-05
VMEM_BYTES = 32 * 1024 * 1024
MEMBERS = 4
STAR = True
TWIST = 0
COST_PRODUCTS = 12
COST_SMALL = 0.1
COST_GRADS = 10
f32 = jnp.float32
bf16 = jnp.bfloat16
IN_VMEM = pl.BlockSpec(memory_space=pltpu.VMEM)
IN_HBM = pl.BlockSpec(memory_space=pltpu.HBM)


def cost(micros):
    return pl.CostEstimate(flops=int(micros * 1.1e9), bytes_accessed=0, transcendentals=0)


def from_partner(value, axis, flip):
    return lax.ppermute(value, axis, [(i, i ^ flip) for i in range(lax.axis_size(axis))])


def dot_nn(left, right):
    return lax.dot_general(left, right, (((1,), (0,)), ((), ())), preferred_element_type=f32)


def dot_nt(left, right):
    return lax.dot_general(left, right, (((1,), (1,)), ((), ())), preferred_element_type=f32)


def split(value):
    high = value.astype(bf16)
    return high, (value - high.astype(f32)).astype(bf16)


def dot_tn(left, right):
    return lax.dot_general(left, right, (((0,), (0,)), ((), ())), preferred_element_type=f32)


def dot_split(left, right, dot=dot_nn):
    high, low = split(left)
    return dot(high, right) + dot(low, right)


LEADERS = (0, 1, 2, 4) if STAR else (0, 1, 2, 3)


def leader(label):
    return label + (label == 3) if STAR else label


def mask(slot, group, chunks):
    section, part = divmod(slot, group)
    low = (part & 1) * 7 + (part >> 1) * 8 if STAR else part * 4
    return section * chunks ^ (section & 1) * TWIST ^ low


def label_slot(replica, group, chunks):
    section = replica // chunks
    local = replica % chunks ^ (section & 1) * TWIST
    if not STAR:
        return local % 4, section * group + local // 4
    low = local & 7
    label = (low & 3) ^ (low >> 2) * 3
    odd = (low != 0) & (low != 1) & (low != 2) & (low != 4)
    return label, section * group + (local >> 3) * 2 + odd.astype(jnp.int32)


def whereabouts(group, chunks):
    section = lax.axis_index("section")
    label, slot = label_slot(lax.axis_index("dp"), group, chunks)
    return section, label, slot


def chunk_of(label, part, section):
    low = (part & 1) * 7 + (part >> 1) * 8 if STAR else part * 4
    return leader(label) ^ low ^ (section & 1) * TWIST


def pack_kernel(width, group, chunks, *refs):
    acts, gain, down = refs[:4], refs[4], refs[5]
    both, tall = refs[6:8]
    outs = refs[8:-2]
    line, sems = refs[-2:]
    micro, tokens = acts[0].shape[0], acts[0].shape[1]
    bottle = down.shape[1]
    section, label, _ = whereabouts(group, chunks)
    copies = []
    for a, act in enumerate(acts):
        for m in range(micro):
            start = ((a % 2) * micro + m) * tokens
            copies.append(
                pltpu.make_async_copy(
                    act.at[m], both.at[a // 2, pl.ds(start, tokens)], sems.at[len(copies)]
                )
            )
    count = len(copies)
    copies.append(pltpu.make_async_copy(gain.at[0], line, sems.at[count]))
    copies.append(
        pltpu.make_async_copy(down.at[0], tall.at[pl.ds(0, bottle)], sems.at[count + 1])
    )
    for copy in copies:
        copy.start()
    for n in range(count):
        copies[n].wait()
        a, m = divmod(n, micro)
        start = ((a % 2) * micro + m) * tokens
        for k, out in enumerate(outs):
            for part in range(group):
                chunk = chunk_of(label ^ k, part, section)
                span = pl.ds(pl.multiple_of(chunk * width, width), width)
                out[a // 2, start : start + tokens, part * width : (part + 1) * width] = both[
                    a // 2, start : start + tokens, span
                ]
    copies[count].wait()
    tall[bottle:] = jnp.broadcast_to(line[...], (tall.shape[0] - bottle, tall.shape[1]))
    copies[count + 1].wait()


def two_parts(refs):
    if len(refs) == 2:
        return refs
    height, side = refs[0].shape
    return refs[0].at[: height - side // 2], refs[0].at[height - side // 2 :]


def products_kernel(layers, *refs):
    acts = refs[0]
    weights = [refs[1 + 2 * k : 3 + 2 * k] for k in range(layers)]
    outs = refs[1 + 2 * layers : -3]
    prod_out, gram_out = two_parts(outs)
    low_scr, fine_scr, high_scr = refs[-3:]
    bottle = weights[0][1].shape[1]
    gain_row = slice(bottle, bottle + 1)
    features = acts.shape[2]
    section = lax.axis_index("section")
    mine = pl.ds(pl.multiple_of(section * features, features), features)
    for k in range(layers):
        tall, up = weights[k]
        layer = section ^ k
        exact = tall[gain_row, mine].astype(f32) * tall[:bottle, mine].astype(f32)
        low, fine = split(exact)
        low_scr[layer] = low
        fine_scr[layer] = fine
        high_scr[layer] = up[0, :, mine]
    hidden = acts[0]
    low_all = low_scr[...].reshape(layers * bottle, features)
    fine_all = fine_scr[...].reshape(layers * bottle, features)
    high_all = high_scr[...].reshape(layers * bottle, features)
    size = (layers - 1) * bottle
    at = layers * bottle
    prod_out[:at] = dot_nt(low_all, hidden) + dot_nt(fine_all, hidden)
    if layers > 1:
        prod_out[at : at + size] = dot_nt(high_all[:size], hidden)
    at += size
    prod_out[at : at + layers * bottle] = dot_nt(high_all, acts[1])
    at += layers * bottle
    square = dot_nt(hidden, hidden)
    eye = lax.broadcasted_iota(jnp.int32, square.shape, 0) == lax.broadcasted_iota(
        jnp.int32, square.shape, 1
    )
    norms = jnp.sum(jnp.where(eye, square, 0.0), axis=0, keepdims=True)
    prod_out[at : at + 8] = jnp.broadcast_to(norms, (8, norms.shape[1]))
    if layers > 1:
        high_part = high_all[:size]
        low_part = low_all[bottle:]
        fine_part = fine_all[bottle:]
        gram_out[:, :size] = dot_nt(high_part, low_part) + dot_nt(high_part, fine_part)
        gram_out[:, size:] = dot_nt(high_part, high_part)
    else:
        gram_out[...] = jnp.zeros_like(gram_out)


def relay_kernel(layers, bottle, features, sections, *refs):
    coef_out, hold = refs[-2:]
    each = (len(refs) - 2) // sections
    prods, grams = zip(
        *(two_parts(refs[each * k : each * (k + 1)]) for k in range(sections)), strict=True
    )
    section = lax.axis_index("section")
    prod = sum((ref[...] for ref in prods[1:]), prods[0][...])
    gram = sum((ref[...] for ref in grams[1:]), grams[0][...])
    K = bottle
    inner = layers - 1
    h_low = [prod[l * K : (l + 1) * K] for l in range(layers)]
    at = layers * K
    h_high = [prod[at + l * K : at + (l + 1) * K] for l in range(inner)]
    at += inner * K
    u_high = [prod[at + l * K : at + (l + 1) * K] for l in range(layers)]
    at += layers * K
    norm = prod[at : at + 1]

    def high_low(m, l):
        return gram[m * K : (m + 1) * K, (l - 1) * K : l * K]

    def high_high(m, n):
        return gram[m * K : (m + 1) * K, (inner + n) * K : (inner + n + 1) * K]

    inverses, bottles, hidden_high = [], [], []
    for l in range(layers):
        inverse = lax.rsqrt(jnp.maximum(norm, 0.0) * (1.0 / features) + epsilon)
        value = h_low[l] * inverse
        active = (value * jax.nn.sigmoid(value)).astype(bf16)
        inverses.append(inverse)
        bottles.append(value)
        hold[l] = active
        hidden_high.append(list(h_high))
        if l < inner:
            before = h_high[l]
            h_high = [h_high[n] + dot_split(high_high(n, l), active) for n in range(inner)]
            for n in range(l + 1, layers):
                h_low[n] = h_low[n] + dot_split(high_low(l, n), active, dot_tn)
            norm = norm + jnp.sum(
                active.astype(f32) * (before + h_high[l]), axis=0, keepdims=True
            )
    pulls = [None] * layers
    for l in range(layers - 1, -1, -1):
        sigma = jax.nn.sigmoid(bottles[l])
        coarse = (u_high[l] * sigma * (1.0 + bottles[l] * (1.0 - sigma))).astype(bf16)
        hold[layers + l] = coarse
        if l == 0:
            break
        grad = coarse.astype(f32)
        scaled, fine = split(grad * inverses[l])
        pull = (
            inverses[l]
            * inverses[l]
            * jnp.sum(grad * bottles[l], axis=0, keepdims=True)
            * (1.0 / features)
        )
        pulls[l] = pull
        for n in range(l):
            u_high[n] = (
                u_high[n]
                + dot_split(high_low(n, l), scaled)
                + dot_nn(high_low(n, l).astype(bf16), fine)
                - pull * hidden_high[l][n]
            )
    blocks = [hold[layers + section], hold[section]]
    for i in range(inner):
        other = i + jnp.where(section <= i, 1, 0)
        blocks.append(hold[jnp.where(section <= i, layers + other, other)])
    blocks += [hold[n] for n in range(1, inner)]
    for n, block in enumerate(blocks):
        coef_out[n * K : (n + 1) * K] = block

    def inverse_at(layer):
        value = inverses[0]
        for l in range(1, layers):
            value = jnp.where(layer == l, inverses[l], value)
        return value

    lines = [line.astype(bf16).astype(f32) for line in pulls[1:]]
    scales = [inverse_at(section)]
    scales += [inverse_at(i + jnp.where(section <= i, 1, 0)) for i in range(inner)]
    for scale in scales:
        lines.extend(part.astype(f32) for part in split(scale))
    tail = coef_out.shape[0] - len(blocks) * K
    lines += [jnp.zeros_like(norm)] * (tail - len(lines))
    coef_out[len(blocks) * K :] = jnp.concatenate(lines, axis=0).astype(bf16)


def cut_kernel(layers, width, group, chunks, *refs):
    weights = [refs[2 * k : 2 * k + 2] for k in range(layers)]
    gain_out, both_out = refs[2 * layers :]
    bottle = weights[0][1].shape[1]
    gain_row = slice(bottle, bottle + 1)
    here_section, label, _ = whereabouts(group, chunks)
    for k in range(layers):
        section = here_section ^ k
        for part in range(group):
            chunk = section * chunks + chunk_of(label, part, section)
            span = pl.ds(pl.multiple_of(chunk * width, width), width)
            here = slice(part * width, (part + 1) * width)
            gain_out[k, :, here] = weights[0][0][gain_row, span].astype(f32)
            for w in range(layers):
                tall, up = weights[w]
                layer = here_section ^ w
                low = tall[gain_row, span].astype(f32) * tall[:bottle, span].astype(f32)
                both_out[k, layer, :, here] = low.astype(bf16)
                both_out[k, layers + layer, :, here] = up[0, :, span]


def stack_kernel(*refs):
    rows = refs[0].shape[1]
    for k, ref in enumerate(refs[:-1]):
        refs[-1][:, k * rows : (k + 1) * rows] = ref[...]


def factors_kernel_part(layers, bottle, section, coefs, lefts, mates):
    K = bottle
    inner = layers - 1
    above = [section <= i for i in range(inner)]
    mates_of = [([], [], [], []) for _ in range(inner)]
    for m in range(MEMBERS):
        coef = coefs[m][...]
        grad, active = coef[:K], coef[K : 2 * K]
        others = [coef[(2 + i) * K : (3 + i) * K] for i in range(inner)]
        extras = [coef[(1 + layers + i) * K : (2 + layers + i) * K] for i in range(inner - 1)]
        at = (2 + inner + max(inner - 1, 0)) * K
        lines = coef[at:].astype(f32)
        active_f = active.astype(f32)

        def scale(i):
            row = inner + 2 * i
            return lines[row : row + 1] + lines[row + 1 : row + 2]

        def weight(n):
            total = jnp.zeros_like(lines[:1])
            for l in range(n + 1, layers):
                total = total + jnp.where(section < l, lines[l - 1 : l], 0.0)
            return total

        coarse, fine = split(grad.astype(f32) * scale(0))
        here = slice(m * coef.shape[1], (m + 1) * coef.shape[1])
        lefts[:K, here] = coarse
        lefts[K : 2 * K, here] = fine
        lefts[2 * K : 3 * K, here] = (-weight(0) * active_f).astype(bf16)
        lefts[3 * K :, here] = active
        for i in range(inner):
            factor = jnp.where(above[i], scale(1 + i), 1.0)
            other = (others[i].astype(f32) * factor).astype(bf16)
            mate = jnp.where(above[i], active_f, coarse.astype(f32)).astype(bf16)
            held = others[i]
            if i >= 1:
                held = jnp.where(section < i, extras[i - 1].astype(f32), held.astype(f32))
            held = jnp.where(section == i, active_f, held.astype(f32)).astype(bf16)
            pulled = (-weight(i) * active_f).astype(bf16)
            for values, value in zip(mates_of[i], (mate, other, pulled, held), strict=True):
                values.append(value)
    for i in range(inner):
        mate, other, pulled, held = (jnp.concatenate(v, axis=1) for v in mates_of[i])
        mates[4 * i], mates[4 * i + 1] = split(dot_nt(mate, other))
        mates[4 * i + 2], mates[4 * i + 3] = split(dot_nt(pulled, held))


def grads_kernel(layers, bottle, width, group, chunks, turn, *refs):
    K = bottle
    inner = layers - 1
    section, _, own_slot = whereabouts(group, chunks)
    final = turn == layers - 1
    if turn == 0:
        coefs, refs = refs[:MEMBERS], refs[MEMBERS:]
        pieces, gain, both, *outs, lefts, mates = refs
        factors_kernel_part(layers, bottle, section, coefs, lefts, mates)
        before = []
    else:
        lefts, mates, pieces, gain, both = refs[:5]
        before, outs = refs[5 : 5 + turn], list(refs[5 + turn :])
    parcel = outs.pop() if final else outs[0]
    by_hidden = dot_nn(lefts[: 3 * K], pieces[0])
    by_close = dot_nn(lefts[3 * K :], pieces[1])
    down = by_hidden[:K] + by_hidden[K : 2 * K]
    up = by_close + by_hidden[2 * K :]
    for i in range(inner):
        above = section <= i
        other = i + jnp.where(above, 1, 0)
        basis = both[turn, jnp.where(above, other, layers + other)]
        term = dot_nn(mates[4 * i], basis) + dot_nn(mates[4 * i + 1], basis)
        up = up + jnp.where(above, term, 0.0)
        down = down + jnp.where(above, 0.0, term)
        basis = both[turn, layers + i]
        up = up + dot_nn(mates[4 * i + 2], basis) + dot_nn(mates[4 * i + 3], basis)
    down = down * gain[turn]
    start = (section ^ turn) * group if final else 0
    for part in range(group):
        here = slice(part * width, (part + 1) * width)
        parcel[start + part, 0] = down[:, here]
        parcel[start + part, 1] = up[:, here]
    if not final:
        return
    for k, ref in enumerate(before):
        for part in range(group):
            parcel[(section ^ k) * group + part] = ref[part]
    if len(outs) == 1:
        outs[0][...] = parcel[...]
    else:
        for r, out in enumerate(outs):
            out[...] = parcel[own_slot ^ r].astype(out.dtype)


def per_device(inputs_down, inputs_up, cotan_down, cotan_up, norm_gains, adapt_down, adapt_up):
    sections = lax.axis_size("section")
    replicas = lax.axis_size("dp")
    section = lax.axis_index("section")
    replica = lax.axis_index("dp")
    layers = sections
    chunks = replicas // sections
    group = chunks // MEMBERS
    slots = replicas // MEMBERS
    bottle = adapt_down.shape[1]
    features = adapt_down.shape[2]
    share = features // sections
    width = features // replicas
    columns = group * width
    label, slot = label_slot(replica, group, chunks)
    micro, tokens = inputs_down.shape[0], inputs_down.shape[1]
    half = micro * tokens
    rows = 2 * half
    inner = layers - 1
    aligned = width % 128 == 0
    params = pltpu.CompilerParams(vmem_limit_bytes=VMEM_BYTES)

    acts = (inputs_down, inputs_up, cotan_down, cotan_up)
    if aligned:
        taken = (*acts, norm_gains[:, None, :], adapt_down)
        both, tall, *packed = pl.pallas_call(
            functools.partial(pack_kernel, width, group, chunks),
            out_shape=[
                pltpu.VMEM((2, rows, share), bf16),
                pltpu.VMEM((bottle + 16, features), bf16),
            ]
            + [pltpu.VMEM((2, rows, columns), bf16)] * MEMBERS,
            in_specs=[IN_HBM] * 6,
            out_specs=[IN_VMEM] * (2 + MEMBERS),
            scratch_shapes=[
                pltpu.VMEM((1, features), bf16),
                pltpu.SemaphoreType.DMA((4 * micro + 2,)),
            ],
            compiler_params=params,
            name="pack",
        )(*[pltpu.with_memory_space_constraint(v, pltpu.HBM) for v in taken])
    else:
        tall = jnp.concatenate(
            [adapt_down[0], jnp.broadcast_to(norm_gains, (16, features))], axis=0
        )
        both = jnp.concatenate([v.reshape(half, share) for v in acts], axis=0)
        both = both.reshape(2, rows, share)
        parts = both.reshape(2, rows, chunks, width)
        packed = []
        for k in range(MEMBERS):
            cuts = [
                lax.dynamic_index_in_dim(
                    parts, chunk_of(label ^ k, part, section), 2, keepdims=False
                )
                for part in range(group)
            ]
            packed.append(jnp.concatenate(cuts, axis=2))

    own = (tall, lax.optimization_barrier((adapt_up, *packed))[0])
    weights = [own]
    for k in range(1, sections):
        weights.append(tuple(from_partner(w, "section", k) for w in own))
    flat = [w for ws in weights for w in ws]
    pieces = [packed[0]]
    for k in range(1, MEMBERS):
        pieces.append(from_partner(packed[k], "dp", LEADERS[k]))
    prod_rows = (3 * layers - 1) * bottle + 8
    gram_rows = max(inner, 1) * bottle
    sides = [(prod_rows, rows), (gram_rows, 2 * gram_rows)]
    if rows == 2 * gram_rows:
        sides = [(prod_rows + gram_rows, rows)]
    sums = pl.pallas_call(
        functools.partial(products_kernel, layers),
        out_shape=[jax.ShapeDtypeStruct(side, f32) for side in sides],
        in_specs=[IN_VMEM] * (1 + 2 * sections),
        out_specs=[IN_VMEM] * len(sides),
        scratch_shapes=[pltpu.VMEM((layers, bottle, share), bf16)] * 3,
        compiler_params=params,
        cost_estimate=cost(COST_PRODUCTS),
        name="products",
    )(both, *flat)
    sums = list(sums)
    for k in range(1, sections):
        sums += [from_partner(v, "section", k) for v in sums[: len(sides)]]

    tail = inner + 2 * layers
    coef_rows = (2 + inner + max(inner - 1, 0)) * bottle + -(-tail // 16) * 16
    coef = pl.pallas_call(
        functools.partial(relay_kernel, layers, bottle, features, sections),
        out_shape=jax.ShapeDtypeStruct((coef_rows, rows), bf16),
        in_specs=[IN_VMEM] * len(sums),
        out_specs=IN_VMEM,
        scratch_shapes=[pltpu.VMEM((2 * layers, bottle, rows), bf16)],
        compiler_params=params,
        cost_estimate=cost(COST_SMALL),
        name="relay",
    )(*sums)
    coefs = [coef] + [from_partner(coef, "dp", LEADERS[k]) for k in range(1, MEMBERS)]
    cut_shapes = [
        jax.ShapeDtypeStruct((layers, 1, columns), f32),
        jax.ShapeDtypeStruct((layers, 2 * layers, bottle, columns), bf16),
    ]
    if aligned:
        gain_cut, both_cut = pl.pallas_call(
            functools.partial(cut_kernel, layers, width, group, chunks),
            out_shape=cut_shapes,
            in_specs=[IN_VMEM] * len(flat),
            out_specs=[IN_VMEM] * 2,
            compiler_params=params,
            cost_estimate=cost(COST_SMALL),
            name="cut",
        )(*flat)
    else:
        gain_cut = jnp.zeros(cut_shapes[0].shape, f32)
        both_cut = jnp.zeros(cut_shapes[1].shape, bf16)
        for k in range(layers):
            for part in range(group):
                at = section ^ k
                chunk = at * chunks + chunk_of(label, part, at)
                for w, ws in enumerate(weights):
                    down, up = (
                        lax.dynamic_index_in_dim(
                            v.reshape(-1, replicas, width), chunk, 1, keepdims=False
                        )
                        for v in ws
                    )
                    down, gain = down[:bottle], down[bottle : bottle + 1]
                    low = (gain.astype(f32) * down.astype(f32)).astype(bf16)
                    layer = section ^ w
                    spot = (k, layer, 0, part * width)
                    both_cut = lax.dynamic_update_slice(both_cut, low[None, None], spot)
                    spot = (k, layers + layer, 0, part * width)
                    both_cut = lax.dynamic_update_slice(both_cut, up[None, None], spot)
                    if w == 0:
                        gain_cut = lax.dynamic_update_slice(
                            gain_cut, gain.astype(f32)[None], (k, 0, part * width)
                        )

    gated = list(lax.optimization_barrier((*pieces, coef))[:-1])
    stacked = pl.pallas_call(
        stack_kernel,
        out_shape=jax.ShapeDtypeStruct((2, MEMBERS * rows, columns), bf16),
        in_specs=[IN_VMEM] * MEMBERS,
        out_specs=IN_VMEM,
        compiler_params=params,
        cost_estimate=cost(COST_SMALL),
        name="stack",
    )(*gated)
    handed = [None] + [from_partner(stacked, "section", k) for k in range(1, sections)]

    message = (2, bottle, width)
    left_shape = jax.ShapeDtypeStruct((4 * bottle, MEMBERS * rows), bf16)
    mate_shape = jax.ShapeDtypeStruct((max(4 * inner, 1), bottle, bottle), bf16)
    held = jax.ShapeDtypeStruct((group,) + message, f32)
    before = []
    for k in range(sections):
        shapes, scratch = [held], []
        if k == sections - 1:
            scratch = [pltpu.VMEM((slots,) + message, f32)]
            shapes = [jax.ShapeDtypeStruct((slots,) + message, f32)]
            if aligned:
                shapes = [jax.ShapeDtypeStruct(message, f32)]
                shapes += [jax.ShapeDtypeStruct(message, bf16)] * (slots - 1)
        if k == 0:
            shapes += [left_shape, mate_shape]
            operands = (*coefs, stacked, gain_cut, both_cut)
        else:
            operands = (lefts, mates, handed[k], gain_cut, both_cut, *before)
        parcels = pl.pallas_call(
            functools.partial(grads_kernel, layers, bottle, width, group, chunks, k),
            out_shape=shapes,
            in_specs=[IN_VMEM] * len(operands),
            out_specs=[IN_VMEM] * len(shapes),
            scratch_shapes=scratch,
            compiler_params=params,
            cost_estimate=cost(COST_GRADS),
            name="grads",
        )(*operands)
        if k == 0:
            *parcels, lefts, mates = parcels
        if k < sections - 1:
            before += parcels
    if not aligned:
        parcels = [
            lax.dynamic_index_in_dim(parcels[0], slot ^ r, 0, keepdims=False)
            for r in range(slots)
        ]
        parcels[1:] = [v.astype(bf16) for v in parcels[1:]]

    total = parcels[0]
    for r in (*range(slots // 2, slots), *range(1, slots // 2)):
        received = from_partner(parcels[r], "dp", mask(r, group, chunks))
        total = total + received.astype(f32)
    return (total[0][None], total[1][None])


def solution(mesh):
    placed = (
        P(None, "dp", "section"),
        P(None, "dp", "section"),
        P(None, "dp", "section"),
        P(None, "dp", "section"),
        P("section", None),
        P("section", None, None),
        P("section", None, None),
    )
    return jax.shard_map(
        per_device,
        mesh=mesh,
        in_specs=placed,
        out_specs=(P("section", None, "dp"), P("section", None, "dp")),
        check_vma=False,
    )
```

```python
import functools

import jax
import jax.numpy as jnp
from jax import lax
from jax.experimental import pallas as pl
from jax.experimental.pallas import tpu as pltpu
from jax.sharding import PartitionSpec as P

epsilon = 1e-05
VMEM_BYTES = 32 * 1024 * 1024
MEMBERS = 4
STAR = True
TWIST = 0
COST_PRODUCTS = 12
COST_SMALL = 0.1
COST_GRADS = 10
f32 = jnp.float32
bf16 = jnp.bfloat16
IN_VMEM = pl.BlockSpec(memory_space=pltpu.VMEM)
IN_HBM = pl.BlockSpec(memory_space=pltpu.HBM)


def cost(micros):
    return pl.CostEstimate(flops=int(micros * 1.1e9), bytes_accessed=0, transcendentals=0)


def from_partner(value, axis, flip):
    return lax.ppermute(value, axis, [(i, i ^ flip) for i in range(lax.axis_size(axis))])


def dot_nn(left, right):
    return lax.dot_general(left, right, (((1,), (0,)), ((), ())), preferred_element_type=f32)


def dot_nt(left, right):
    return lax.dot_general(left, right, (((1,), (1,)), ((), ())), preferred_element_type=f32)


def split(value):
    high = value.astype(bf16)
    return high, (value - high.astype(f32)).astype(bf16)


def dot_tn(left, right):
    return lax.dot_general(left, right, (((0,), (0,)), ((), ())), preferred_element_type=f32)


def dot_split(left, right, dot=dot_nn):
    high, low = split(left)
    return dot(high, right) + dot(low, right)


LEADERS = (0, 1, 2, 4) if STAR else (0, 1, 2, 3)


def leader(label):
    return label + (label == 3) if STAR else label


def mask(slot, group, chunks):
    section, part = divmod(slot, group)
    low = (part & 1) * 7 + (part >> 1) * 8 if STAR else part * 4
    return section * chunks ^ (section & 1) * TWIST ^ low


def label_slot(replica, group, chunks):
    section = replica // chunks
    local = replica % chunks ^ (section & 1) * TWIST
    if not STAR:
        return local % 4, section * group + local // 4
    low = local & 7
    label = (low & 3) ^ (low >> 2) * 3
    odd = (low != 0) & (low != 1) & (low != 2) & (low != 4)
    return label, section * group + (local >> 3) * 2 + odd.astype(jnp.int32)


def whereabouts(group, chunks):
    section = lax.axis_index("section")
    label, slot = label_slot(lax.axis_index("dp"), group, chunks)
    return section, label, slot


def chunk_of(label, part, section):
    low = (part & 1) * 7 + (part >> 1) * 8 if STAR else part * 4
    return leader(label) ^ low ^ (section & 1) * TWIST


def pack_kernel(width, group, chunks, *refs):
    acts, gain, down = refs[:4], refs[4], refs[5]
    both, tall = refs[6:8]
    outs = refs[8:-2]
    line, sems = refs[-2:]
    micro, tokens = acts[0].shape[0], acts[0].shape[1]
    bottle = down.shape[1]
    section, label, _ = whereabouts(group, chunks)
    copies = []
    for a, act in enumerate(acts):
        for m in range(micro):
            start = ((a % 2) * micro + m) * tokens
            copies.append(
                pltpu.make_async_copy(
                    act.at[m], both.at[a // 2, pl.ds(start, tokens)], sems.at[len(copies)]
                )
            )
    count = len(copies)
    copies.append(pltpu.make_async_copy(gain.at[0], line, sems.at[count]))
    copies.append(
        pltpu.make_async_copy(down.at[0], tall.at[pl.ds(0, bottle)], sems.at[count + 1])
    )
    for copy in copies:
        copy.start()
    for n in range(count):
        copies[n].wait()
        a, m = divmod(n, micro)
        start = ((a % 2) * micro + m) * tokens
        for k, out in enumerate(outs, 1):
            for part in range(group):
                chunk = chunk_of(label ^ k, part, section)
                span = pl.ds(pl.multiple_of(chunk * width, width), width)
                out[a // 2, start : start + tokens, part * width : (part + 1) * width] = both[
                    a // 2, start : start + tokens, span
                ]
    copies[count].wait()
    tall[bottle:] = jnp.broadcast_to(line[...], (tall.shape[0] - bottle, tall.shape[1]))
    copies[count + 1].wait()


def two_parts(refs):
    if len(refs) == 2:
        return refs
    height, side = refs[0].shape
    return refs[0].at[: height - side // 2], refs[0].at[height - side // 2 :]


def products_kernel(layers, *refs):
    acts = refs[0]
    weights = [refs[1 + 2 * k : 3 + 2 * k] for k in range(layers)]
    outs = refs[1 + 2 * layers : -3]
    prod_out, gram_out = two_parts(outs)
    low_scr, fine_scr, high_scr = refs[-3:]
    bottle = weights[0][1].shape[1]
    gain_row = slice(bottle, bottle + 1)
    features = acts.shape[2]
    section = lax.axis_index("section")
    mine = pl.ds(pl.multiple_of(section * features, features), features)
    for k in range(layers):
        tall, up = weights[k]
        layer = section ^ k
        exact = tall[gain_row, mine].astype(f32) * tall[:bottle, mine].astype(f32)
        low, fine = split(exact)
        low_scr[layer] = low
        fine_scr[layer] = fine
        high_scr[layer] = up[0, :, mine]
    hidden = acts[0]
    low_all = low_scr[...].reshape(layers * bottle, features)
    fine_all = fine_scr[...].reshape(layers * bottle, features)
    high_all = high_scr[...].reshape(layers * bottle, features)
    size = (layers - 1) * bottle
    at = layers * bottle
    prod_out[:at] = dot_nt(low_all, hidden) + dot_nt(fine_all, hidden)
    if layers > 1:
        prod_out[at : at + size] = dot_nt(high_all[:size], hidden)
    at += size
    prod_out[at : at + layers * bottle] = dot_nt(high_all, acts[1])
    at += layers * bottle
    square = dot_nt(hidden, hidden)
    eye = lax.broadcasted_iota(jnp.int32, square.shape, 0) == lax.broadcasted_iota(
        jnp.int32, square.shape, 1
    )
    norms = jnp.sum(jnp.where(eye, square, 0.0), axis=0, keepdims=True)
    prod_out[at : at + 8] = jnp.broadcast_to(norms, (8, norms.shape[1]))
    if layers > 1:
        high_part = high_all[:size]
        low_part = low_all[bottle:]
        fine_part = fine_all[bottle:]
        gram_out[:, :size] = dot_nt(high_part, low_part) + dot_nt(high_part, fine_part)
        gram_out[:, size:] = dot_nt(high_part, high_part)
    else:
        gram_out[...] = jnp.zeros_like(gram_out)


def relay_kernel(layers, bottle, features, sections, *refs):
    coef_out, hold = refs[-2:]
    each = (len(refs) - 2) // sections
    prods, grams = zip(
        *(two_parts(refs[each * k : each * (k + 1)]) for k in range(sections)), strict=True
    )
    section = lax.axis_index("section")
    prod = sum((ref[...] for ref in prods[1:]), prods[0][...])
    gram = sum((ref[...] for ref in grams[1:]), grams[0][...])
    K = bottle
    inner = layers - 1
    h_low = [prod[l * K : (l + 1) * K] for l in range(layers)]
    at = layers * K
    h_high = [prod[at + l * K : at + (l + 1) * K] for l in range(inner)]
    at += inner * K
    u_high = [prod[at + l * K : at + (l + 1) * K] for l in range(layers)]
    at += layers * K
    norm = prod[at : at + 1]

    def high_low(m, l):
        return gram[m * K : (m + 1) * K, (l - 1) * K : l * K]

    def high_high(m, n):
        return gram[m * K : (m + 1) * K, (inner + n) * K : (inner + n + 1) * K]

    inverses, bottles, hidden_high = [], [], []
    for l in range(layers):
        inverse = lax.rsqrt(jnp.maximum(norm, 0.0) * (1.0 / features) + epsilon)
        value = h_low[l] * inverse
        active = (value * jax.nn.sigmoid(value)).astype(bf16)
        inverses.append(inverse)
        bottles.append(value)
        hold[l] = active
        hidden_high.append(list(h_high))
        if l < inner:
            before = h_high[l]
            h_high = [h_high[n] + dot_split(high_high(n, l), active) for n in range(inner)]
            for n in range(l + 1, layers):
                h_low[n] = h_low[n] + dot_split(high_low(l, n), active, dot_tn)
            norm = norm + jnp.sum(
                active.astype(f32) * (before + h_high[l]), axis=0, keepdims=True
            )
    pulls = [None] * layers
    for l in range(layers - 1, -1, -1):
        sigma = jax.nn.sigmoid(bottles[l])
        coarse = (u_high[l] * sigma * (1.0 + bottles[l] * (1.0 - sigma))).astype(bf16)
        hold[layers + l] = coarse
        if l == 0:
            break
        grad = coarse.astype(f32)
        scaled, fine = split(grad * inverses[l])
        pull = (
            inverses[l]
            * inverses[l]
            * jnp.sum(grad * bottles[l], axis=0, keepdims=True)
            * (1.0 / features)
        )
        pulls[l] = pull
        for n in range(l):
            u_high[n] = (
                u_high[n]
                + dot_split(high_low(n, l), scaled)
                + dot_nn(high_low(n, l).astype(bf16), fine)
                - pull * hidden_high[l][n]
            )
    blocks = [hold[layers + section], hold[section]]
    for i in range(inner):
        other = i + jnp.where(section <= i, 1, 0)
        blocks.append(hold[jnp.where(section <= i, layers + other, other)])
    blocks += [hold[n] for n in range(1, inner)]
    for n, block in enumerate(blocks):
        coef_out[n * K : (n + 1) * K] = block

    def inverse_at(layer):
        value = inverses[0]
        for l in range(1, layers):
            value = jnp.where(layer == l, inverses[l], value)
        return value

    lines = [line.astype(bf16).astype(f32) for line in pulls[1:]]
    scales = [inverse_at(section)]
    scales += [inverse_at(i + jnp.where(section <= i, 1, 0)) for i in range(inner)]
    for scale in scales:
        lines.extend(part.astype(f32) for part in split(scale))
    tail = coef_out.shape[0] - len(blocks) * K
    lines += [jnp.zeros_like(norm)] * (tail - len(lines))
    coef_out[len(blocks) * K :] = jnp.concatenate(lines, axis=0).astype(bf16)


def cut_kernel(layers, width, group, chunks, *refs):
    weights = [refs[2 * k : 2 * k + 2] for k in range(layers)]
    gain_out, both_out = refs[2 * layers :]
    bottle = weights[0][1].shape[1]
    gain_row = slice(bottle, bottle + 1)
    here_section, label, _ = whereabouts(group, chunks)
    for k in range(layers):
        section = here_section ^ k
        for part in range(group):
            chunk = section * chunks + chunk_of(label, part, section)
            span = pl.ds(pl.multiple_of(chunk * width, width), width)
            here = slice(part * width, (part + 1) * width)
            gain_out[k, :, here] = weights[0][0][gain_row, span].astype(f32)
            for w in range(layers):
                tall, up = weights[w]
                layer = here_section ^ w
                low = tall[gain_row, span].astype(f32) * tall[:bottle, span].astype(f32)
                both_out[k, layer, :, here] = low.astype(bf16)
                both_out[k, layers + layer, :, here] = up[0, :, span]


def stack_kernel(width, group, chunks, *refs):
    rows = refs[0].shape[1]
    out = refs[-1]
    if refs[0].shape[2] == out.shape[2]:
        out[:, :rows] = refs[0][...]
    else:
        section, label, _ = whereabouts(group, chunks)
        for part in range(group):
            chunk = chunk_of(label, part, section)
            span = pl.ds(pl.multiple_of(chunk * width, width), width)
            out[:, :rows, part * width : (part + 1) * width] = refs[0][:, :, span]
    for k, ref in enumerate(refs[1:-1], 1):
        out[:, k * rows : (k + 1) * rows] = ref[...]


def factors_kernel_part(layers, bottle, section, coefs, lefts, mates):
    K = bottle
    inner = layers - 1
    above = [section <= i for i in range(inner)]
    mates_of = [([], [], [], []) for _ in range(inner)]
    for m in range(MEMBERS):
        coef = coefs[m][...]
        grad, active = coef[:K], coef[K : 2 * K]
        others = [coef[(2 + i) * K : (3 + i) * K] for i in range(inner)]
        extras = [coef[(1 + layers + i) * K : (2 + layers + i) * K] for i in range(inner - 1)]
        at = (2 + inner + max(inner - 1, 0)) * K
        lines = coef[at:].astype(f32)
        active_f = active.astype(f32)

        def scale(i):
            row = inner + 2 * i
            return lines[row : row + 1] + lines[row + 1 : row + 2]

        def weight(n):
            total = jnp.zeros_like(lines[:1])
            for l in range(n + 1, layers):
                total = total + jnp.where(section < l, lines[l - 1 : l], 0.0)
            return total

        coarse, fine = split(grad.astype(f32) * scale(0))
        here = slice(m * coef.shape[1], (m + 1) * coef.shape[1])
        lefts[:K, here] = coarse
        lefts[K : 2 * K, here] = fine
        lefts[2 * K : 3 * K, here] = (-weight(0) * active_f).astype(bf16)
        lefts[3 * K :, here] = active
        for i in range(inner):
            factor = jnp.where(above[i], scale(1 + i), 1.0)
            other = (others[i].astype(f32) * factor).astype(bf16)
            mate = jnp.where(above[i], active_f, coarse.astype(f32)).astype(bf16)
            held = others[i]
            if i >= 1:
                held = jnp.where(section < i, extras[i - 1].astype(f32), held.astype(f32))
            held = jnp.where(section == i, active_f, held.astype(f32)).astype(bf16)
            pulled = (-weight(i) * active_f).astype(bf16)
            for values, value in zip(mates_of[i], (mate, other, pulled, held), strict=True):
                values.append(value)
    for i in range(inner):
        mate, other, pulled, held = (jnp.concatenate(v, axis=1) for v in mates_of[i])
        mates[2 * i] = dot_nt(mate, other).astype(bf16)
        mates[2 * i + 1] = dot_nt(pulled, held).astype(bf16)


def grads_kernel(layers, bottle, width, group, chunks, turn, *refs):
    K = bottle
    inner = layers - 1
    section, _, own_slot = whereabouts(group, chunks)
    final = turn == layers - 1
    if turn == 0:
        coefs, refs = refs[:MEMBERS], refs[MEMBERS:]
        pieces, gain, both, *outs, lefts, mates = refs
        factors_kernel_part(layers, bottle, section, coefs, lefts, mates)
        before = []
    else:
        lefts, mates, pieces, gain, both = refs[:5]
        before, outs = refs[5 : 5 + turn], list(refs[5 + turn :])
    parcel = outs.pop() if final else outs[0]
    by_hidden = dot_nn(lefts[: 3 * K], pieces[0])
    by_close = dot_nn(lefts[3 * K :], pieces[1])
    down = by_hidden[:K] + by_hidden[K : 2 * K]
    up = by_close + by_hidden[2 * K :]
    for i in range(inner):
        above = section <= i
        other = i + jnp.where(above, 1, 0)
        term = dot_nn(mates[2 * i], both[turn, jnp.where(above, other, layers + other)])
        up = up + jnp.where(above, term, 0.0)
        down = down + jnp.where(above, 0.0, term)
        up = up + dot_nn(mates[2 * i + 1], both[turn, layers + i])
    down = down * gain[turn]
    start = (section ^ turn) * group if final else 0
    for part in range(group):
        here = slice(part * width, (part + 1) * width)
        parcel[start + part, 0] = down[:, here]
        parcel[start + part, 1] = up[:, here]
    if not final:
        return
    for k, ref in enumerate(before):
        for part in range(group):
            parcel[(section ^ k) * group + part] = ref[part]
    if len(outs) == 1:
        outs[0][...] = parcel[...]
    else:
        for r, out in enumerate(outs):
            out[...] = parcel[own_slot ^ r].astype(out.dtype)


def per_device(inputs_down, inputs_up, cotan_down, cotan_up, norm_gains, adapt_down, adapt_up):
    sections = lax.axis_size("section")
    replicas = lax.axis_size("dp")
    section = lax.axis_index("section")
    replica = lax.axis_index("dp")
    layers = sections
    chunks = replicas // sections
    group = chunks // MEMBERS
    slots = replicas // MEMBERS
    bottle = adapt_down.shape[1]
    features = adapt_down.shape[2]
    share = features // sections
    width = features // replicas
    columns = group * width
    label, slot = label_slot(replica, group, chunks)
    micro, tokens = inputs_down.shape[0], inputs_down.shape[1]
    half = micro * tokens
    rows = 2 * half
    inner = layers - 1
    aligned = width % 128 == 0
    params = pltpu.CompilerParams(vmem_limit_bytes=VMEM_BYTES)

    acts = (inputs_down, inputs_up, cotan_down, cotan_up)
    if aligned:
        taken = (*acts, norm_gains[:, None, :], adapt_down)
        both, tall, *packed = pl.pallas_call(
            functools.partial(pack_kernel, width, group, chunks),
            out_shape=[
                pltpu.VMEM((2, rows, share), bf16),
                pltpu.VMEM((bottle + 16, features), bf16),
            ]
            + [pltpu.VMEM((2, rows, columns), bf16)] * (MEMBERS - 1),
            in_specs=[IN_HBM] * 6,
            out_specs=[IN_VMEM] * (1 + MEMBERS),
            scratch_shapes=[
                pltpu.VMEM((1, features), bf16),
                pltpu.SemaphoreType.DMA((4 * micro + 2,)),
            ],
            compiler_params=params,
            name="pack",
        )(*[pltpu.with_memory_space_constraint(v, pltpu.HBM) for v in taken])
        packed = [both, *packed]
    else:
        tall = jnp.concatenate(
            [adapt_down[0], jnp.broadcast_to(norm_gains, (16, features))], axis=0
        )
        both = jnp.concatenate([v.reshape(half, share) for v in acts], axis=0)
        both = both.reshape(2, rows, share)
        parts = both.reshape(2, rows, chunks, width)
        packed = []
        for k in range(MEMBERS):
            cuts = [
                lax.dynamic_index_in_dim(
                    parts, chunk_of(label ^ k, part, section), 2, keepdims=False
                )
                for part in range(group)
            ]
            packed.append(jnp.concatenate(cuts, axis=2))

    own = (tall, lax.optimization_barrier((adapt_up, *packed))[0])
    weights = [own]
    for k in range(1, sections):
        weights.append(tuple(from_partner(w, "section", k) for w in own))
    flat = [w for ws in weights for w in ws]
    pieces = [packed[0]]
    for k in range(1, MEMBERS):
        pieces.append(from_partner(packed[k], "dp", LEADERS[k]))
    prod_rows = (3 * layers - 1) * bottle + 8
    gram_rows = max(inner, 1) * bottle
    sides = [(prod_rows, rows), (gram_rows, 2 * gram_rows)]
    if rows == 2 * gram_rows:
        sides = [(prod_rows + gram_rows, rows)]
    sums = pl.pallas_call(
        functools.partial(products_kernel, layers),
        out_shape=[jax.ShapeDtypeStruct(side, f32) for side in sides],
        in_specs=[IN_VMEM] * (1 + 2 * sections),
        out_specs=[IN_VMEM] * len(sides),
        scratch_shapes=[pltpu.VMEM((layers, bottle, share), bf16)] * 3,
        compiler_params=params,
        cost_estimate=cost(COST_PRODUCTS),
        name="products",
    )(both, *flat)
    sums = list(sums)
    for k in range(1, sections):
        sums += [from_partner(v, "section", k) for v in sums[: len(sides)]]

    tail = inner + 2 * layers
    coef_rows = (2 + inner + max(inner - 1, 0)) * bottle + -(-tail // 16) * 16
    coef = pl.pallas_call(
        functools.partial(relay_kernel, layers, bottle, features, sections),
        out_shape=jax.ShapeDtypeStruct((coef_rows, rows), bf16),
        in_specs=[IN_VMEM] * len(sums),
        out_specs=IN_VMEM,
        scratch_shapes=[pltpu.VMEM((2 * layers, bottle, rows), bf16)],
        compiler_params=params,
        cost_estimate=cost(COST_SMALL),
        name="relay",
    )(*sums)
    coefs = [coef] + [from_partner(coef, "dp", LEADERS[k]) for k in range(1, MEMBERS)]
    cut_shapes = [
        jax.ShapeDtypeStruct((layers, 1, columns), f32),
        jax.ShapeDtypeStruct((layers, 2 * layers, bottle, columns), bf16),
    ]
    if aligned:
        gain_cut, both_cut = pl.pallas_call(
            functools.partial(cut_kernel, layers, width, group, chunks),
            out_shape=cut_shapes,
            in_specs=[IN_VMEM] * len(flat),
            out_specs=[IN_VMEM] * 2,
            compiler_params=params,
            cost_estimate=cost(COST_SMALL),
            name="cut",
        )(*flat)
    else:
        gain_cut = jnp.zeros(cut_shapes[0].shape, f32)
        both_cut = jnp.zeros(cut_shapes[1].shape, bf16)
        for k in range(layers):
            for part in range(group):
                at = section ^ k
                chunk = at * chunks + chunk_of(label, part, at)
                for w, ws in enumerate(weights):
                    down, up = (
                        lax.dynamic_index_in_dim(
                            v.reshape(-1, replicas, width), chunk, 1, keepdims=False
                        )
                        for v in ws
                    )
                    down, gain = down[:bottle], down[bottle : bottle + 1]
                    low = (gain.astype(f32) * down.astype(f32)).astype(bf16)
                    layer = section ^ w
                    spot = (k, layer, 0, part * width)
                    both_cut = lax.dynamic_update_slice(both_cut, low[None, None], spot)
                    spot = (k, layers + layer, 0, part * width)
                    both_cut = lax.dynamic_update_slice(both_cut, up[None, None], spot)
                    if w == 0:
                        gain_cut = lax.dynamic_update_slice(
                            gain_cut, gain.astype(f32)[None], (k, 0, part * width)
                        )

    gated = list(lax.optimization_barrier((*pieces, coef))[:-1])
    stacked = pl.pallas_call(
        functools.partial(stack_kernel, width, group, chunks),
        out_shape=jax.ShapeDtypeStruct((2, MEMBERS * rows, columns), bf16),
        in_specs=[IN_VMEM] * MEMBERS,
        out_specs=IN_VMEM,
        compiler_params=params,
        cost_estimate=cost(COST_SMALL),
        name="stack",
    )(*gated)
    handed = [None] + [from_partner(stacked, "section", k) for k in range(1, sections)]

    message = (2, bottle, width)
    left_shape = jax.ShapeDtypeStruct((4 * bottle, MEMBERS * rows), bf16)
    mate_shape = jax.ShapeDtypeStruct((max(2 * inner, 1), bottle, bottle), bf16)
    held = jax.ShapeDtypeStruct((group,) + message, f32)
    before = []
    for k in range(sections):
        shapes, scratch = [held], []
        if k == sections - 1:
            scratch = [pltpu.VMEM((slots,) + message, f32)]
            shapes = [jax.ShapeDtypeStruct((slots,) + message, f32)]
            if aligned:
                shapes = [jax.ShapeDtypeStruct(message, f32)]
                shapes += [jax.ShapeDtypeStruct(message, bf16)] * (slots - 1)
        if k == 0:
            shapes += [left_shape, mate_shape]
            operands = (*coefs, stacked, gain_cut, both_cut)
        else:
            operands = (lefts, mates, handed[k], gain_cut, both_cut, *before)
        parcels = pl.pallas_call(
            functools.partial(grads_kernel, layers, bottle, width, group, chunks, k),
            out_shape=shapes,
            in_specs=[IN_VMEM] * len(operands),
            out_specs=[IN_VMEM] * len(shapes),
            scratch_shapes=scratch,
            compiler_params=params,
            cost_estimate=cost(COST_GRADS),
            name="grads",
        )(*operands)
        if k == 0:
            *parcels, lefts, mates = parcels
        if k < sections - 1:
            before += parcels
    if not aligned:
        parcels = [
            lax.dynamic_index_in_dim(parcels[0], slot ^ r, 0, keepdims=False)
            for r in range(slots)
        ]
        parcels[1:] = [v.astype(bf16) for v in parcels[1:]]

    total = parcels[0]
    for r in (*range(slots // 2, slots), *range(1, slots // 2)):
        received = from_partner(parcels[r], "dp", mask(r, group, chunks))
        total = total + received.astype(f32)
    return (total[0][None], total[1][None])


def solution(mesh):
    placed = (
        P(None, "dp", "section"),
        P(None, "dp", "section"),
        P(None, "dp", "section"),
        P(None, "dp", "section"),
        P("section", None),
        P("section", None, None),
        P("section", None, None),
    )
    return jax.shard_map(
        per_device,
        mesh=mesh,
        in_specs=placed,
        out_specs=(P("section", None, "dp"), P("section", None, "dp")),
        check_vma=False,
    )
```

```python
import functools

import jax
import jax.numpy as jnp
from jax import lax
from jax.experimental import pallas as pl
from jax.experimental.pallas import tpu as pltpu
from jax.sharding import PartitionSpec as P

epsilon = 1e-05
VMEM_BYTES = 32 * 1024 * 1024
MEMBERS = 4
STAR = True
TWIST = 4
COST_PRODUCTS = 12
COST_SMALL = 0.1
COST_GRADS = 10
f32 = jnp.float32
bf16 = jnp.bfloat16
IN_VMEM = pl.BlockSpec(memory_space=pltpu.VMEM)
IN_HBM = pl.BlockSpec(memory_space=pltpu.HBM)


def cost(micros):
    return pl.CostEstimate(flops=int(micros * 1.1e9), bytes_accessed=0, transcendentals=0)


def from_partner(value, axis, flip):
    return lax.ppermute(value, axis, [(i, i ^ flip) for i in range(lax.axis_size(axis))])


def dot_nn(left, right):
    return lax.dot_general(left, right, (((1,), (0,)), ((), ())), preferred_element_type=f32)


def dot_nt(left, right):
    return lax.dot_general(left, right, (((1,), (1,)), ((), ())), preferred_element_type=f32)


def split(value):
    high = value.astype(bf16)
    return high, (value - high.astype(f32)).astype(bf16)


def dot_tn(left, right):
    return lax.dot_general(left, right, (((0,), (0,)), ((), ())), preferred_element_type=f32)


def dot_split(left, right, dot=dot_nn):
    high, low = split(left)
    return dot(high, right) + dot(low, right)


LEADERS = (0, 1, 2, 4) if STAR else (0, 1, 2, 3)


def leader(label):
    return label + (label == 3) if STAR else label


def mask(slot, group, chunks):
    section, part = divmod(slot, group)
    low = (part & 1) * 7 + (part >> 1) * 8 if STAR else part * 4
    return section * chunks ^ (section & 1) * TWIST ^ low


def label_slot(replica, group, chunks):
    section = replica // chunks
    local = replica % chunks ^ (section & 1) * TWIST
    if not STAR:
        return local % 4, section * group + local // 4
    low = local & 7
    label = (low & 3) ^ (low >> 2) * 3
    odd = (low != 0) & (low != 1) & (low != 2) & (low != 4)
    return label, section * group + (local >> 3) * 2 + odd.astype(jnp.int32)


def whereabouts(group, chunks):
    section = lax.axis_index("section")
    label, slot = label_slot(lax.axis_index("dp"), group, chunks)
    return section, label, slot


def chunk_of(label, part, section):
    low = (part & 1) * 7 + (part >> 1) * 8 if STAR else part * 4
    return leader(label) ^ low ^ (section & 1) * TWIST


def pack_kernel(width, group, chunks, *refs):
    acts, gain, down = refs[:4], refs[4], refs[5]
    both, tall = refs[6:8]
    outs = refs[8:-2]
    line, sems = refs[-2:]
    micro, tokens = acts[0].shape[0], acts[0].shape[1]
    bottle = down.shape[1]
    section, label, _ = whereabouts(group, chunks)
    copies = []
    for a, act in enumerate(acts):
        for m in range(micro):
            start = ((a % 2) * micro + m) * tokens
            copies.append(
                pltpu.make_async_copy(
                    act.at[m], both.at[a // 2, pl.ds(start, tokens)], sems.at[len(copies)]
                )
            )
    count = len(copies)
    copies.append(pltpu.make_async_copy(gain.at[0], line, sems.at[count]))
    copies.append(
        pltpu.make_async_copy(down.at[0], tall.at[pl.ds(0, bottle)], sems.at[count + 1])
    )
    for copy in copies:
        copy.start()
    for n in range(count):
        copies[n].wait()
        a, m = divmod(n, micro)
        start = ((a % 2) * micro + m) * tokens
        for k, out in enumerate(outs, 1):
            for part in range(group):
                chunk = chunk_of(label ^ k, part, section)
                span = pl.ds(pl.multiple_of(chunk * width, width), width)
                out[a // 2, start : start + tokens, part * width : (part + 1) * width] = both[
                    a // 2, start : start + tokens, span
                ]
    copies[count].wait()
    tall[bottle:] = jnp.broadcast_to(line[...], (tall.shape[0] - bottle, tall.shape[1]))
    copies[count + 1].wait()


def two_parts(refs):
    if len(refs) == 2:
        return refs
    height, side = refs[0].shape
    return refs[0].at[: height - side // 2], refs[0].at[height - side // 2 :]


def products_kernel(layers, *refs):
    acts = refs[0]
    weights = [refs[1 + 2 * k : 3 + 2 * k] for k in range(layers)]
    outs = refs[1 + 2 * layers : -3]
    prod_out, gram_out = two_parts(outs)
    low_scr, fine_scr, high_scr = refs[-3:]
    bottle = weights[0][1].shape[1]
    gain_row = slice(bottle, bottle + 1)
    features = acts.shape[2]
    section = lax.axis_index("section")
    mine = pl.ds(pl.multiple_of(section * features, features), features)
    for k in range(layers):
        tall, up = weights[k]
        layer = section ^ k
        exact = tall[gain_row, mine].astype(f32) * tall[:bottle, mine].astype(f32)
        low, fine = split(exact)
        low_scr[layer] = low
        fine_scr[layer] = fine
        high_scr[layer] = up[0, :, mine]
    hidden = acts[0]
    low_all = low_scr[...].reshape(layers * bottle, features)
    fine_all = fine_scr[...].reshape(layers * bottle, features)
    high_all = high_scr[...].reshape(layers * bottle, features)
    size = (layers - 1) * bottle
    at = layers * bottle
    prod_out[:at] = dot_nt(low_all, hidden) + dot_nt(fine_all, hidden)
    if layers > 1:
        prod_out[at : at + size] = dot_nt(high_all[:size], hidden)
    at += size
    prod_out[at : at + layers * bottle] = dot_nt(high_all, acts[1])
    at += layers * bottle
    square = dot_nt(hidden, hidden)
    eye = lax.broadcasted_iota(jnp.int32, square.shape, 0) == lax.broadcasted_iota(
        jnp.int32, square.shape, 1
    )
    norms = jnp.sum(jnp.where(eye, square, 0.0), axis=0, keepdims=True)
    prod_out[at : at + 8] = jnp.broadcast_to(norms, (8, norms.shape[1]))
    if layers > 1:
        high_part = high_all[:size]
        low_part = low_all[bottle:]
        fine_part = fine_all[bottle:]
        gram_out[:, :size] = dot_nt(high_part, low_part) + dot_nt(high_part, fine_part)
        gram_out[:, size:] = dot_nt(high_part, high_part)
    else:
        gram_out[...] = jnp.zeros_like(gram_out)


def relay_kernel(layers, bottle, features, sections, *refs):
    coef_out, hold = refs[-2:]
    each = (len(refs) - 2) // sections
    prods, grams = zip(
        *(two_parts(refs[each * k : each * (k + 1)]) for k in range(sections)), strict=True
    )
    section = lax.axis_index("section")
    prod = sum((ref[...] for ref in prods[1:]), prods[0][...])
    gram = sum((ref[...] for ref in grams[1:]), grams[0][...])
    K = bottle
    inner = layers - 1
    h_low = [prod[l * K : (l + 1) * K] for l in range(layers)]
    at = layers * K
    h_high = [prod[at + l * K : at + (l + 1) * K] for l in range(inner)]
    at += inner * K
    u_high = [prod[at + l * K : at + (l + 1) * K] for l in range(layers)]
    at += layers * K
    norm = prod[at : at + 1]

    def high_low(m, l):
        return gram[m * K : (m + 1) * K, (l - 1) * K : l * K]

    def high_high(m, n):
        return gram[m * K : (m + 1) * K, (inner + n) * K : (inner + n + 1) * K]

    inverses, bottles, hidden_high = [], [], []
    for l in range(layers):
        inverse = lax.rsqrt(jnp.maximum(norm, 0.0) * (1.0 / features) + epsilon)
        value = h_low[l] * inverse
        active = (value * jax.nn.sigmoid(value)).astype(bf16)
        inverses.append(inverse)
        bottles.append(value)
        hold[l] = active
        hidden_high.append(list(h_high))
        if l < inner:
            before = h_high[l]
            h_high = [h_high[n] + dot_split(high_high(n, l), active) for n in range(inner)]
            for n in range(l + 1, layers):
                h_low[n] = h_low[n] + dot_split(high_low(l, n), active, dot_tn)
            norm = norm + jnp.sum(
                active.astype(f32) * (before + h_high[l]), axis=0, keepdims=True
            )
    pulls = [None] * layers
    for l in range(layers - 1, -1, -1):
        sigma = jax.nn.sigmoid(bottles[l])
        coarse = (u_high[l] * sigma * (1.0 + bottles[l] * (1.0 - sigma))).astype(bf16)
        hold[layers + l] = coarse
        if l == 0:
            break
        grad = coarse.astype(f32)
        scaled, fine = split(grad * inverses[l])
        pull = (
            inverses[l]
            * inverses[l]
            * jnp.sum(grad * bottles[l], axis=0, keepdims=True)
            * (1.0 / features)
        )
        pulls[l] = pull
        for n in range(l):
            u_high[n] = (
                u_high[n]
                + dot_split(high_low(n, l), scaled)
                + dot_nn(high_low(n, l).astype(bf16), fine)
                - pull * hidden_high[l][n]
            )
    blocks = [hold[layers + section], hold[section]]
    for i in range(inner):
        other = i + jnp.where(section <= i, 1, 0)
        blocks.append(hold[jnp.where(section <= i, layers + other, other)])
    blocks += [hold[n] for n in range(1, inner)]
    for n, block in enumerate(blocks):
        coef_out[n * K : (n + 1) * K] = block

    def inverse_at(layer):
        value = inverses[0]
        for l in range(1, layers):
            value = jnp.where(layer == l, inverses[l], value)
        return value

    lines = [line.astype(bf16).astype(f32) for line in pulls[1:]]
    scales = [inverse_at(section)]
    scales += [inverse_at(i + jnp.where(section <= i, 1, 0)) for i in range(inner)]
    for scale in scales:
        lines.extend(part.astype(f32) for part in split(scale))
    tail = coef_out.shape[0] - len(blocks) * K
    lines += [jnp.zeros_like(norm)] * (tail - len(lines))
    coef_out[len(blocks) * K :] = jnp.concatenate(lines, axis=0).astype(bf16)


def cut_kernel(layers, width, group, chunks, *refs):
    weights = [refs[2 * k : 2 * k + 2] for k in range(layers)]
    gain_out, both_out = refs[2 * layers :]
    bottle = weights[0][1].shape[1]
    gain_row = slice(bottle, bottle + 1)
    here_section, label, _ = whereabouts(group, chunks)
    for k in range(layers):
        section = here_section ^ k
        for part in range(group):
            chunk = section * chunks + chunk_of(label, part, section)
            span = pl.ds(pl.multiple_of(chunk * width, width), width)
            here = slice(part * width, (part + 1) * width)
            gain_out[k, :, here] = weights[0][0][gain_row, span].astype(f32)
            for w in range(layers):
                tall, up = weights[w]
                layer = here_section ^ w
                low = tall[gain_row, span].astype(f32) * tall[:bottle, span].astype(f32)
                both_out[k, layer, :, here] = low.astype(bf16)
                both_out[k, layers + layer, :, here] = up[0, :, span]


def stack_kernel(width, group, chunks, *refs):
    rows = refs[0].shape[1]
    out = refs[-1]
    if refs[0].shape[2] == out.shape[2]:
        out[:, :rows] = refs[0][...]
    else:
        section, label, _ = whereabouts(group, chunks)
        for part in range(group):
            chunk = chunk_of(label, part, section)
            span = pl.ds(pl.multiple_of(chunk * width, width), width)
            out[:, :rows, part * width : (part + 1) * width] = refs[0][:, :, span]
    for k, ref in enumerate(refs[1:-1], 1):
        out[:, k * rows : (k + 1) * rows] = ref[...]


def factors_kernel_part(layers, bottle, section, coefs, lefts, mates):
    K = bottle
    inner = layers - 1
    above = [section <= i for i in range(inner)]
    mates_of = [([], [], [], []) for _ in range(inner)]
    for m in range(MEMBERS):
        coef = coefs[m][...]
        grad, active = coef[:K], coef[K : 2 * K]
        others = [coef[(2 + i) * K : (3 + i) * K] for i in range(inner)]
        extras = [coef[(1 + layers + i) * K : (2 + layers + i) * K] for i in range(inner - 1)]
        at = (2 + inner + max(inner - 1, 0)) * K
        lines = coef[at:].astype(f32)
        active_f = active.astype(f32)

        def scale(i):
            row = inner + 2 * i
            return lines[row : row + 1] + lines[row + 1 : row + 2]

        def weight(n):
            total = jnp.zeros_like(lines[:1])
            for l in range(n + 1, layers):
                total = total + jnp.where(section < l, lines[l - 1 : l], 0.0)
            return total

        coarse, fine = split(grad.astype(f32) * scale(0))
        here = slice(m * coef.shape[1], (m + 1) * coef.shape[1])
        lefts[:K, here] = coarse
        lefts[K : 2 * K, here] = fine
        lefts[2 * K : 3 * K, here] = (-weight(0) * active_f).astype(bf16)
        lefts[3 * K :, here] = active
        for i in range(inner):
            factor = jnp.where(above[i], scale(1 + i), 1.0)
            other = (others[i].astype(f32) * factor).astype(bf16)
            mate = jnp.where(above[i], active_f, coarse.astype(f32)).astype(bf16)
            held = others[i]
            if i >= 1:
                held = jnp.where(section < i, extras[i - 1].astype(f32), held.astype(f32))
            held = jnp.where(section == i, active_f, held.astype(f32)).astype(bf16)
            pulled = (-weight(i) * active_f).astype(bf16)
            for values, value in zip(mates_of[i], (mate, other, pulled, held), strict=True):
                values.append(value)
    for i in range(inner):
        mate, other, pulled, held = (jnp.concatenate(v, axis=1) for v in mates_of[i])
        mates[2 * i] = dot_nt(mate, other).astype(bf16)
        mates[2 * i + 1] = dot_nt(pulled, held).astype(bf16)


def grads_kernel(layers, bottle, width, group, chunks, turn, *refs):
    K = bottle
    inner = layers - 1
    section, _, own_slot = whereabouts(group, chunks)
    final = turn == layers - 1
    if turn == 0:
        coefs, refs = refs[:MEMBERS], refs[MEMBERS:]
        pieces, gain, both, *outs, lefts, mates = refs
        factors_kernel_part(layers, bottle, section, coefs, lefts, mates)
        before = []
    else:
        lefts, mates, pieces, gain, both = refs[:5]
        before, outs = refs[5 : 5 + turn], list(refs[5 + turn :])
    parcel = outs.pop() if final else outs[0]
    by_hidden = dot_nn(lefts[: 3 * K], pieces[0])
    by_close = dot_nn(lefts[3 * K :], pieces[1])
    down = by_hidden[:K] + by_hidden[K : 2 * K]
    up = by_close + by_hidden[2 * K :]
    for i in range(inner):
        above = section <= i
        other = i + jnp.where(above, 1, 0)
        term = dot_nn(mates[2 * i], both[turn, jnp.where(above, other, layers + other)])
        up = up + jnp.where(above, term, 0.0)
        down = down + jnp.where(above, 0.0, term)
        up = up + dot_nn(mates[2 * i + 1], both[turn, layers + i])
    down = down * gain[turn]
    start = (section ^ turn) * group if final else 0
    for part in range(group):
        here = slice(part * width, (part + 1) * width)
        parcel[start + part, 0] = down[:, here]
        parcel[start + part, 1] = up[:, here]
    if not final:
        return
    for k, ref in enumerate(before):
        for part in range(group):
            parcel[(section ^ k) * group + part] = ref[part]
    if len(outs) == 1:
        outs[0][...] = parcel[...]
    else:
        for r, out in enumerate(outs):
            out[...] = parcel[own_slot ^ r].astype(out.dtype)


def per_device(inputs_down, inputs_up, cotan_down, cotan_up, norm_gains, adapt_down, adapt_up):
    sections = lax.axis_size("section")
    replicas = lax.axis_size("dp")
    section = lax.axis_index("section")
    replica = lax.axis_index("dp")
    layers = sections
    chunks = replicas // sections
    group = chunks // MEMBERS
    slots = replicas // MEMBERS
    bottle = adapt_down.shape[1]
    features = adapt_down.shape[2]
    share = features // sections
    width = features // replicas
    columns = group * width
    label, slot = label_slot(replica, group, chunks)
    micro, tokens = inputs_down.shape[0], inputs_down.shape[1]
    half = micro * tokens
    rows = 2 * half
    inner = layers - 1
    aligned = width % 128 == 0
    params = pltpu.CompilerParams(vmem_limit_bytes=VMEM_BYTES)

    acts = (inputs_down, inputs_up, cotan_down, cotan_up)
    if aligned:
        taken = (*acts, norm_gains[:, None, :], adapt_down)
        both, tall, *packed = pl.pallas_call(
            functools.partial(pack_kernel, width, group, chunks),
            out_shape=[
                pltpu.VMEM((2, rows, share), bf16),
                pltpu.VMEM((bottle + 16, features), bf16),
            ]
            + [pltpu.VMEM((2, rows, columns), bf16)] * (MEMBERS - 1),
            in_specs=[IN_HBM] * 6,
            out_specs=[IN_VMEM] * (1 + MEMBERS),
            scratch_shapes=[
                pltpu.VMEM((1, features), bf16),
                pltpu.SemaphoreType.DMA((4 * micro + 2,)),
            ],
            compiler_params=params,
            name="pack",
        )(*[pltpu.with_memory_space_constraint(v, pltpu.HBM) for v in taken])
        packed = [both, *packed]
    else:
        tall = jnp.concatenate(
            [adapt_down[0], jnp.broadcast_to(norm_gains, (16, features))], axis=0
        )
        both = jnp.concatenate([v.reshape(half, share) for v in acts], axis=0)
        both = both.reshape(2, rows, share)
        parts = both.reshape(2, rows, chunks, width)
        packed = []
        for k in range(MEMBERS):
            cuts = [
                lax.dynamic_index_in_dim(
                    parts, chunk_of(label ^ k, part, section), 2, keepdims=False
                )
                for part in range(group)
            ]
            packed.append(jnp.concatenate(cuts, axis=2))

    own = (tall, lax.optimization_barrier((adapt_up, *packed))[0])
    weights = [own]
    for k in range(1, sections):
        weights.append(tuple(from_partner(w, "section", k) for w in own))
    flat = [w for ws in weights for w in ws]
    pieces = [packed[0]]
    for k in range(1, MEMBERS):
        pieces.append(from_partner(packed[k], "dp", LEADERS[k]))
    prod_rows = (3 * layers - 1) * bottle + 8
    gram_rows = max(inner, 1) * bottle
    sides = [(prod_rows, rows), (gram_rows, 2 * gram_rows)]
    if rows == 2 * gram_rows:
        sides = [(prod_rows + gram_rows, rows)]
    sums = pl.pallas_call(
        functools.partial(products_kernel, layers),
        out_shape=[jax.ShapeDtypeStruct(side, f32) for side in sides],
        in_specs=[IN_VMEM] * (1 + 2 * sections),
        out_specs=[IN_VMEM] * len(sides),
        scratch_shapes=[pltpu.VMEM((layers, bottle, share), bf16)] * 3,
        compiler_params=params,
        cost_estimate=cost(COST_PRODUCTS),
        name="products",
    )(both, *flat)
    sums = list(sums)
    for k in range(1, sections):
        sums += [from_partner(v, "section", k) for v in sums[: len(sides)]]

    tail = inner + 2 * layers
    coef_rows = (2 + inner + max(inner - 1, 0)) * bottle + -(-tail // 16) * 16
    coef = pl.pallas_call(
        functools.partial(relay_kernel, layers, bottle, features, sections),
        out_shape=jax.ShapeDtypeStruct((coef_rows, rows), bf16),
        in_specs=[IN_VMEM] * len(sums),
        out_specs=IN_VMEM,
        scratch_shapes=[pltpu.VMEM((2 * layers, bottle, rows), bf16)],
        compiler_params=params,
        cost_estimate=cost(COST_SMALL),
        name="relay",
    )(*sums)
    coefs = [coef] + [from_partner(coef, "dp", LEADERS[k]) for k in range(1, MEMBERS)]
    cut_shapes = [
        jax.ShapeDtypeStruct((layers, 1, columns), f32),
        jax.ShapeDtypeStruct((layers, 2 * layers, bottle, columns), bf16),
    ]
    if aligned:
        gain_cut, both_cut = pl.pallas_call(
            functools.partial(cut_kernel, layers, width, group, chunks),
            out_shape=cut_shapes,
            in_specs=[IN_VMEM] * len(flat),
            out_specs=[IN_VMEM] * 2,
            compiler_params=params,
            cost_estimate=cost(COST_SMALL),
            name="cut",
        )(*flat)
    else:
        gain_cut = jnp.zeros(cut_shapes[0].shape, f32)
        both_cut = jnp.zeros(cut_shapes[1].shape, bf16)
        for k in range(layers):
            for part in range(group):
                at = section ^ k
                chunk = at * chunks + chunk_of(label, part, at)
                for w, ws in enumerate(weights):
                    down, up = (
                        lax.dynamic_index_in_dim(
                            v.reshape(-1, replicas, width), chunk, 1, keepdims=False
                        )
                        for v in ws
                    )
                    down, gain = down[:bottle], down[bottle : bottle + 1]
                    low = (gain.astype(f32) * down.astype(f32)).astype(bf16)
                    layer = section ^ w
                    spot = (k, layer, 0, part * width)
                    both_cut = lax.dynamic_update_slice(both_cut, low[None, None], spot)
                    spot = (k, layers + layer, 0, part * width)
                    both_cut = lax.dynamic_update_slice(both_cut, up[None, None], spot)
                    if w == 0:
                        gain_cut = lax.dynamic_update_slice(
                            gain_cut, gain.astype(f32)[None], (k, 0, part * width)
                        )

    gated = list(lax.optimization_barrier((*pieces, coef))[:-1])
    stacked = pl.pallas_call(
        functools.partial(stack_kernel, width, group, chunks),
        out_shape=jax.ShapeDtypeStruct((2, MEMBERS * rows, columns), bf16),
        in_specs=[IN_VMEM] * MEMBERS,
        out_specs=IN_VMEM,
        compiler_params=params,
        cost_estimate=cost(COST_SMALL),
        name="stack",
    )(*gated)
    handed = [None] + [from_partner(stacked, "section", k) for k in range(1, sections)]

    message = (2, bottle, width)
    left_shape = jax.ShapeDtypeStruct((4 * bottle, MEMBERS * rows), bf16)
    mate_shape = jax.ShapeDtypeStruct((max(2 * inner, 1), bottle, bottle), bf16)
    held = jax.ShapeDtypeStruct((group,) + message, f32)
    before = []
    for k in range(sections):
        shapes, scratch = [held], []
        if k == sections - 1:
            scratch = [pltpu.VMEM((slots,) + message, f32)]
            shapes = [jax.ShapeDtypeStruct((slots,) + message, f32)]
            if aligned:
                shapes = [jax.ShapeDtypeStruct(message, f32)]
                shapes += [jax.ShapeDtypeStruct(message, bf16)] * (slots - 1)
        if k == 0:
            shapes += [left_shape, mate_shape]
            operands = (*coefs, stacked, gain_cut, both_cut)
        else:
            operands = (lefts, mates, handed[k], gain_cut, both_cut, *before)
        parcels = pl.pallas_call(
            functools.partial(grads_kernel, layers, bottle, width, group, chunks, k),
            out_shape=shapes,
            in_specs=[IN_VMEM] * len(operands),
            out_specs=[IN_VMEM] * len(shapes),
            scratch_shapes=scratch,
            compiler_params=params,
            cost_estimate=cost(COST_GRADS),
            name="grads",
        )(*operands)
        if k == 0:
            *parcels, lefts, mates = parcels
        if k < sections - 1:
            before += parcels
    if not aligned:
        parcels = [
            lax.dynamic_index_in_dim(parcels[0], slot ^ r, 0, keepdims=False)
            for r in range(slots)
        ]
        parcels[1:] = [v.astype(bf16) for v in parcels[1:]]

    total = parcels[0]
    for r in range(slots - 1, 0, -1):
        received = from_partner(parcels[r], "dp", mask(r, group, chunks))
        total = total + received.astype(f32)
    return (total[0][None], total[1][None])


def solution(mesh):
    placed = (
        P(None, "dp", "section"),
        P(None, "dp", "section"),
        P(None, "dp", "section"),
        P(None, "dp", "section"),
        P("section", None),
        P("section", None, None),
        P("section", None, None),
    )
    return jax.shard_map(
        per_device,
        mesh=mesh,
        in_specs=placed,
        out_specs=(P("section", None, "dp"), P("section", None, "dp")),
        check_vma=False,
    )
```

```python
import functools

import jax
import jax.numpy as jnp
from jax import lax
from jax.experimental import pallas as pl
from jax.experimental.pallas import tpu as pltpu
from jax.sharding import PartitionSpec as P

epsilon = 1e-05
VMEM_BYTES = 32 * 1024 * 1024
MEMBERS = 4
STAR = True
TWIST = 2
COST_PRODUCTS = 12
COST_SMALL = 0.1
COST_GRADS = 10
f32 = jnp.float32
bf16 = jnp.bfloat16
IN_VMEM = pl.BlockSpec(memory_space=pltpu.VMEM)
IN_HBM = pl.BlockSpec(memory_space=pltpu.HBM)


def cost(micros):
    return pl.CostEstimate(flops=int(micros * 1.1e9), bytes_accessed=0, transcendentals=0)


def from_partner(value, axis, flip):
    return lax.ppermute(value, axis, [(i, i ^ flip) for i in range(lax.axis_size(axis))])


def dot_nn(left, right):
    return lax.dot_general(left, right, (((1,), (0,)), ((), ())), preferred_element_type=f32)


def dot_nt(left, right):
    return lax.dot_general(left, right, (((1,), (1,)), ((), ())), preferred_element_type=f32)


def split(value):
    high = value.astype(bf16)
    return high, (value - high.astype(f32)).astype(bf16)


def dot_tn(left, right):
    return lax.dot_general(left, right, (((0,), (0,)), ((), ())), preferred_element_type=f32)


def dot_split(left, right, dot=dot_nn):
    high, low = split(left)
    return dot(high, right) + dot(low, right)


LEADERS = (0, 1, 2, 4) if STAR else (0, 1, 2, 3)


def leader(label):
    return label + (label == 3) if STAR else label


def mask(slot, group, chunks):
    section, part = divmod(slot, group)
    low = (part & 1) * 7 + (part >> 1) * 8 if STAR else part * 4
    return section * chunks ^ (section & 1) * TWIST ^ low


def label_slot(replica, group, chunks):
    section = replica // chunks
    local = replica % chunks ^ (section & 1) * TWIST
    if not STAR:
        return local % 4, section * group + local // 4
    low = local & 7
    label = (low & 3) ^ (low >> 2) * 3
    odd = (low != 0) & (low != 1) & (low != 2) & (low != 4)
    return label, section * group + (local >> 3) * 2 + odd.astype(jnp.int32)


def whereabouts(group, chunks):
    section = lax.axis_index("section")
    label, slot = label_slot(lax.axis_index("dp"), group, chunks)
    return section, label, slot


def chunk_of(label, part, section):
    low = (part & 1) * 7 + (part >> 1) * 8 if STAR else part * 4
    return leader(label) ^ low ^ (section & 1) * TWIST


def pack_kernel(width, group, chunks, *refs):
    acts, gain, down = refs[:4], refs[4], refs[5]
    both, tall = refs[6:8]
    outs = refs[8:-2]
    line, sems = refs[-2:]
    micro, tokens = acts[0].shape[0], acts[0].shape[1]
    bottle = down.shape[1]
    section, label, _ = whereabouts(group, chunks)
    copies = []
    for a, act in enumerate(acts):
        for m in range(micro):
            start = ((a % 2) * micro + m) * tokens
            copies.append(
                pltpu.make_async_copy(
                    act.at[m], both.at[a // 2, pl.ds(start, tokens)], sems.at[len(copies)]
                )
            )
    count = len(copies)
    copies.append(pltpu.make_async_copy(gain.at[0], line, sems.at[count]))
    copies.append(
        pltpu.make_async_copy(down.at[0], tall.at[pl.ds(0, bottle)], sems.at[count + 1])
    )
    for copy in copies:
        copy.start()
    for n in range(count):
        copies[n].wait()
        a, m = divmod(n, micro)
        start = ((a % 2) * micro + m) * tokens
        for k, out in enumerate(outs, 1):
            for part in range(group):
                chunk = chunk_of(label ^ k, part, section)
                span = pl.ds(pl.multiple_of(chunk * width, width), width)
                out[a // 2, start : start + tokens, part * width : (part + 1) * width] = both[
                    a // 2, start : start + tokens, span
                ]
    copies[count].wait()
    tall[bottle:] = jnp.broadcast_to(line[...], (tall.shape[0] - bottle, tall.shape[1]))
    copies[count + 1].wait()


def two_parts(refs):
    if len(refs) == 2:
        return refs
    height, side = refs[0].shape
    return refs[0].at[: height - side // 2], refs[0].at[height - side // 2 :]


def products_kernel(layers, *refs):
    acts = refs[0]
    weights = [refs[1 + 2 * k : 3 + 2 * k] for k in range(layers)]
    outs = refs[1 + 2 * layers : -3]
    prod_out, gram_out = two_parts(outs)
    low_scr, fine_scr, high_scr = refs[-3:]
    bottle = weights[0][1].shape[1]
    gain_row = slice(bottle, bottle + 1)
    features = acts.shape[2]
    section = lax.axis_index("section")
    mine = pl.ds(pl.multiple_of(section * features, features), features)
    for k in range(layers):
        tall, up = weights[k]
        layer = section ^ k
        exact = tall[gain_row, mine].astype(f32) * tall[:bottle, mine].astype(f32)
        low, fine = split(exact)
        low_scr[layer] = low
        fine_scr[layer] = fine
        high_scr[layer] = up[0, :, mine]
    hidden = acts[0]
    low_all = low_scr[...].reshape(layers * bottle, features)
    fine_all = fine_scr[...].reshape(layers * bottle, features)
    high_all = high_scr[...].reshape(layers * bottle, features)
    size = (layers - 1) * bottle
    at = layers * bottle
    prod_out[:at] = dot_nt(low_all, hidden) + dot_nt(fine_all, hidden)
    if layers > 1:
        prod_out[at : at + size] = dot_nt(high_all[:size], hidden)
    at += size
    prod_out[at : at + layers * bottle] = dot_nt(high_all, acts[1])
    at += layers * bottle
    square = dot_nt(hidden, hidden)
    eye = lax.broadcasted_iota(jnp.int32, square.shape, 0) == lax.broadcasted_iota(
        jnp.int32, square.shape, 1
    )
    norms = jnp.sum(jnp.where(eye, square, 0.0), axis=0, keepdims=True)
    prod_out[at : at + 8] = jnp.broadcast_to(norms, (8, norms.shape[1]))
    if layers > 1:
        high_part = high_all[:size]
        low_part = low_all[bottle:]
        fine_part = fine_all[bottle:]
        gram_out[:, :size] = dot_nt(high_part, low_part) + dot_nt(high_part, fine_part)
        gram_out[:, size:] = dot_nt(high_part, high_part)
    else:
        gram_out[...] = jnp.zeros_like(gram_out)


def relay_kernel(layers, bottle, features, sections, *refs):
    coef_out, hold = refs[-2:]
    each = (len(refs) - 2) // sections
    prods, grams = zip(
        *(two_parts(refs[each * k : each * (k + 1)]) for k in range(sections)), strict=True
    )
    section = lax.axis_index("section")
    prod = sum((ref[...] for ref in prods[1:]), prods[0][...])
    gram = sum((ref[...] for ref in grams[1:]), grams[0][...])
    K = bottle
    inner = layers - 1
    h_low = [prod[l * K : (l + 1) * K] for l in range(layers)]
    at = layers * K
    h_high = [prod[at + l * K : at + (l + 1) * K] for l in range(inner)]
    at += inner * K
    u_high = [prod[at + l * K : at + (l + 1) * K] for l in range(layers)]
    at += layers * K
    norm = prod[at : at + 1]

    def high_low(m, l):
        return gram[m * K : (m + 1) * K, (l - 1) * K : l * K]

    def high_high(m, n):
        return gram[m * K : (m + 1) * K, (inner + n) * K : (inner + n + 1) * K]

    inverses, bottles, hidden_high = [], [], []
    for l in range(layers):
        inverse = lax.rsqrt(jnp.maximum(norm, 0.0) * (1.0 / features) + epsilon)
        value = h_low[l] * inverse
        active = (value * jax.nn.sigmoid(value)).astype(bf16)
        inverses.append(inverse)
        bottles.append(value)
        hold[l] = active
        hidden_high.append(list(h_high))
        if l < inner:
            before = h_high[l]
            h_high = [h_high[n] + dot_split(high_high(n, l), active) for n in range(inner)]
            for n in range(l + 1, layers):
                h_low[n] = h_low[n] + dot_split(high_low(l, n), active, dot_tn)
            norm = norm + jnp.sum(
                active.astype(f32) * (before + h_high[l]), axis=0, keepdims=True
            )
    pulls = [None] * layers
    for l in range(layers - 1, -1, -1):
        sigma = jax.nn.sigmoid(bottles[l])
        coarse = (u_high[l] * sigma * (1.0 + bottles[l] * (1.0 - sigma))).astype(bf16)
        hold[layers + l] = coarse
        if l == 0:
            break
        grad = coarse.astype(f32)
        scaled, fine = split(grad * inverses[l])
        pull = (
            inverses[l]
            * inverses[l]
            * jnp.sum(grad * bottles[l], axis=0, keepdims=True)
            * (1.0 / features)
        )
        pulls[l] = pull
        for n in range(l):
            u_high[n] = (
                u_high[n]
                + dot_split(high_low(n, l), scaled)
                + dot_nn(high_low(n, l).astype(bf16), fine)
                - pull * hidden_high[l][n]
            )
    blocks = [hold[layers + section], hold[section]]
    for i in range(inner):
        other = i + jnp.where(section <= i, 1, 0)
        blocks.append(hold[jnp.where(section <= i, layers + other, other)])
    blocks += [hold[n] for n in range(1, inner)]
    for n, block in enumerate(blocks):
        coef_out[n * K : (n + 1) * K] = block

    def inverse_at(layer):
        value = inverses[0]
        for l in range(1, layers):
            value = jnp.where(layer == l, inverses[l], value)
        return value

    lines = [line.astype(bf16).astype(f32) for line in pulls[1:]]
    scales = [inverse_at(section)]
    scales += [inverse_at(i + jnp.where(section <= i, 1, 0)) for i in range(inner)]
    for scale in scales:
        lines.extend(part.astype(f32) for part in split(scale))
    tail = coef_out.shape[0] - len(blocks) * K
    lines += [jnp.zeros_like(norm)] * (tail - len(lines))
    coef_out[len(blocks) * K :] = jnp.concatenate(lines, axis=0).astype(bf16)


def cut_kernel(layers, width, group, chunks, *refs):
    weights = [refs[2 * k : 2 * k + 2] for k in range(layers)]
    gain_out, both_out = refs[2 * layers :]
    bottle = weights[0][1].shape[1]
    gain_row = slice(bottle, bottle + 1)
    here_section, label, _ = whereabouts(group, chunks)
    for k in range(layers):
        section = here_section ^ k
        for part in range(group):
            chunk = section * chunks + chunk_of(label, part, section)
            span = pl.ds(pl.multiple_of(chunk * width, width), width)
            here = slice(part * width, (part + 1) * width)
            gain_out[k, :, here] = weights[0][0][gain_row, span].astype(f32)
            for w in range(layers):
                tall, up = weights[w]
                layer = here_section ^ w
                low = tall[gain_row, span].astype(f32) * tall[:bottle, span].astype(f32)
                both_out[k, layer, :, here] = low.astype(bf16)
                both_out[k, layers + layer, :, here] = up[0, :, span]


def stack_kernel(width, group, chunks, *refs):
    rows = refs[0].shape[1]
    out = refs[-1]
    if refs[0].shape[2] == out.shape[2]:
        out[:, :rows] = refs[0][...]
    else:
        section, label, _ = whereabouts(group, chunks)
        for part in range(group):
            chunk = chunk_of(label, part, section)
            span = pl.ds(pl.multiple_of(chunk * width, width), width)
            out[:, :rows, part * width : (part + 1) * width] = refs[0][:, :, span]
    for k, ref in enumerate(refs[1:-1], 1):
        out[:, k * rows : (k + 1) * rows] = ref[...]


def factors_kernel_part(layers, bottle, section, coefs, lefts, mates):
    K = bottle
    inner = layers - 1
    above = [section <= i for i in range(inner)]
    mates_of = [([], [], [], []) for _ in range(inner)]
    for m in range(MEMBERS):
        coef = coefs[m][...]
        grad, active = coef[:K], coef[K : 2 * K]
        others = [coef[(2 + i) * K : (3 + i) * K] for i in range(inner)]
        extras = [coef[(1 + layers + i) * K : (2 + layers + i) * K] for i in range(inner - 1)]
        at = (2 + inner + max(inner - 1, 0)) * K
        lines = coef[at:].astype(f32)
        active_f = active.astype(f32)

        def scale(i):
            row = inner + 2 * i
            return lines[row : row + 1] + lines[row + 1 : row + 2]

        def weight(n):
            total = jnp.zeros_like(lines[:1])
            for l in range(n + 1, layers):
                total = total + jnp.where(section < l, lines[l - 1 : l], 0.0)
            return total

        coarse, fine = split(grad.astype(f32) * scale(0))
        here = slice(m * coef.shape[1], (m + 1) * coef.shape[1])
        lefts[:K, here] = coarse
        lefts[K : 2 * K, here] = fine
        lefts[2 * K : 3 * K, here] = (-weight(0) * active_f).astype(bf16)
        lefts[3 * K :, here] = active
        for i in range(inner):
            factor = jnp.where(above[i], scale(1 + i), 1.0)
            other = (others[i].astype(f32) * factor).astype(bf16)
            mate = jnp.where(above[i], active_f, coarse.astype(f32)).astype(bf16)
            held = others[i]
            if i >= 1:
                held = jnp.where(section < i, extras[i - 1].astype(f32), held.astype(f32))
            held = jnp.where(section == i, active_f, held.astype(f32)).astype(bf16)
            pulled = (-weight(i) * active_f).astype(bf16)
            for values, value in zip(mates_of[i], (mate, other, pulled, held), strict=True):
                values.append(value)
    for i in range(inner):
        mate, other, pulled, held = (jnp.concatenate(v, axis=1) for v in mates_of[i])
        mates[2 * i] = dot_nt(mate, other).astype(bf16)
        mates[2 * i + 1] = dot_nt(pulled, held).astype(bf16)


def grads_kernel(layers, bottle, width, group, chunks, turn, *refs):
    K = bottle
    inner = layers - 1
    section, _, own_slot = whereabouts(group, chunks)
    final = turn == layers - 1
    if turn == 0:
        coefs, refs = refs[:MEMBERS], refs[MEMBERS:]
        pieces, gain, both, *outs, lefts, mates = refs
        factors_kernel_part(layers, bottle, section, coefs, lefts, mates)
        before = []
    else:
        lefts, mates, pieces, gain, both = refs[:5]
        before, outs = refs[5 : 5 + turn], list(refs[5 + turn :])
    parcel = outs.pop() if final else outs[0]
    by_hidden = dot_nn(lefts[: 3 * K], pieces[0])
    by_close = dot_nn(lefts[3 * K :], pieces[1])
    down = by_hidden[:K] + by_hidden[K : 2 * K]
    up = by_close + by_hidden[2 * K :]
    for i in range(inner):
        above = section <= i
        other = i + jnp.where(above, 1, 0)
        term = dot_nn(mates[2 * i], both[turn, jnp.where(above, other, layers + other)])
        up = up + jnp.where(above, term, 0.0)
        down = down + jnp.where(above, 0.0, term)
        up = up + dot_nn(mates[2 * i + 1], both[turn, layers + i])
    down = down * gain[turn]
    start = (section ^ turn) * group if final else 0
    for part in range(group):
        here = slice(part * width, (part + 1) * width)
        parcel[start + part, 0] = down[:, here]
        parcel[start + part, 1] = up[:, here]
    if not final:
        return
    for k, ref in enumerate(before):
        for part in range(group):
            parcel[(section ^ k) * group + part] = ref[part]
    if len(outs) == 1:
        outs[0][...] = parcel[...]
    else:
        for r, out in enumerate(outs):
            out[...] = parcel[own_slot ^ r].astype(out.dtype)


def per_device(inputs_down, inputs_up, cotan_down, cotan_up, norm_gains, adapt_down, adapt_up):
    sections = lax.axis_size("section")
    replicas = lax.axis_size("dp")
    section = lax.axis_index("section")
    replica = lax.axis_index("dp")
    layers = sections
    chunks = replicas // sections
    group = chunks // MEMBERS
    slots = replicas // MEMBERS
    bottle = adapt_down.shape[1]
    features = adapt_down.shape[2]
    share = features // sections
    width = features // replicas
    columns = group * width
    label, slot = label_slot(replica, group, chunks)
    micro, tokens = inputs_down.shape[0], inputs_down.shape[1]
    half = micro * tokens
    rows = 2 * half
    inner = layers - 1
    aligned = width % 128 == 0
    params = pltpu.CompilerParams(vmem_limit_bytes=VMEM_BYTES)

    acts = (inputs_down, inputs_up, cotan_down, cotan_up)
    if aligned:
        taken = (*acts, norm_gains[:, None, :], adapt_down)
        both, tall, *packed = pl.pallas_call(
            functools.partial(pack_kernel, width, group, chunks),
            out_shape=[
                pltpu.VMEM((2, rows, share), bf16),
                pltpu.VMEM((bottle + 16, features), bf16),
            ]
            + [pltpu.VMEM((2, rows, columns), bf16)] * (MEMBERS - 1),
            in_specs=[IN_HBM] * 6,
            out_specs=[IN_VMEM] * (1 + MEMBERS),
            scratch_shapes=[
                pltpu.VMEM((1, features), bf16),
                pltpu.SemaphoreType.DMA((4 * micro + 2,)),
            ],
            compiler_params=params,
            name="pack",
        )(*[pltpu.with_memory_space_constraint(v, pltpu.HBM) for v in taken])
        packed = [both, *packed]
    else:
        tall = jnp.concatenate(
            [adapt_down[0], jnp.broadcast_to(norm_gains, (16, features))], axis=0
        )
        both = jnp.concatenate([v.reshape(half, share) for v in acts], axis=0)
        both = both.reshape(2, rows, share)
        parts = both.reshape(2, rows, chunks, width)
        packed = []
        for k in range(MEMBERS):
            cuts = [
                lax.dynamic_index_in_dim(
                    parts, chunk_of(label ^ k, part, section), 2, keepdims=False
                )
                for part in range(group)
            ]
            packed.append(jnp.concatenate(cuts, axis=2))

    own = (tall, lax.optimization_barrier((adapt_up, *packed))[0])
    weights = [own]
    for k in range(1, sections):
        weights.append(tuple(from_partner(w, "section", k) for w in own))
    flat = [w for ws in weights for w in ws]
    pieces = [packed[0]]
    for k in range(1, MEMBERS):
        pieces.append(from_partner(packed[k], "dp", LEADERS[k]))
    prod_rows = (3 * layers - 1) * bottle + 8
    gram_rows = max(inner, 1) * bottle
    sides = [(prod_rows, rows), (gram_rows, 2 * gram_rows)]
    if rows == 2 * gram_rows:
        sides = [(prod_rows + gram_rows, rows)]
    sums = pl.pallas_call(
        functools.partial(products_kernel, layers),
        out_shape=[jax.ShapeDtypeStruct(side, f32) for side in sides],
        in_specs=[IN_VMEM] * (1 + 2 * sections),
        out_specs=[IN_VMEM] * len(sides),
        scratch_shapes=[pltpu.VMEM((layers, bottle, share), bf16)] * 3,
        compiler_params=params,
        cost_estimate=cost(COST_PRODUCTS),
        name="products",
    )(both, *flat)
    sums = list(sums)
    for k in range(1, sections):
        sums += [from_partner(v, "section", k) for v in sums[: len(sides)]]

    tail = inner + 2 * layers
    coef_rows = (2 + inner + max(inner - 1, 0)) * bottle + -(-tail // 16) * 16
    coef = pl.pallas_call(
        functools.partial(relay_kernel, layers, bottle, features, sections),
        out_shape=jax.ShapeDtypeStruct((coef_rows, rows), bf16),
        in_specs=[IN_VMEM] * len(sums),
        out_specs=IN_VMEM,
        scratch_shapes=[pltpu.VMEM((2 * layers, bottle, rows), bf16)],
        compiler_params=params,
        cost_estimate=cost(COST_SMALL),
        name="relay",
    )(*sums)
    coefs = [coef] + [from_partner(coef, "dp", LEADERS[k]) for k in range(1, MEMBERS)]
    cut_shapes = [
        jax.ShapeDtypeStruct((layers, 1, columns), f32),
        jax.ShapeDtypeStruct((layers, 2 * layers, bottle, columns), bf16),
    ]
    if aligned:
        gain_cut, both_cut = pl.pallas_call(
            functools.partial(cut_kernel, layers, width, group, chunks),
            out_shape=cut_shapes,
            in_specs=[IN_VMEM] * len(flat),
            out_specs=[IN_VMEM] * 2,
            compiler_params=params,
            cost_estimate=cost(COST_SMALL),
            name="cut",
        )(*flat)
    else:
        gain_cut = jnp.zeros(cut_shapes[0].shape, f32)
        both_cut = jnp.zeros(cut_shapes[1].shape, bf16)
        for k in range(layers):
            for part in range(group):
                at = section ^ k
                chunk = at * chunks + chunk_of(label, part, at)
                for w, ws in enumerate(weights):
                    down, up = (
                        lax.dynamic_index_in_dim(
                            v.reshape(-1, replicas, width), chunk, 1, keepdims=False
                        )
                        for v in ws
                    )
                    down, gain = down[:bottle], down[bottle : bottle + 1]
                    low = (gain.astype(f32) * down.astype(f32)).astype(bf16)
                    layer = section ^ w
                    spot = (k, layer, 0, part * width)
                    both_cut = lax.dynamic_update_slice(both_cut, low[None, None], spot)
                    spot = (k, layers + layer, 0, part * width)
                    both_cut = lax.dynamic_update_slice(both_cut, up[None, None], spot)
                    if w == 0:
                        gain_cut = lax.dynamic_update_slice(
                            gain_cut, gain.astype(f32)[None], (k, 0, part * width)
                        )

    gated = list(lax.optimization_barrier((*pieces, coef))[:-1])
    stacked = pl.pallas_call(
        functools.partial(stack_kernel, width, group, chunks),
        out_shape=jax.ShapeDtypeStruct((2, MEMBERS * rows, columns), bf16),
        in_specs=[IN_VMEM] * MEMBERS,
        out_specs=IN_VMEM,
        compiler_params=params,
        cost_estimate=cost(COST_SMALL),
        name="stack",
    )(*gated)
    handed = [None] + [from_partner(stacked, "section", k) for k in range(1, sections)]

    message = (2, bottle, width)
    left_shape = jax.ShapeDtypeStruct((4 * bottle, MEMBERS * rows), bf16)
    mate_shape = jax.ShapeDtypeStruct((max(2 * inner, 1), bottle, bottle), bf16)
    held = jax.ShapeDtypeStruct((group,) + message, f32)
    before = []
    for k in range(sections):
        shapes, scratch = [held], []
        if k == sections - 1:
            scratch = [pltpu.VMEM((slots,) + message, f32)]
            shapes = [jax.ShapeDtypeStruct((slots,) + message, f32)]
            if aligned:
                shapes = [jax.ShapeDtypeStruct(message, f32)]
                shapes += [jax.ShapeDtypeStruct(message, bf16)] * (slots - 1)
        if k == 0:
            shapes += [left_shape, mate_shape]
            operands = (*coefs, stacked, gain_cut, both_cut)
        else:
            operands = (lefts, mates, handed[k], gain_cut, both_cut, *before)
        parcels = pl.pallas_call(
            functools.partial(grads_kernel, layers, bottle, width, group, chunks, k),
            out_shape=shapes,
            in_specs=[IN_VMEM] * len(operands),
            out_specs=[IN_VMEM] * len(shapes),
            scratch_shapes=scratch,
            compiler_params=params,
            cost_estimate=cost(COST_GRADS),
            name="grads",
        )(*operands)
        if k == 0:
            *parcels, lefts, mates = parcels
        if k < sections - 1:
            before += parcels
    if not aligned:
        parcels = [
            lax.dynamic_index_in_dim(parcels[0], slot ^ r, 0, keepdims=False)
            for r in range(slots)
        ]
        parcels[1:] = [v.astype(bf16) for v in parcels[1:]]

    total = parcels[0]
    for r in (*range(slots // 2, slots), *range(1, slots // 2)):
        received = from_partner(parcels[r], "dp", mask(r, group, chunks))
        total = total + received.astype(f32)
    return (total[0][None], total[1][None])


def solution(mesh):
    placed = (
        P(None, "dp", "section"),
        P(None, "dp", "section"),
        P(None, "dp", "section"),
        P(None, "dp", "section"),
        P("section", None),
        P("section", None, None),
        P("section", None, None),
    )
    return jax.shard_map(
        per_device,
        mesh=mesh,
        in_specs=placed,
        out_specs=(P("section", None, "dp"), P("section", None, "dp")),
        check_vma=False,
    )
```
